32 devices in a mesh: section: 2 (over core), ctx: 4 (over z), heads: 4 (over y, x).
Axes of the slice: x: 2, y: 2, z: 4, core: 2. Of those that a mesh axis runs over, the one named last changes fastest.
Arguments:
- boundary: bfloat16 [2, 2, 1024, 768], P('section', None, 'ctx'), may hold values from -6 to 6
- norm_first: bfloat16 [2, 768], P('section'), may hold values from 0.5 to 1.5
- qkv_weight: bfloat16 [2, 3, 768, 768], P('section', None, None, 'heads'), may hold values from -0.21875 to 0.21875
- position_bias: float32 [2, 32, 12], P('section', None, 'heads'), may hold values from -4 to 4
- out_weight: bfloat16 [2, 768, 768], P('section', 'heads'), may hold values from -0.875 to 0.875
- norm_second: bfloat16 [2, 768], P('section'), may hold values from 0.5 to 1.5
- router: bfloat16 [2, 768, 4], P('section'), may hold values from -0.15625 to 0.15625
- expert_up: bfloat16 [2, 4, 768, 3072], P('section', 'ctx', None, 'heads'), may hold values from -0.21875 to 0.21875
- expert_down: bfloat16 [2, 4, 3072, 768], P('section', 'ctx', 'heads'), may hold values from -0.15625 to 0.15625
- routes: int32 [2, 2, 1024, 2], P('section', None, 'ctx'), may hold values from 0 to 3, all different within a row; in each aligned block of 256 rows (0 to 255, 256 to 511, ..., all dimensions but the last counted through in order) at most 160 rows name the same one
Outputs:
- boundary_out: float32 [2, 2, 1024, 768], P('section', None, 'ctx')
- grad_norm_first: float32 [2, 768], P('section', 'ctx')
- grad_qkv_weight: float32 [2, 3, 768, 768], P('section', None, 'ctx', 'heads')
- grad_position_bias: float32 [2, 32, 12], P('section', 'ctx', 'heads')
- grad_out_weight: float32 [2, 768, 768], P('section', 'heads', 'ctx')
- grad_norm_second: float32 [2, 768], P('section', 'ctx')
- grad_router: float32 [2, 768, 4], P('section', 'ctx')
- grad_expert_up: float32 [2, 4, 768, 3072], P('section', 'ctx', None, 'heads')
- grad_expert_down: float32 [2, 4, 3072, 768], P('section', 'ctx', 'heads')
The draws below stay inside these ranges and needn't reach their ends.
Inputs may be any that keep to these rules, and one draw needn't show every extreme that they name: `routes`: each token's two experts differ and every expert is named somewhere. Among the 256 rows of one index of ctx, for one layer and micro-batch, no expert is named more than 160 times, and in some of these blocks one expert is named exactly 160 times.
All inputs are finite; a program needn't handle non-finite values.
Results may differ from the reference program's by a relative error of at most 0.04.
Values may be sent and summed in bfloat16 or wider, within the bound.
No kernel may reach another device: no remote copies, remote signals or barrier semaphores. Data moves between devices by JAX's collectives and lax.ppermute only.
A program may use at most 256 MiB of HBM per device.

```python
import math
import jax
import jax.numpy as jnp
import numpy as np
from jax import lax

D = 768
HEADS = 12
HD = 64
FF = 3072
TOK_DEV = 256
MICRO = 2
BUCKETS = 32
REACH = 128
EXPERTS = 4
SEQ = 1024
CAP = 160
N_SECTION = 2
N_CTX = 4


def levels(key, dims, cuts, low, top_value):
    gain, own = 1.0, jax.random.fold_in(key, 6)
    for dim, parts in cuts:
        draws = jnp.exp(jax.random.uniform(jax.random.fold_in(own, dim), (parts,), jnp.float32, low / len(cuts), top_value / len(cuts)))
        gain = gain * jnp.repeat(draws, dims[dim] // parts).reshape([-1 if axis == dim else 1 for axis in range(len(dims))])
    return gain


def routed_block(stream_key, own, number, rows, number_of, top, bound, skew):
    order = jax.random.permutation(stream_key, number_of)
    crowded, common = shares(number_of, rows * top, bound, skew, True), shares(number_of, rows * top, bound, skew, False)
    places = jnp.arange(number_of)

    def named(sizes, rotation):
        used = int((sizes > 0).sum())
        fixed = max(1, used // 4)
        shifted = fixed + (places - fixed + rotation * (used - fixed)) % max(1, number_of - fixed)
        return jnp.zeros((number_of,), jnp.int32).at[order[jnp.where(places < fixed, places, shifted)]].set(jnp.asarray(sizes, jnp.int32))

    sizes = jnp.where(number % 4 == 0, named(crowded, number // 4), named(common, number - number // 4 - 1))
    mixed = jax.random.permutation(jax.random.fold_in(own, 3), number_of)
    giver, sink = mixed[0:number_of // 2 * 2:2], mixed[1:number_of // 2 * 2:2]
    slack = jnp.minimum(sizes[giver] - 1, bound - sizes[sink]) // 2
    slack = jnp.where((giver == order[0]) | (sink == order[0]) | (sizes[sink] == 0), 0, jnp.maximum(slack, 0))
    shifted = jax.random.randint(jax.random.fold_in(own, 4), (number_of // 2,), 0, 1 << 20) % (slack + 1)
    sizes = sizes.at[giver].add(-shifted).at[sink].add(shifted)
    items = jnp.searchsorted(jnp.cumsum(sizes), jnp.arange(rows * top), side="right").astype(jnp.int32)
    table = items.reshape(top, rows).T
    table = table[jax.random.permutation(jax.random.fold_in(own, 1), rows)]
    rotation = jax.random.randint(jax.random.fold_in(own, 2), (rows, 1), 0, top)
    return jnp.take_along_axis(table, (jnp.arange(top)[None, :] + rotation) % top, axis=1)


def shares(number_of, total, limit, slope, full):
    portions = [(1 << 20) // math.isqrt(grade ** slope) + 1 for grade in range(1, number_of + 1)]
    largest = limit if full else min(limit, max(-(-total // number_of), total * portions[0] // sum(portions)))
    least = 1 if total - largest >= number_of - 1 else 0
    holding, surplus = [largest] + [least] * (number_of - 1), total - largest - least * (number_of - 1)
    while surplus > 0:
        movable = [i for i in range(1, number_of) if holding[i] < largest] or [i for i in range(1, number_of) if holding[i] < limit]
        whole, budget = sum([portions[i] for i in movable]), surplus
        for i in movable:
            extra = min(limit - holding[i], max(1, budget * portions[i] // whole), surplus)
            holding[i] = holding[i] + extra
            surplus = surplus - extra
    return np.array(holding)


def bell_draw(own_key, shape, scale, most, pieces=(), kind=jnp.bfloat16):
    values = jax.random.normal(own_key, shape, jnp.float32) * scale
    if len(pieces) > 0:
        values = levels(own_key, shape, pieces, -0.22, 0.18) * values
    return jnp.clip(values, min=-most, max=most).astype(kind)


def setup_inputs(seed: int = 0) -> dict:
    streams_of = jax.random.split(jax.random.key(seed), 11)
    boundary = bell_draw(streams_of[0], (N_SECTION, MICRO, SEQ, D), 1.0, 6.0, ((0, 2), (2, 4)))
    norm_first = jnp.clip(1.0 + 0.1 * jax.random.normal(streams_of[1], (N_SECTION, D), jnp.float32), 0.5, 1.5).astype(jnp.bfloat16)
    qkv_weight = bell_draw(streams_of[2], (N_SECTION, 3, D, HEADS * HD), D ** -0.5, 0.21875, ((0, 2), (3, 4)))
    position_bias = bell_draw(streams_of[3], (N_SECTION, BUCKETS, HEADS), 1.0, 4.0, ((0, 2), (2, 4)), jnp.float32)
    out_weight = bell_draw(streams_of[4], (N_SECTION, HEADS * HD, D), (HEADS * HD // 16) ** -0.5, 0.875, ((0, 2), (1, 4)))
    norm_second = jnp.clip(1.0 + 0.1 * jax.random.normal(streams_of[5], (N_SECTION, D), jnp.float32), 0.5, 1.5).astype(jnp.bfloat16)
    router = bell_draw(streams_of[6], (N_SECTION, D, EXPERTS), (2 * D) ** -0.5, 0.15625, ((0, 2),))
    expert_up = bell_draw(streams_of[7], (N_SECTION, EXPERTS, D, FF), D ** -0.5, 0.21875, ((0, 2), (1, 4), (3, 4)))
    expert_down = bell_draw(streams_of[8], (N_SECTION, EXPERTS, FF, D), (FF // 2) ** -0.5, 0.15625, ((0, 2), (1, 4), (2, 4)))
    routes_keys = jax.random.split(jax.random.fold_in(streams_of[9], 1), N_SECTION * MICRO * SEQ // TOK_DEV)
    routes_turns = jax.random.permutation(jax.random.fold_in(streams_of[9], 3), N_SECTION * MICRO * SEQ // TOK_DEV)
    routes = jax.vmap(lambda own, number: routed_block(jax.random.fold_in(streams_of[9], 2), own, number, TOK_DEV, EXPERTS, 2, CAP, 1))(routes_keys, routes_turns).reshape((N_SECTION, MICRO, SEQ, 2))
    return dict(boundary=boundary, norm_first=norm_first, qkv_weight=qkv_weight, position_bias=position_bias, out_weight=out_weight, norm_second=norm_second, router=router, expert_up=expert_up, expert_down=expert_down, routes=routes)


EPSILON = 1e-06
NEGATIVE = -1e+30
HIGHEST = lax.Precision.HIGHEST

@jax.custom_vjp
def low(v):
    return lax.optimization_barrier(v.astype(jnp.bfloat16)).astype(jnp.float32)

@jax.custom_vjp
def low_back(v):
    return v

def low_keep(v):
    return (low(v), None)

def low_pass(kept, grad):
    return (grad,)

def back_keep(v):
    return (v, None)

def back_low(kept, grad):
    return (low(grad),)
low.defvjp(low_keep, low_pass)
low_back.defvjp(back_keep, back_low)

def bucket_of(distance, buckets, reach_max):
    exact_span = buckets // 2
    result = jnp.minimum(distance, exact_span)
    for edge_rank in range(1, buckets - exact_span):
        threshold = int(math.ceil(exact_span * (reach_max / exact_span) ** (edge_rank / (buckets - exact_span))))
        result = result + (distance >= threshold).astype(jnp.int32)
    return result

def rms_norm(values, gain_row):
    scale_rows = lax.rsqrt(lax.optimization_barrier(jnp.mean(values * values, axis=-1, keepdims=True)) + EPSILON)
    return values * scale_rows * gain_row

def dealt_positions(token_count):
    rows = lax.iota(jnp.int32, token_count)
    half = TOK_DEV // 2
    device = rows // TOK_DEV
    local = rows % TOK_DEV
    block = jnp.where(local // half == 0, device, 2 * N_CTX - 1 - device)
    return block * half + local % half

def attend(queries, key_rows, value_rows, bias_table):
    token_count = queries.shape[0]
    block_rows = math.gcd(token_count, 512)
    places = dealt_positions(token_count)
    table_heads = bias_table.T

    def one_block(block_index):
        first_row = block_index * block_rows
        query_block = lax.dynamic_slice_in_dim(queries, first_row, block_rows, 0)
        query_places = lax.dynamic_slice_in_dim(places, first_row, block_rows, 0)
        distance = query_places[:, None] - places[None, :]
        position_term = table_heads[:, bucket_of(jnp.maximum(distance, 0), BUCKETS, REACH)]
        scores = jnp.einsum('qhe,khe->hqk', query_block, key_rows, precision=HIGHEST) * 0.125 + position_term
        scores = jnp.where((distance >= 0)[None], low_back(scores), NEGATIVE)
        row_max = lax.optimization_barrier(jnp.max(scores, axis=2, keepdims=True))
        logsum = row_max + jnp.log(lax.optimization_barrier(jnp.sum(jnp.exp(scores - row_max), axis=2, keepdims=True)))
        return jnp.einsum('hqk,khe->qhe', low(jnp.exp(scores - logsum)), value_rows, precision=HIGHEST)
    mixed_blocks = lax.map(jax.checkpoint(one_block), jnp.arange(token_count // block_rows, dtype=jnp.int32))
    return mixed_blocks.reshape(queries.shape)

def run_layer(inputs, weights, layer_index, pair_routes):
    gain_first = weights[0][layer_index]
    qkv_w = weights[1][layer_index]
    bias_table = weights[2][layer_index]
    out_w = weights[3][layer_index]
    gain_second = weights[4][layer_index]
    router_w = weights[5][layer_index]
    up_w = weights[6][layer_index]
    down_w = weights[7][layer_index]
    token_count = inputs.shape[0]
    width_model = inputs.shape[1]
    head_count = qkv_w.shape[2] // HD
    normed = low(rms_norm(inputs, gain_first))
    projected = low_back(low(jnp.einsum('td,cdf->ctf', normed, qkv_w, precision=HIGHEST)))
    heads_shape = (token_count, head_count, HD)
    mixed = attend(projected[0].reshape(heads_shape), projected[1].reshape(heads_shape), projected[2].reshape(heads_shape), bias_table)
    head_mix = low_back(low(mixed)).reshape(token_count, head_count * HD)
    attended = low_back(jnp.dot(head_mix, out_w, precision=HIGHEST))
    middle = inputs + attended
    expert_in = low(rms_norm(middle, gain_second))
    logits = jnp.dot(expert_in, router_w, precision=HIGHEST)
    gate_values = jax.nn.softmax(jnp.take_along_axis(logits, pair_routes, axis=1), axis=1)
    experts_count = router_w.shape[1]
    block_count = token_count // TOK_DEV
    pair_experts = pair_routes.reshape(block_count, 2 * TOK_DEV)
    onehot = (pair_experts[:, :, None] == jnp.arange(experts_count, dtype=jnp.int32)[None, None, :]).astype(jnp.int32)
    slot_rank = lax.optimization_barrier(jnp.sum(onehot * (jnp.cumsum(onehot, axis=1) - 1), axis=2))
    position = (pair_experts * (block_count * CAP) + jnp.arange(block_count, dtype=jnp.int32)[:, None] * CAP + slot_rank).reshape(-1)
    buffer = jnp.zeros((experts_count * block_count * CAP, width_model), jnp.float32).at[position].set(jnp.repeat(expert_in, 2, axis=0))
    buffer = low_back(buffer).reshape(experts_count, block_count * CAP, width_model)
    pre_act = low_back(jnp.einsum('erd,edf->erf', buffer, up_w, precision=HIGHEST))
    hidden = low(jax.nn.gelu(pre_act, approximate=True))
    slots_out = low_back(low(jnp.einsum('erf,efd->erd', hidden, down_w, precision=HIGHEST)))
    picked = slots_out.reshape(-1, width_model)[position].reshape(token_count, 2, width_model)
    return middle + lax.optimization_barrier(jnp.sum(gate_values[:, :, None] * picked, axis=1))

def reference(boundary, norm_first, qkv_weight, position_bias, out_weight, norm_second, router, expert_up, expert_down, routes):
    weights = (norm_first.astype(jnp.float32), qkv_weight.astype(jnp.float32), position_bias.astype(jnp.float32), out_weight.astype(jnp.float32), norm_second.astype(jnp.float32), router.astype(jnp.float32), expert_up.astype(jnp.float32), expert_down.astype(jnp.float32))

    def forward(inputs, weight_set):
        finals = []
        for micro_index in range(MICRO):
            middle = run_layer(inputs[micro_index], weight_set, 0, routes[0, micro_index])
            passed = low_back(low(middle))
            finals.append(run_layer(passed, weight_set, 1, routes[1, micro_index]))
        return jnp.stack(finals)
    inputs = boundary[0].astype(jnp.float32)
    result, pullback = jax.vjp(forward, inputs, weights)
    grad_inputs, grad_weights = pullback(boundary[1].astype(jnp.float32))
    boundary_out = jnp.stack([grad_inputs, result])
    return (boundary_out, grad_weights[0], grad_weights[1], grad_weights[2], grad_weights[3], grad_weights[4], grad_weights[5], grad_weights[6], grad_weights[7])
```

```python
import math

import jax
import jax.numpy as jnp
from jax import lax
from jax.experimental import pallas as pl
from jax.experimental.pallas import tpu as pltpu
from jax.sharding import PartitionSpec as P

HD = 64
BUCKETS = 32
REACH = 128
EPSILON = 1e-06
NEGATIVE = -1e30
F32 = jnp.float32
BF16 = jnp.bfloat16
LANES = 128
VMEM_BYTES = 40 * 1024 * 1024
ROOT_2_PI = math.sqrt(2.0 / math.pi)


def kernel_call(body, outs, args, scratch=(), flops=0):
    def spec(a):
        scalar = a.ndim == 1 and a.dtype == jnp.int32
        return pl.BlockSpec(memory_space=pltpu.SMEM if scalar else pltpu.VMEM)

    size = sum(math.prod(a.shape) * a.dtype.itemsize for a in list(args) + list(outs))
    return pl.pallas_call(
        body,
        out_shape=outs,
        in_specs=[spec(a) for a in args],
        out_specs=[pl.BlockSpec(memory_space=pltpu.VMEM)] * len(outs),
        scratch_shapes=list(scratch),
        compiler_params=pltpu.CompilerParams(vmem_limit_bytes=VMEM_BYTES),
        cost_estimate=pl.CostEstimate(flops=flops, bytes_accessed=size, transcendentals=0),
    )(*args)


def like(*shape, dtype=BF16):
    return jax.ShapeDtypeStruct(shape, dtype)


def dot(a, b, contract=((1,), (0,))):
    return lax.dot_general(a, b, (contract, ((), ())), preferred_element_type=F32)


def dot_nt(a, b):
    return dot(a, b, ((1,), (1,)))


def dot_tn(a, b):
    return dot(a, b, ((0,), (0,)))


def swap(array, axis, by=1):
    devices = lax.axis_size(axis)
    return lax.ppermute(array, axis, [(i, i ^ by) for i in range(devices)])


def one_way(array, source):
    return lax.ppermute(array, "section", [(source, 1 - source)])


def exchange(chunks, axis):
    return [chunks[0]] + [swap(chunks[r], axis, r) for r in range(1, len(chunks))]


def gather_rows(array, axis):
    return lax.all_gather(array, axis, axis=0, tiled=True)


def project_rows(x, gain, w_ref, normed_ref, q_ref, kv_ref):
    width = q_ref.shape[1]
    scale = lax.rsqrt(jnp.mean(x * x, axis=-1, keepdims=True) + EPSILON)
    normed = (x * scale * gain).astype(BF16)
    normed_ref[...] = normed
    q_ref[...] = dot(normed, w_ref[0]).astype(BF16)
    kv_ref[:, :width] = dot(normed, w_ref[1]).astype(BF16)
    kv_ref[:, width:] = dot(normed, w_ref[2]).astype(BF16)


def project(x, gain, qkv):
    rows, model = x.shape
    width = qkv.shape[2]

    def body(x_ref, gain_ref, w_ref, *outs):
        project_rows(x_ref[...].astype(F32), gain_ref[...], w_ref, *outs)

    return kernel_call(
        body,
        [like(rows, model), like(rows, width), like(rows, 2 * width)],
        [x, gain, qkv],
        flops=6 * rows * model * width,
    )


def score_rows(q, keys, table_ref, scores_ref, head, query_block, n_ctx):
    half = q.shape[0]
    raw = dot_nt(q, keys)
    for key_tile in range(2 * n_ctx):
        owner = key_tile // 2
        key_block = owner if key_tile % 2 == 0 else 2 * n_ctx - 1 - owner
        pick = jnp.clip(query_block - key_block, -1, 2) + 1
        span = slice(key_tile * half, (key_tile + 1) * half)
        scores_ref[:, span] = raw[:, span] * 0.125 + table_ref[head, pick]


def attend(place, q, kv_all, table, n_ctx):
    rows, width = q.shape
    half, heads, keys = rows // 2, width // HD, kv_all.shape[0]

    def body(place_ref, q_ref, kv_ref, table_ref, mix_ref, lse_ref, scores_ref):
        mine = place_ref[0]
        for head in range(heads):
            cols = slice(head * HD, (head + 1) * HD)
            key_rows = kv_ref[:, cols]
            value_rows = kv_ref[:, width + head * HD : width + (head + 1) * HD]
            for part in range(2):
                span = slice(part * half, (part + 1) * half)
                block = mine if part == 0 else 2 * n_ctx - 1 - mine
                score_rows(q_ref[span, cols], key_rows, table_ref, scores_ref, head, block, n_ctx)
                scores = scores_ref[...]
                top = jnp.max(scores, axis=1, keepdims=True)
                mass = jnp.exp(scores - top)
                total = jnp.sum(mass, axis=1, keepdims=True)
                out = dot(mass.astype(BF16), value_rows) / total
                mix_ref[span, cols] = out.astype(BF16)
                lse_ref[span, head : head + 1] = top + jnp.log(total)

    return kernel_call(
        body,
        [like(rows, width), like(rows, heads, dtype=F32)],
        [place, q, kv_all, table],
        [pltpu.VMEM((half, keys), F32)],
        flops=4 * rows * keys * width,
    )


def attend_back(place, q, kv_all, table, lse, dmix, n_ctx):
    rows, width = q.shape
    half, heads, keys = rows // 2, width // HD, kv_all.shape[0]

    def body(place_ref, q_ref, kv_ref, table_ref, lse_ref, dmix_ref, dq_ref, dtable_ref, *rest):
        chunk_refs, (scores_ref, total_ref) = rest[:n_ctx], rest[n_ctx:]
        mine = place_ref[0]
        dtable_ref[...] = jnp.zeros(dtable_ref.shape, F32)
        for head in range(heads):
            cols = slice(head * HD, (head + 1) * HD)
            value_cols = slice(width + head * HD, width + (head + 1) * HD)
            key_rows = kv_ref[:, cols]
            value_rows = kv_ref[:, value_cols]
            for part in range(2):
                span = slice(part * half, (part + 1) * half)
                block = mine if part == 0 else 2 * n_ctx - 1 - mine
                q = q_ref[span, cols]
                dmix = dmix_ref[span, cols]
                score_rows(q, key_rows, table_ref, scores_ref, head, block, n_ctx)
                probs = jnp.exp(scores_ref[...] - lse_ref[span, head : head + 1])
                dprobs = dot_nt(dmix, value_rows)
                delta = jnp.sum(probs * dprobs, axis=1, keepdims=True)
                dscores = (probs * (dprobs - delta)).astype(BF16)
                dq_ref[span, cols] = (dot(dscores, key_rows) * 0.125).astype(BF16)
                dkeys = dot_tn(dscores, q) * 0.125
                dvalues = dot_tn(probs.astype(BF16), dmix)
                if part == 0:
                    total_ref[:, cols] = dkeys
                    total_ref[:, value_cols] = dvalues
                else:
                    total_ref[:, cols] += dkeys
                    total_ref[:, value_cols] += dvalues
                for key_tile in range(2 * n_ctx):
                    owner = key_tile // 2
                    key_block = owner if key_tile % 2 == 0 else 2 * n_ctx - 1 - owner
                    pick = jnp.clip(block - key_block, -1, 2) + 1
                    tile = dscores[:, key_tile * half : (key_tile + 1) * half]
                    dtable_ref[head, pick] += tile.astype(F32)
        for r in range(n_ctx):
            first = pl.multiple_of((mine ^ r) * rows, rows)
            chunk_refs[r][...] = total_ref[pl.ds(first, rows), :].astype(BF16)

    outs = kernel_call(
        body,
        [like(rows, width), like(*table.shape, dtype=F32)] + [like(rows, 2 * width)] * n_ctx,
        [place, q, kv_all, table, lse, dmix],
        [pltpu.VMEM((half, keys), F32), pltpu.VMEM((keys, 2 * width), F32)],
        flops=10 * rows * keys * width,
    )
    return outs[0], outs[1], outs[2:]


def slot_picks(slots_ref, first, count):
    ids = first + lax.broadcasted_iota(jnp.int32, (count, slots_ref.shape[1]), 0)
    hit = (ids == slots_ref[0:1, :]) | (ids == slots_ref[1:2, :])
    return jnp.where(hit, 1.0, 0.0).astype(BF16)


def token_picks(slots_ref, count):
    ids = lax.broadcasted_iota(jnp.int32, (slots_ref.shape[0], count), 1)
    hit = (ids == slots_ref[:, 0:1]) | (ids == slots_ref[:, 1:2])
    return jnp.where(hit, 1.0, 0.0).astype(BF16)


def dispatch_into(rows, place_ref, slots_ref, chunk_refs):
    per = chunk_refs[0].shape[0]
    first = place_ref[1] * (per * len(chunk_refs))
    for r, chunk_ref in enumerate(chunk_refs):
        picks = slot_picks(slots_ref, first + r * per, per)
        chunk_ref[...] = dot(picks, rows).astype(BF16)


def dispatch(place, rows, slots, n_ctx, per):
    model = rows.shape[1]

    def body(place_ref, rows_ref, slots_ref, *chunk_refs):
        dispatch_into(rows_ref[...], place_ref, slots_ref, chunk_refs)

    return kernel_call(body, [like(per, model)] * n_ctx, [place, rows, slots])


def finish_attention(place, mixes, out_w, x, gain, slots, n_ctx, per):
    rows, model = x.shape
    n_heads, width = len(mixes), mixes[0].shape[1]

    def body(place_ref, *refs):
        mix_refs, refs = refs[:n_heads], refs[n_heads:]
        w_ref, x_ref, gain_ref, slots_ref, middle_ref = refs[:5]
        chunk_refs, mixed_ref = refs[5:-1], refs[-1]
        for r in range(n_heads):
            mixed_ref[place_ref[1] ^ r] = mix_refs[r][...]
        middle = x_ref[...].astype(F32)
        attended = dot(mixed_ref[0], w_ref[:width, :])
        for h in range(1, n_heads):
            attended += dot(mixed_ref[h], w_ref[h * width : (h + 1) * width, :])
        middle = middle + attended
        middle_ref[...] = middle
        scale = lax.rsqrt(jnp.mean(middle * middle, axis=-1, keepdims=True) + EPSILON)
        expert_in = (middle * scale * gain_ref[...]).astype(BF16)
        dispatch_into(expert_in, place_ref, slots_ref, chunk_refs)

    outs = kernel_call(
        body,
        [like(rows, model, dtype=F32)] + [like(per, model)] * n_ctx,
        [place, *mixes, out_w, x, gain, slots],
        [pltpu.VMEM((n_heads, rows, width), BF16)],
        flops=2 * rows * model * model + 2 * rows * model * per * n_ctx,
    )
    return outs[0], outs[1:]


def gelu_parts(v):
    inner = jnp.tanh(ROOT_2_PI * (v + 0.044715 * v * v * v))
    return inner, 0.5 * v * (1.0 + inner)


def experts(place, arrived, up, down, router, other, n_heads):
    slots, model = arrived.shape
    per, hidden_width = slots // n_heads, up.shape[1]

    def body(place_ref, in_ref, up_ref, down_ref, router_ref, other_ref, *refs):
        chunk_refs, (pre_ref, hidden_ref, margin_ref) = refs[:n_heads], refs[n_heads:]
        for r in range(n_heads):
            span = pl.ds(pl.multiple_of((place_ref[1] ^ r) * per, per), per)
            rows = in_ref[span, :]
            logits = dot(rows, router_ref[...])
            lane = lax.broadcasted_iota(jnp.int32, logits.shape, 1)
            signs = jnp.where(lane == place_ref[0], 1.0, 0.0) - jnp.where(
                lane == other_ref[span, :], 1.0, 0.0
            )
            margin = jnp.sum(logits * signs, axis=1, keepdims=True)
            margin_ref[span, :] = margin
            gate = 1.0 / (1.0 + jnp.exp(-margin))
            pre_act = dot(rows, up_ref[...])
            pre_ref[span, :] = pre_act
            hidden = gelu_parts(pre_act)[1].astype(BF16)
            hidden_ref[span, :] = hidden
            chunk_refs[r][...] = (gate * dot(hidden, down_ref[...])).astype(BF16)

    outs = kernel_call(
        body,
        [like(per, model)] * n_heads
        + [
            like(slots, hidden_width, dtype=F32),
            like(slots, hidden_width),
            like(slots, 1, dtype=F32),
        ],
        [place, arrived, up, down, router, other],
        flops=4 * slots * model * hidden_width,
    )
    return outs[:n_heads], outs[n_heads:]


def experts_back(place, dout_rows, kept, up, down, router, other, n_heads):
    pre_act, hidden, margin = kept
    slots, model = dout_rows.shape
    per, hidden_width = slots // n_heads, up.shape[1]

    def body(place_ref, dout_ref, pre_ref, hidden_ref, margin_ref, up_ref, down_ref, router_ref, other_ref, *refs):
        chunk_refs, (dpre_ref, dslots_ref, dlogits_ref) = refs[:n_heads], refs[n_heads:]
        for r in range(n_heads):
            span = pl.ds(pl.multiple_of((place_ref[1] ^ r) * per, per), per)
            dout = dout_ref[span, :]
            dhidden = dot_nt(dout, down_ref[...])
            margin = margin_ref[span, :]
            gate = 1.0 / (1.0 + jnp.exp(-margin))
            other_gate = 1.0 / (1.0 + jnp.exp(margin))
            dgate = jnp.sum(dhidden * hidden_ref[span, :].astype(F32), axis=1, keepdims=True)
            v = pre_ref[span, :]
            inner, _ = gelu_parts(v)
            slope = 0.5 * (1.0 + inner) + 0.5 * v * (1.0 - inner * inner) * ROOT_2_PI * (
                1.0 + 3.0 * 0.044715 * v * v
            )
            dpre = (gate * dhidden * slope).astype(BF16)
            dpre_ref[span, :] = dpre
            dslots_ref[span, :] = (gate * dout.astype(F32)).astype(BF16)
            lane = lax.broadcasted_iota(jnp.int32, (per, LANES), 1)
            signs = jnp.where(lane == place_ref[0], 1.0, 0.0) - jnp.where(
                lane == other_ref[span, :], 1.0, 0.0
            )
            dlogits = (gate * other_gate * dgate * signs).astype(BF16)
            dlogits_ref[span, :] = dlogits
            chunk_refs[r][...] = (
                dot_nt(dpre, up_ref[...]) + dot_nt(dlogits, router_ref[...])
            ).astype(BF16)

    outs = kernel_call(
        body,
        [like(per, model)] * n_heads
        + [like(slots, hidden_width), like(slots, model), like(slots, LANES)],
        [place, dout_rows, pre_act, hidden, margin, up, down, router, other],
        flops=4 * slots * model * hidden_width,
    )
    return outs[:n_heads], outs[n_heads:]


def combine(middle, returned, tokens):
    rows, model = middle.shape

    def body(middle_ref, returned_ref, tokens_ref, out_ref):
        picks = token_picks(tokens_ref, returned_ref.shape[0])
        out_ref[...] = middle_ref[...] + dot(picks, returned_ref[...])

    return kernel_call(
        body,
        [like(rows, model, dtype=F32)],
        [middle, returned, tokens],
        flops=2 * rows * model * returned.shape[0],
    )[0]


def combine_project(middle, returned, tokens, gain, qkv):
    rows, model = middle.shape
    width = qkv.shape[2]

    def body(middle_ref, returned_ref, tokens_ref, gain_ref, w_ref, passed_ref, *outs):
        picks = token_picks(tokens_ref, returned_ref.shape[0])
        passed = (middle_ref[...] + dot(picks, returned_ref[...])).astype(BF16)
        passed_ref[...] = passed
        project_rows(passed.astype(F32), gain_ref[...], w_ref, *outs)

    return kernel_call(
        body,
        [like(rows, model), like(rows, model), like(rows, width), like(rows, 2 * width)],
        [middle, returned, tokens, gain, qkv],
        flops=2 * rows * model * returned.shape[0] + 6 * rows * model * width,
    )


def norm_back(values, gain, upstream):
    scale = lax.rsqrt(jnp.mean(values * values, axis=-1, keepdims=True) + EPSILON)
    unit = values * scale
    scaled = upstream * gain
    dvalues = scale * (scaled - unit * jnp.mean(unit * scaled, axis=-1, keepdims=True))
    return dvalues, jnp.sum(upstream * unit, axis=0, keepdims=True)


def middle_back(returned, tokens, middle, gain, dout, out_w):
    rows, model = middle.shape
    width = out_w.shape[0]

    def body(returned_ref, tokens_ref, middle_ref, gain_ref, dout_ref, w_ref, dmiddle_ref, datt_ref, dmix_ref, dgain_ref):
        picks = token_picks(tokens_ref, returned_ref.shape[0])
        dexpert_in = dot(picks, returned_ref[...])
        part, dgain = norm_back(middle_ref[...], gain_ref[...], dexpert_in)
        dgain_ref[...] = dgain
        dmiddle = dout_ref[...].astype(F32) + part
        dmiddle_ref[...] = dmiddle
        datt = dmiddle.astype(BF16)
        datt_ref[...] = datt
        dmix_ref[...] = dot_nt(datt, w_ref[...]).astype(BF16)

    return kernel_call(
        body,
        [
            like(rows, model, dtype=F32),
            like(rows, model),
            like(rows, width),
            like(1, model, dtype=F32),
        ],
        [returned, tokens, middle, gain, dout, out_w],
        flops=2 * rows * model * (returned.shape[0] + width),
    )


def project_back(place, dq, dkv_parts, qkv, n_heads):
    rows, width = dq.shape
    model, n_parts = qkv.shape[1], len(dkv_parts)
    share = rows // n_heads

    def body(place_ref, dq_ref, *refs):
        part_refs, refs = refs[:n_parts], refs[n_parts:]
        w_ref, dkv_ref = refs[:2]
        chunk_refs, total_ref = refs[2:-1], refs[-1]
        dkv = part_refs[0][...].astype(F32)
        for ref in part_refs[1:]:
            dkv += ref[...].astype(F32)
        dkv = dkv.astype(BF16)
        dkv_ref[...] = dkv
        total_ref[...] = (
            dot_nt(dq_ref[...], w_ref[0])
            + dot_nt(dkv[:, :width], w_ref[1])
            + dot_nt(dkv[:, width:], w_ref[2])
        )
        for r in range(n_heads):
            first = pl.multiple_of((place_ref[1] ^ r) * share, share)
            chunk_refs[r][...] = total_ref[pl.ds(first, share), :].astype(BF16)

    outs = kernel_call(
        body,
        [like(rows, 2 * width)] + [like(share, model)] * n_heads,
        [place, dq, *dkv_parts, qkv],
        [pltpu.VMEM((rows, model), F32)],
        flops=6 * rows * model * width,
    )
    return outs[0], outs[1:]


def input_back(place, dnormed_parts, x, gain, dmiddle, slots=None, n_ctx=0, per=0):
    rows, model = x.shape
    n_heads, share = len(dnormed_parts), dnormed_parts[0].shape[0]

    def body(place_ref, *refs):
        part_refs, refs = refs[:n_heads], refs[n_heads:]
        x_ref, gain_ref, dmiddle_ref = refs[:3]
        refs = refs[3:] if slots is None else refs[4:]
        dx_ref, dgain_ref = refs[:2]
        chunk_refs, dnormed_ref = refs[2:-1], refs[-1]
        for r in range(n_heads):
            first = pl.multiple_of((place_ref[1] ^ r) * share, share)
            dnormed_ref[pl.ds(first, share), :] = part_refs[r][...].astype(F32)
        part, dgain = norm_back(x_ref[...].astype(F32), gain_ref[...], dnormed_ref[...])
        dgain_ref[...] = dgain
        dx = (dmiddle_ref[...] + part).astype(dx_ref.dtype)
        dx_ref[...] = dx
        if chunk_refs:
            dispatch_into(dx, place_ref, refs_slots[0], chunk_refs)

    refs_slots = []

    def wrapped(place_ref, *refs):
        if slots is not None:
            refs_slots[:] = [refs[n_heads + 3]]
        body(place_ref, *refs)

    outs = kernel_call(
        wrapped,
        [like(rows, model, dtype=F32 if slots is None else BF16), like(1, model, dtype=F32)]
        + [like(per, model)] * n_ctx,
        [place, *dnormed_parts, x, gain, dmiddle] + ([] if slots is None else [slots]),
        [pltpu.VMEM((rows, model), F32)],
    )
    return outs[0], outs[1], outs[2:]


def table_back(dtable, buckets):
    heads, half = dtable.shape[0], dtable.shape[3]

    def body(dtable_ref, buckets_ref, out_ref):
        held = buckets_ref[...]
        for bucket in range(BUCKETS):
            hit = held == bucket
            for head in range(heads):
                kept = jnp.where(hit, dtable_ref[head, 1:], 0.0)
                out_ref[bucket * heads + head : bucket * heads + head + 1, :] = jnp.sum(
                    jnp.sum(kept, axis=0), axis=0, keepdims=True
                )

    return kernel_call(body, [like(BUCKETS * heads, half, dtype=F32)], [dtable, buckets])[0]


def bucket_of(distance):
    exact_span = BUCKETS // 2
    result = jnp.minimum(distance, exact_span)
    for rank in range(1, BUCKETS - exact_span):
        edge = int(
            math.ceil(exact_span * (REACH / exact_span) ** (rank / (BUCKETS - exact_span)))
        )
        result = result + (distance >= edge).astype(jnp.int32)
    return result


def tile_buckets(half):
    row = lax.broadcasted_iota(jnp.int32, (half, half), 0)
    col = lax.broadcasted_iota(jnp.int32, (half, half), 1)
    same = jnp.where(row >= col, bucket_of(jnp.maximum(row - col, 0)), -1)
    return jnp.stack([same, bucket_of(half + row - col), bucket_of(2 * half + row - col)])


def bias_table(buckets, bias):
    half = buckets.shape[1]
    value = jnp.full((bias.shape[1],) + buckets.shape, NEGATIVE, F32)
    for bucket in range(BUCKETS):
        value = jnp.where(buckets[None] == bucket, bias[bucket][:, None, None, None], value)
    hidden = jnp.full((bias.shape[1], 1, half, half), NEGATIVE, F32)
    return jnp.concatenate([hidden, value], axis=1)


def slot_ids(routes, n_experts, per, n_heads, ctx_index):
    rows = routes.shape[0]
    pairs = routes.reshape(-1)
    hot = (pairs[:, None] == lax.iota(jnp.int32, n_experts)[None, :]).astype(BF16)
    order = lax.iota(jnp.int32, 2 * rows)
    before = (order[:, None] > order[None, :]).astype(BF16)
    rank = jnp.sum(dot(before, hot) * hot.astype(F32), axis=1).astype(jnp.int32)
    slot = (rank // per) * (per * n_experts) + (pairs ^ ctx_index) * per + rank % per
    return slot.reshape(rows, 2)


def return_rows(chunks, n_ctx):
    parts = exchange(chunks, "heads")
    total = parts[0].astype(F32)
    for part in parts[1:]:
        total = total + part.astype(F32)
    total = total.astype(BF16)
    per = total.shape[0] // n_ctx
    back = exchange([total[r * per : (r + 1) * per] for r in range(n_ctx)], "ctx")
    return gather_rows(jnp.concatenate(back, axis=0), "heads")


def send_rows(chunks):
    return gather_rows(jnp.concatenate(exchange(chunks, "ctx"), axis=0), "heads")


def body(
    boundary,
    norm_first,
    qkv_weight,
    position_bias,
    out_weight,
    norm_second,
    router,
    expert_up,
    expert_down,
    routes,
):
    section = lax.axis_index("section")
    ctx_index = lax.axis_index("ctx")
    heads_index = lax.axis_index("heads")
    n_ctx, n_heads = lax.axis_size("ctx"), lax.axis_size("heads")
    first = section == 0
    place = jnp.stack([ctx_index, heads_index]).astype(jnp.int32)
    rows, model = boundary.shape[2:]
    half = rows // 2
    n_experts = router.shape[2]
    per = 5 * rows // (2 * n_experts) // n_heads

    def both(own):
        other = swap(own, "section")
        return jnp.where(first, own, other), jnp.where(first, other, own)

    given = swap(jnp.where(first, boundary[0, 1], boundary[0, 0]), "section")
    x0 = jnp.where(first, boundary[0, 0], given)
    cotangent = jnp.where(first, given, boundary[0, 1])
    gains_first = [g.astype(F32) for g in both(norm_first)]
    qkv = both(qkv_weight[0])
    tables = both(position_bias[0])
    own_routes = jnp.where(first, routes[0, 0], routes[0, 1])
    got_routes = swap(jnp.where(first, routes[0, 1], routes[0, 0]), "section")
    layer_routes = (
        jnp.where(first, own_routes, got_routes),
        jnp.where(first, got_routes, own_routes),
    )
    gains_second = [g.astype(F32) for g in both(norm_second)]
    out_full = both(gather_rows(out_weight[0], "heads"))
    out_own = both(out_weight[0])
    router_wide = both(jnp.pad(router[0], ((0, 0), (0, LANES - n_experts))))
    up = both(expert_up[0, 0])
    down = both(expert_down[0, 0])

    tokens = [slot_ids(r, n_experts, per, n_heads, ctx_index) for r in layer_routes]
    slots = [t.T for t in tokens]
    quarter = n_ctx * per
    here = heads_index * quarter + lax.iota(jnp.int32, quarter)
    others = []
    for t, r in zip(tokens, layer_routes):
        hit = here[:, None, None] == t[None]
        others.append(jnp.sum(jnp.where(hit, r[:, ::-1][None], 0), axis=(1, 2)))
    others = jnp.stack(others).astype(F32).reshape(2, n_ctx, per)
    others = jnp.stack(exchange([others[:, r] for r in range(n_ctx)], "ctx"))
    others = lax.all_gather(others, "heads")
    others = [others[:, :, layer].reshape(-1, 1).astype(jnp.int32) for layer in range(2)]
    buckets = tile_buckets(half)
    biases = [bias_table(buckets, t) for t in tables]

    def forward(layer, x, normed, q, kv):
        kv_all = gather_rows(kv, "ctx")
        mix, lse = attend(place, q, kv_all, biases[layer], n_ctx)
        mixes = exchange([mix] * n_heads, "heads")
        middle, chunks = finish_attention(
            place, mixes, out_full[layer], x, gains_second[layer], slots[layer], n_ctx, per
        )
        arrived = send_rows(chunks)
        partial, kept = experts(
            place, arrived, up[layer], down[layer], router_wide[layer], others[layer], n_heads
        )
        state = (x, normed, q, kv_all, lse, mix, middle, arrived, kept)
        return state, partial

    def backward(layer, state, dout, dout_rows):
        x, normed, q, kv_all, lse, mix, middle, arrived, kept = state
        chunks, (dpre, dslots, dlogits) = experts_back(
            place,
            dout_rows,
            kept,
            up[layer],
            down[layer],
            router_wide[layer],
            others[layer],
            n_heads,
        )
        dreturned = return_rows(chunks, n_ctx)
        grad_up = dot_tn(arrived, dpre)
        grad_down = dot_tn(kept[1], dslots)
        grad_router = dot_tn(arrived, dlogits)[:, :n_experts]
        dmiddle, datt, dmix, dgain_second = middle_back(
            dreturned, tokens[layer], middle, gains_second[layer], dout, out_own[layer]
        )
        grad_out = dot_tn(datt, mix)
        dq, dtable, dkv = attend_back(place, q, kv_all, biases[layer], lse, dmix, n_ctx)
        dkv_parts = exchange(dkv, "ctx")
        lanes = table_back(dtable, buckets)
        grad_bias = jnp.sum(lanes, axis=1).reshape(BUCKETS, -1)
        dkv_sum, chunks = project_back(place, dq, dkv_parts, qkv[layer], n_heads)
        parts = exchange(chunks, "heads")
        total = parts[0].astype(F32)
        for part in parts[1:]:
            total = total + part.astype(F32)
        dnormed_parts = exchange([total.astype(BF16)] * n_heads, "heads")
        grad_qkv = dot_tn(normed, jnp.concatenate([dq, dkv_sum], axis=1))
        if layer == 1:
            dx, dgain_first, sent = input_back(
                place, dnormed_parts, x, gains_first[layer], dmiddle, slots[0], n_ctx, per
            )
        else:
            dx, dgain_first, sent = input_back(
                place, dnormed_parts, x, gains_first[layer], dmiddle
            )
        dense = jnp.concatenate([grad_qkv, grad_out], axis=1)
        small = (dgain_first[0], dgain_second[0], grad_bias, grad_router)
        return dx, sent, dense, small, (grad_up, grad_down)

    dout_rows1 = send_rows(dispatch(place, cotangent, slots[1], n_ctx, per))
    normed, q, kv = project(x0, gains_first[0], qkv[0])
    state0, partial = forward(0, x0, normed, q, kv)
    returned = return_rows(partial, n_ctx)
    x1, normed, q, kv = combine_project(
        state0[6], returned, tokens[0], gains_first[1], qkv[1]
    )
    state1, partial = forward(1, x1, normed, q, kv)
    returned1 = return_rows(partial, n_ctx)
    out = combine(state1[6], returned1, tokens[1])
    dx1, sent, dense1, small1, expert1 = backward(1, state1, cotangent, dout_rows1)
    dx0, _, dense0, small0, expert0 = backward(0, state0, dx1, send_rows(sent))

    def settle(layer0, layer1):
        got = jnp.where(
            first,
            one_way(layer0.astype(BF16), 1).astype(F32),
            one_way(layer1.astype(BF16), 0).astype(F32),
        )
        return jnp.where(first, layer0, layer1) + got

    grad_up, grad_down = (settle(a, b) for a, b in zip(expert0, expert1))
    dense = settle(dense0, dense1)
    gain_first_sum, gain_second_sum, bias_sum, router_sum = (
        settle(a, b) for a, b in zip(small0, small1)
    )
    dense = lax.psum_scatter(
        dense.astype(BF16), "ctx", scatter_dimension=0, tiled=True
    ).astype(F32)
    width = qkv_weight.shape[3]
    grad_qkv = jnp.stack([dense[:, i * width : (i + 1) * width] for i in range(3)])
    grad_out = dense[:, 3 * width :].T

    def share(array):
        return lax.psum_scatter(array, "ctx", scatter_dimension=0, tiled=True)

    router_sum = lax.psum(router_sum, "heads")
    got_out = one_way(out, 0)
    got_dx = one_way(dx0, 1)
    boundary_out = jnp.stack([jnp.where(first, dx0, got_out), jnp.where(first, got_dx, out)])
    return (
        boundary_out[None],
        share(gain_first_sum)[None],
        grad_qkv[None],
        share(bias_sum)[None],
        grad_out[None],
        share(gain_second_sum)[None],
        share(router_sum)[None],
        grad_up[None, None],
        grad_down[None, None],
    )


def solution(mesh):
    placed = (
        P("section", None, "ctx", None),
        P("section", None),
        P("section", None, None, "heads"),
        P("section", None, "heads"),
        P("section", "heads", None),
        P("section", None),
        P("section", None, None),
        P("section", "ctx", None, "heads"),
        P("section", "ctx", "heads", None),
        P("section", None, "ctx", None),
    )
    return jax.shard_map(
        body,
        mesh=mesh,
        in_specs=placed,
        out_specs=(
            P("section", None, "ctx", None),
            P("section", "ctx"),
            P("section", None, "ctx", "heads"),
            P("section", "ctx", "heads"),
            P("section", "heads", "ctx"),
            P("section", "ctx"),
            P("section", "ctx", None),
            P("section", "ctx", None, "heads"),
            P("section", "ctx", "heads", None),
        ),
        check_vma=False,
    )
```

```python
import math

import jax
import jax.numpy as jnp
from jax import lax
from jax.experimental import pallas as pl
from jax.experimental.pallas import tpu as pltpu
from jax.sharding import PartitionSpec as P

HD = 64
BUCKETS = 32
REACH = 128
EPSILON = 1e-06
NEGATIVE = -1e30
F32 = jnp.float32
BF16 = jnp.bfloat16
LANES = 128
SPARE_BYTES = 6 * 1024 * 1024
ROOT_2_PI = math.sqrt(2.0 / math.pi)


class Pick:
    def __init__(self, first, second):
        self.arrays, self.shape = (first, second), first.shape
        self.dtype, self.ndim = first.dtype, first.ndim


class Rows:
    def __init__(self, array, layer, width, own=False):
        n_heads = array.shape[0] // (2 * width)
        self.array, self.layer, self.width, self.own = array, layer, width, own
        self.shape = (width if own else n_heads * width,) + array.shape[1:]
        self.dtype, self.ndim, self.n_heads = array.dtype, array.ndim, n_heads


class Held:
    def __init__(self, buffer, wait):
        self.buffer, self.wait, self.here = buffer, wait, False

    def ready(self):
        if not self.here:
            self.wait()
        self.here = True
        return self.buffer


def padded_bytes(array):
    *lead, rows, lanes = (1, 1) + tuple(array.shape)
    return math.prod(lead) * (-(-rows // 16) * 16) * (-(-lanes // LANES) * LANES) * jnp.dtype(array.dtype).itemsize


def kernel_call(body, outs, args, scratch=(), flops=0, after=()):
    picks = [a for a in args if isinstance(a, (Pick, Rows))]
    operands, in_specs = [], []
    for a in args:
        if isinstance(a, (Pick, Rows)):
            arrays = a.arrays if isinstance(a, Pick) else (a.array,)
            operands += arrays
            in_specs += [pl.BlockSpec(memory_space=pltpu.HBM)] * len(arrays)
        else:
            scalar = a.ndim == 1 and a.dtype == jnp.int32
            operands.append(a)
            in_specs.append(pl.BlockSpec(memory_space=pltpu.SMEM if scalar else pltpu.VMEM))
    operands += after
    in_specs += [pl.BlockSpec(memory_space=pl.ANY)] * len(after)
    scratch = list(scratch) + [pltpu.VMEM(p.shape, p.dtype) for p in picks]
    if picks:
        scratch.append(pltpu.SemaphoreType.DMA((len(picks),)))
    n_out, n_own = len(outs), len(scratch) - len(picks) - (1 if picks else 0)

    def hold(a, sources, place_ref, buffer, sem):
        if isinstance(a, Pick):
            for section, src in enumerate(sources):

                @pl.when(place_ref[2] == section)
                def _(src=src):
                    pltpu.make_async_copy(src, buffer, sem).start()

            return Held(buffer, pltpu.make_async_copy(sources[0], buffer, sem).wait)
        copies = []
        for h in range(1 if a.own else a.n_heads):
            block = 2 * (place_ref[1] if a.own else h) + (place_ref[2] ^ a.layer)
            src = sources[0].at[pl.ds(pl.multiple_of(block * a.width, a.width), a.width)]
            dst = buffer.at[pl.ds(h * a.width, a.width)]
            copies.append(pltpu.make_async_copy(src, dst, sem))
            copies[-1].start()

        def wait():
            for copy in copies:
                copy.wait()

        return Held(buffer, wait)

    def wrapped(*refs):
        ins, rest = refs[: len(operands)], refs[len(operands) :]
        buffers = list(rest[n_out + n_own :])
        given, at, number = [], 0, 0
        for a in args:
            if not isinstance(a, (Pick, Rows)):
                given.append(ins[at])
                at += 1
                continue
            count = 2 if isinstance(a, Pick) else 1
            sem = buffers[-1].at[number]
            given.append(hold(a, ins[at : at + count], ins[0], buffers[number], sem))
            at, number = at + count, number + 1
        body(*given, *rest[: n_out + n_own])

    size = sum(math.prod(a.shape) * a.dtype.itemsize for a in list(args) + list(outs))
    held = sum(map(padded_bytes, list(args) + list(outs)))
    held += sum(padded_bytes(s) for s in scratch[: n_own])
    return pl.pallas_call(
        wrapped,
        out_shape=outs,
        in_specs=in_specs,
        out_specs=[pl.BlockSpec(memory_space=pltpu.VMEM)] * n_out,
        scratch_shapes=scratch,
        compiler_params=pltpu.CompilerParams(vmem_limit_bytes=held + SPARE_BYTES),
        cost_estimate=pl.CostEstimate(flops=flops, bytes_accessed=size, transcendentals=0),
    )(*operands)


def like(*shape, dtype=BF16):
    return jax.ShapeDtypeStruct(shape, dtype)


def dot(a, b, contract=((1,), (0,))):
    return lax.dot_general(a, b, (contract, ((), ())), preferred_element_type=F32)


def dot_nt(a, b):
    return dot(a, b, ((1,), (1,)))


def dot_tn(a, b):
    return dot(a, b, ((0,), (0,)))


def swap(array, axis, by=1):
    devices = lax.axis_size(axis)
    return lax.ppermute(array, axis, [(i, i ^ by) for i in range(devices)])


def one_way(array, source):
    return lax.ppermute(array, "section", [(source, 1 - source)])


def exchange(chunks, axis):
    return [chunks[0]] + [swap(chunks[r], axis, r) for r in range(1, len(chunks))]


def gather_rows(array, axis):
    return lax.all_gather(array, axis, axis=0, tiled=True)


def project_rows(x, gain, w, normed_ref, q_ref, kv_ref):
    width = q_ref.shape[1]
    scale = lax.rsqrt(jnp.mean(x * x, axis=-1, keepdims=True) + EPSILON)
    normed = (x * scale * gain).astype(BF16)
    normed_ref[...] = normed
    w_ref = w.ready()
    kv_ref[:, :width] = dot(normed, w_ref[1]).astype(BF16)
    kv_ref[:, width:] = dot(normed, w_ref[2]).astype(BF16)
    q_ref[...] = dot(normed, w_ref[0]).astype(BF16)


def either(place_ref, first, second):
    return jnp.where(place_ref[2] == 0, first, second)


def begin(place, own, given, gain_own, gain_other, qkv):
    _, rows, model = own.shape
    width = qkv.shape[2]

    def body(place_ref, own_ref, given_ref, gain_ref, other_ref, w, x_ref, cotangent_ref, *outs):
        x = either(place_ref, own_ref[0], given_ref[...])
        x_ref[...] = x
        cotangent_ref[...] = either(place_ref, given_ref[...], own_ref[1])
        gain = either(place_ref, gain_ref[...].astype(F32), other_ref[...].astype(F32))
        project_rows(x.astype(F32), gain, w, *outs)

    return kernel_call(
        body,
        [like(rows, model)] * 3 + [like(rows, width), like(rows, 2 * width)],
        [place, own, given, gain_own, gain_other, qkv],
        flops=6 * rows * model * width,
    )


def tile_pick(block, key_tile, mine, ordered, n_ctx):
    owner = key_tile // 2 if ordered else mine ^ (key_tile // 2)
    key_block = owner if key_tile % 2 == 0 else 2 * n_ctx - 1 - owner
    return jnp.clip(block - key_block, -1, 2) + 1


def query_parts(mine, half, n_ctx):
    return [
        (slice(0, half), mine),
        (slice(half, 2 * half), 2 * n_ctx - 1 - mine),
    ]


def load_keys(kv_refs, kv_ref):
    rows = kv_refs[0].shape[0]
    for r, ref in enumerate(kv_refs):
        kv_ref[r * rows : (r + 1) * rows, :] = ref[...]


def attend(place, q, kv_parts, table, n_ctx):
    rows, width = q.shape
    half, heads, keys = rows // 2, width // HD, rows * n_ctx
    ordered, count = len(kv_parts) == 1, len(kv_parts)

    def body(place_ref, q_ref, *refs):
        kv_refs, (table_ref, mix_ref, lse_ref, scores_ref, kv_ref) = refs[:count], refs[count:]
        mine = place_ref[0]
        load_keys(kv_refs, kv_ref)
        for head in range(heads):
            cols = slice(head * HD, (head + 1) * HD)
            key_rows = kv_ref[:, cols]
            value_rows = kv_ref[:, width + head * HD : width + (head + 1) * HD]
            for part, (span, block) in enumerate(query_parts(mine, half, n_ctx)):
                raw = dot_nt(q_ref[span, cols], key_rows)
                for key_tile in range(2 * n_ctx):
                    pick = tile_pick(block, key_tile, mine, ordered, n_ctx)
                    tile = slice(key_tile * half, (key_tile + 1) * half)
                    scores_ref[part, :, tile] = raw[:, tile] * 0.125 + table_ref[head, pick]
                scores = scores_ref[part]
                top = jnp.max(scores, axis=1, keepdims=True)
                mass = jnp.exp(scores - top)
                total = jnp.sum(mass, axis=1, keepdims=True)
                out = dot(mass.astype(BF16), value_rows) / total
                mix_ref[span, cols] = out.astype(BF16)
                lse_ref[span, head : head + 1] = top + jnp.log(total)

    return kernel_call(
        body,
        [like(rows, width), like(rows, heads, dtype=F32)],
        [place, q, *kv_parts, table],
        [pltpu.VMEM((2, half, keys), F32), pltpu.VMEM((keys, 2 * width), BF16)],
        flops=4 * rows * keys * width,
    )


def attend_back(place, q, kv_parts, table, lse, dmix, n_ctx):
    rows, width = q.shape
    half, heads, keys = rows // 2, width // HD, rows * n_ctx
    ordered, count = len(kv_parts) == 1, len(kv_parts)

    def body(place_ref, q_ref, *refs):
        kv_refs, refs = refs[:count], refs[count:]
        table_ref, lse_ref, dmix_ref, dq_ref, dtable_ref = refs[:5]
        chunk_refs, (scores_ref, total_ref, kv_ref) = refs[5 : 5 + n_ctx], refs[5 + n_ctx :]
        mine = place_ref[0]
        load_keys(kv_refs, kv_ref)
        dtable_ref[...] = jnp.zeros(dtable_ref.shape, F32)
        for head in range(heads):
            cols = slice(head * HD, (head + 1) * HD)
            value_cols = slice(width + head * HD, width + (head + 1) * HD)
            key_rows = kv_ref[:, cols]
            value_rows = kv_ref[:, value_cols]
            for part, (span, block) in enumerate(query_parts(mine, half, n_ctx)):
                q = q_ref[span, cols]
                dmix = dmix_ref[span, cols]
                raw = dot_nt(q, key_rows)
                for key_tile in range(2 * n_ctx):
                    pick = tile_pick(block, key_tile, mine, ordered, n_ctx)
                    tile = slice(key_tile * half, (key_tile + 1) * half)
                    scores_ref[part, :, tile] = raw[:, tile] * 0.125 + table_ref[head, pick]
                probs = jnp.exp(scores_ref[part] - lse_ref[span, head : head + 1])
                dprobs = dot_nt(dmix, value_rows)
                delta = jnp.sum(probs * dprobs, axis=1, keepdims=True)
                dscores = (probs * (dprobs - delta)).astype(BF16)
                dq_ref[span, cols] = (dot(dscores, key_rows) * 0.125).astype(BF16)
                dkeys = dot_tn(dscores, q) * 0.125
                dvalues = dot_tn(probs.astype(BF16), dmix)
                if part == 0:
                    total_ref[:, cols] = dkeys
                    total_ref[:, value_cols] = dvalues
                else:
                    total_ref[:, cols] += dkeys
                    total_ref[:, value_cols] += dvalues
                for key_tile in range(2 * n_ctx):
                    pick = tile_pick(block, key_tile, mine, ordered, n_ctx)
                    tile = dscores[:, key_tile * half : (key_tile + 1) * half]
                    dtable_ref[head, pick] += tile.astype(F32)
        for r in range(n_ctx):
            first = pl.multiple_of((mine ^ r if ordered else r) * rows, rows)
            chunk_refs[r][...] = total_ref[pl.ds(first, rows), :].astype(BF16)

    outs = kernel_call(
        body,
        [like(rows, width), like(*table.shape, dtype=F32)] + [like(rows, 2 * width)] * n_ctx,
        [place, q, *kv_parts, table, lse, dmix],
        [
            pltpu.VMEM((2, half, keys), F32),
            pltpu.VMEM((keys, 2 * width), F32),
            pltpu.VMEM((keys, 2 * width), BF16),
        ],
        flops=10 * rows * keys * width,
    )
    return outs[0], outs[1], outs[2:]


def token_picks(tokens_ref, count, first=0):
    ids = first + lax.broadcasted_iota(jnp.int32, (tokens_ref.shape[0], count), 1)
    hit = (ids == tokens_ref[:, 0:1]) | (ids == tokens_ref[:, 1:2])
    return jnp.where(hit, 1.0, 0.0).astype(BF16)


def dispatch_into(rows, place_ref, tokens_ref, chunk_refs):
    per = chunk_refs[0].shape[0]
    first = place_ref[1] * (per * len(chunk_refs))
    for r, chunk_ref in enumerate(chunk_refs):
        picks = token_picks(tokens_ref, per, first + r * per)
        chunk_ref[...] = dot_tn(picks, rows).astype(BF16)


def dispatch_whole(place, rows, tokens, n_ctx, per, n_heads, after):
    count, model = rows.shape

    def body(place_ref, rows_ref, tokens_ref, *chunk_refs):
        lane = lax.broadcasted_iota(jnp.int32, (count, n_heads * per), 1)
        ids = lane
        for h in range(1, n_heads):
            ids += jnp.where(lane >= h * per, (n_ctx - 1) * per, 0)
        for r, chunk_ref in enumerate(chunk_refs):
            here = ids + r * per
            hit = (here == tokens_ref[:, 0:1]) | (here == tokens_ref[:, 1:2])
            picks = jnp.where(hit, 1.0, 0.0).astype(BF16)
            chunk_ref[...] = dot_tn(picks, rows_ref[...]).astype(BF16)

    return kernel_call(
        body, [like(n_heads * per, model)] * n_ctx, [place, rows, tokens], after=after
    )


def finish_attention(place, mixes, out_w, x, gain, tokens, n_ctx, per):
    rows, model = x.shape
    n_heads, width = len(mixes), mixes[0].shape[1]

    def body(place_ref, *refs):
        mix_refs, refs = refs[:n_heads], refs[n_heads:]
        w_ref, x_ref, gain_ref, tokens_ref, middle_ref = refs[:5]
        chunk_refs, mixed_ref = refs[5:-1], refs[-1]
        for r in range(n_heads):
            mixed_ref[place_ref[1] ^ r] = mix_refs[r][...]
        middle = x_ref[...].astype(F32)
        w_ref = w_ref.ready()
        attended = dot(mixed_ref[0], w_ref[:width, :])
        for h in range(1, n_heads):
            attended += dot(mixed_ref[h], w_ref[h * width : (h + 1) * width, :])
        middle = middle + attended
        middle_ref[...] = middle
        scale = lax.rsqrt(jnp.mean(middle * middle, axis=-1, keepdims=True) + EPSILON)
        expert_in = (middle * scale * gain_ref[...]).astype(BF16)
        dispatch_into(expert_in, place_ref, tokens_ref, chunk_refs)

    outs = kernel_call(
        body,
        [like(rows, model, dtype=F32)] + [like(per, model)] * n_ctx,
        [place, *mixes, out_w, x, gain, tokens],
        [pltpu.VMEM((n_heads, rows, width), BF16)],
        flops=2 * rows * model * model + 2 * rows * model * per * n_ctx,
    )
    return outs[0], outs[1:]


def gelu_parts(v):
    inner = jnp.tanh(ROOT_2_PI * (v + 0.044715 * v * v * v))
    return inner, 0.5 * v * (1.0 + inner)


def route_signs(place_ref, other):
    lane = lax.broadcasted_iota(jnp.int32, (other.shape[0], LANES), 1)
    return jnp.where(lane == place_ref[0], 1.0, 0.0) - jnp.where(lane == other, 1.0, 0.0)


def expert_hidden(place_ref, rows, up_ref, router_ref, other):
    logits = dot(rows, router_ref[...])
    margin = jnp.sum(logits * route_signs(place_ref, other), axis=1, keepdims=True)
    pre_act = dot(rows, up_ref[...])
    return margin, pre_act, gelu_parts(pre_act)[1].astype(BF16)


def sigmoid(v):
    return 1.0 / (1.0 + jnp.exp(-v))


def experts(place, arrived, up, down, router, other, n_heads):
    slots, model = arrived.shape
    per, hidden_width = slots // n_heads, up.shape[1]

    def body(place_ref, in_ref, up, down, router_ref, other_ref, *refs):
        chunk_refs, (pre_ref, hidden_ref, margin_ref) = refs[:n_heads], refs[n_heads:]
        up_ref = up.ready()
        for r in range(n_heads):
            span = pl.ds(pl.multiple_of((place_ref[1] ^ r) * per, per), per)
            margin, pre_act, hidden = expert_hidden(
                place_ref, in_ref[span, :], up_ref, router_ref, other_ref[span, :]
            )
            margin_ref[span, :] = margin
            pre_ref[span, :] = pre_act
            hidden_ref[span, :] = hidden
            out = sigmoid(margin) * dot(hidden, down.ready()[...])
            chunk_refs[r][...] = out.astype(BF16)

    outs = kernel_call(
        body,
        [like(per, model)] * n_heads
        + [
            like(slots, hidden_width, dtype=F32),
            like(slots, hidden_width),
            like(slots, 1, dtype=F32),
        ],
        [place, arrived, up, down, router, other],
        flops=4 * slots * model * hidden_width,
    )
    return outs[:n_heads], outs[n_heads:]


def experts_out(place, hidden, margin, down, n_heads, after):
    slots, model = hidden.shape[0], down.shape[1]
    per = slots // n_heads

    def body(place_ref, hidden_ref, margin_ref, down, *chunk_refs):
        down_ref = down.ready()
        for r in range(n_heads):
            span = pl.ds(pl.multiple_of((place_ref[1] ^ r) * per, per), per)
            out = sigmoid(margin_ref[span, :]) * dot(hidden_ref[span, :], down_ref[...])
            chunk_refs[r][...] = out.astype(BF16)

    return kernel_call(
        body,
        [like(per, model)] * n_heads,
        [place, hidden, margin, down],
        flops=2 * slots * model * hidden.shape[1],
        after=after,
    )


def experts_back(place, dout_rows, kept, arrived, up, down, router, other, n_heads, after=()):
    slots, model = dout_rows.shape
    per, hidden_width = slots // n_heads, up.shape[1]
    taken = [arrived] if kept is None else list(kept)

    def body(place_ref, dout_ref, *refs):
        kept_refs, refs = refs[: len(taken)], refs[len(taken) :]
        up, down, router_ref, other_ref = refs[:4]
        chunk_refs, refs = refs[4 : 4 + n_heads], refs[4 + n_heads :]
        dpre_ref, dslots_ref, dlogits_ref = refs[:3]
        up_ref, down_ref = up.ready(), down.ready()
        for r in range(n_heads):
            span = pl.ds(pl.multiple_of((place_ref[1] ^ r) * per, per), per)
            if kept is None:
                margin, v, hidden = expert_hidden(
                    place_ref, kept_refs[0][span, :], up_ref, router_ref, other_ref[span, :]
                )
                refs[3][span, :] = hidden
                refs[4][span, :] = margin
            else:
                v, hidden, margin = (ref[span, :] for ref in kept_refs)
            dout = dout_ref[span, :]
            dhidden = dot_nt(dout, down_ref[...])
            gate = sigmoid(margin)
            dgate = jnp.sum(dhidden * hidden.astype(F32), axis=1, keepdims=True)
            inner, _ = gelu_parts(v)
            slope = 0.5 * (1.0 + inner) + 0.5 * v * (1.0 - inner * inner) * ROOT_2_PI * (
                1.0 + 3.0 * 0.044715 * v * v
            )
            dpre = (gate * dhidden * slope).astype(BF16)
            dpre_ref[span, :] = dpre
            dslots_ref[span, :] = (gate * dout.astype(F32)).astype(BF16)
            signs = route_signs(place_ref, other_ref[span, :])
            dlogits = (gate * sigmoid(-margin) * dgate * signs).astype(BF16)
            dlogits_ref[span, :] = dlogits
            chunk_refs[r][...] = (
                dot_nt(dpre, up_ref[...]) + dot_nt(dlogits, router_ref[...])
            ).astype(BF16)

    extra = [like(slots, hidden_width), like(slots, 1, dtype=F32)] if kept is None else []
    outs = kernel_call(
        body,
        [like(per, model)] * n_heads
        + [like(slots, hidden_width), like(slots, model), like(slots, LANES)]
        + extra,
        [place, dout_rows, *taken, up, down, router, other],
        flops=4 * slots * model * hidden_width,
        after=after,
    )
    return outs[:n_heads], outs[n_heads:]


def expert_grads(place, pairs, got=None, after=()):
    outs = [like(p[0].shape[1], p[1].shape[1], dtype=BF16 if got is None else F32) for p in pairs]
    picks = [a for pair in pairs for a in pair]

    def body(place_ref, *refs):
        held, refs = refs[: len(picks)], refs[len(picks) :]
        got_refs, out_refs = refs[: len(refs) - len(pairs)], refs[len(refs) - len(pairs) :]
        for i, out_ref in enumerate(out_refs):
            grad = dot_tn(held[2 * i].ready()[...], held[2 * i + 1].ready()[...])
            if got_refs:
                grad += got_refs[i][...].astype(F32)
            out_ref[...] = grad.astype(out_ref.dtype)

    flops = sum(2 * p[0].shape[0] * p[0].shape[1] * p[1].shape[1] for p in pairs)
    return kernel_call(body, outs, [place, *picks, *(got or [])], flops=flops, after=after)


def dense_shares(place, pairs, n_ctx):
    model = pairs[0][0].shape[1]
    widths = [b.shape[1] for _, b in pairs]
    share, width = model // n_ctx, sum(widths)

    def body(place_ref, *refs):
        ins, out_ref, total_ref = refs[: 2 * len(pairs)], refs[-2], refs[-1]
        at = 0
        for i, size in enumerate(widths):
            total_ref[:, at : at + size] = dot_tn(ins[2 * i][...], ins[2 * i + 1][...])
            at += size
        for r in range(n_ctx):
            first = pl.multiple_of((place_ref[0] ^ r) * share, share)
            out_ref[r] = total_ref[pl.ds(first, share), :].astype(BF16)

    rows = pairs[0][0].shape[0]
    return kernel_call(
        body,
        [like(n_ctx, share, width)],
        [place, *(a for pair in pairs for a in pair)],
        [pltpu.VMEM((model, width), F32)],
        flops=2 * rows * model * width,
    )[0]


def add_shares(one, two):
    n_ctx, share, width = one.shape

    def body(one_ref, two_ref, *outs):
        for r, out_ref in enumerate(outs):
            out_ref[...] = (one_ref[r].astype(F32) + two_ref[r].astype(F32)).astype(BF16)

    return kernel_call(body, [like(share, width)] * n_ctx, [one, two])


def sum_shares(parts):
    share, width = parts[0].shape

    def body(*refs):
        refs[-1][...] = tree_sum([ref[...].astype(F32) for ref in refs[:-1]]).astype(BF16)

    return kernel_call(body, [like(share, width)], parts)[0]


def dense_grads(place, parts0, sum1, got1, width):
    share = sum1.shape[0]

    def body(place_ref, *refs):
        part_refs, (sum_ref, got_ref, qkv_ref, out_ref) = refs[:-4], refs[-4:]
        layer0 = tree_sum([ref[...].astype(F32) for ref in part_refs])
        layer1 = sum_ref[...].astype(F32) + got_ref[...].astype(F32)
        total = either(place_ref, layer0, layer1)
        for i, at in enumerate((0, 2, 3)):
            qkv_ref[i] = total[:, at * width : (at + 1) * width]
        out_ref[...] = total[:, width : 2 * width].T

    return kernel_call(
        body,
        [like(3, share, width, dtype=F32), like(width, share, dtype=F32)],
        [place, *parts0, sum1, got1],
    )


def small_pack(place, layers, n_experts, n_heads, after=()):
    model = layers[0][0].shape[1]
    rows = 1 + n_experts + n_heads

    def body(place_ref, *refs):
        out_ref = refs[-1]
        out_ref[...] = jnp.zeros(out_ref.shape, F32)
        for layer in range(2):
            dgain_ref, dlogits_ref, arrived_ref, lanes_ref = refs[4 * layer : 4 * layer + 4]
            at = layer * rows
            out_ref[at : at + 1, :] = dgain_ref[...] * (1.0 / n_heads)
            router = dot_tn(dlogits_ref[...], arrived_ref[...])
            out_ref[at + 1 : at + 1 + n_experts, :] = router[:n_experts]
            count = lanes_ref.shape[0]
            eye = lax.broadcasted_iota(jnp.int32, (count, count), 0) == lax.broadcasted_iota(
                jnp.int32, (count, count), 1
            )
            sums = jnp.sum(lanes_ref[...], axis=1, keepdims=True)
            row = jnp.sum(jnp.where(eye, sums, 0.0), axis=0, keepdims=True)
            for h in range(n_heads):
                spot = at + 1 + n_experts + h
                out_ref[spot : spot + 1, :count] = jnp.where(place_ref[1] == h, row, 0.0)

    return kernel_call(
        body,
        [like(2 * rows, model, dtype=F32)],
        [place, *(a for layer in layers for a in layer)],
        after=after,
    )[0]


def assemble(place, dx, got_out, got_dx, out):
    def body(place_ref, one, two, both_ref):
        both_ref[0] = one.ready()[...]
        both_ref[1] = two.ready()[...]

    picks = [Pick(dx, got_out), Pick(got_dx, out)]
    return kernel_call(body, [like(2, *dx.shape, dtype=F32)], [place, *picks])[0]


def combine(middle, returned, tokens, after):
    rows, model = middle.shape
    share = returned[0].shape[0]

    def body(middle_ref, tokens_ref, *refs):
        total = 0.0
        for r, ref in enumerate(refs[: len(returned)]):
            total += dot(token_picks(tokens_ref, share, r * share), ref[...])
        refs[-1][...] = middle_ref[...] + total

    return kernel_call(
        body,
        [like(rows, model, dtype=F32)],
        [middle, tokens, *returned],
        flops=2 * rows * model * share * len(returned),
        after=after,
    )[0]


def combine_project(place, middle, returned, tokens, gain, qkv):
    rows, model = middle.shape
    width = qkv.shape[2]

    def body(place_ref, middle_ref, returned_ref, tokens_ref, gain_ref, w, passed_ref, *outs):
        picks = token_picks(tokens_ref, returned_ref.shape[0])
        passed = (middle_ref[...] + dot(picks, returned_ref[...])).astype(BF16)
        passed_ref[...] = passed
        project_rows(passed.astype(F32), gain_ref[...], w, *outs)

    return kernel_call(
        body,
        [like(rows, model), like(rows, model), like(rows, width), like(rows, 2 * width)],
        [place, middle, returned, tokens, gain, qkv],
        flops=2 * rows * model * returned.shape[0] + 6 * rows * model * width,
    )


def norm_back(values, gain, upstream):
    scale = lax.rsqrt(jnp.mean(values * values, axis=-1, keepdims=True) + EPSILON)
    unit = values * scale
    scaled = upstream * gain
    dvalues = scale * (scaled - unit * jnp.mean(unit * scaled, axis=-1, keepdims=True))
    return dvalues, jnp.sum(upstream * unit, axis=0, keepdims=True)


def middle_back(place, returned, tokens, middle, gain, dout, out_w, after=()):
    rows, model = middle.shape
    width = out_w.shape[0]

    def body(place_ref, returned_ref, tokens_ref, middle_ref, gain_ref, dout_ref, w, *refs):
        dmiddle_ref, datt_ref, dmix_ref, dgain_ref = refs
        picks = token_picks(tokens_ref, returned_ref.shape[0])
        dexpert_in = dot(picks, returned_ref[...])
        part, dgain = norm_back(middle_ref[...], gain_ref[...], dexpert_in)
        dgain_ref[...] = dgain
        dmiddle = dout_ref[...].astype(F32) + part
        dmiddle_ref[...] = dmiddle
        datt = dmiddle.astype(BF16)
        datt_ref[...] = datt
        dmix_ref[...] = dot_nt(datt, w.ready()[...]).astype(BF16)

    return kernel_call(
        body,
        [
            like(rows, model, dtype=F32),
            like(rows, model),
            like(rows, width),
            like(1, model, dtype=F32),
        ],
        [place, returned, tokens, middle, gain, dout, out_w],
        flops=2 * rows * model * (returned.shape[0] + width),
        after=after,
    )


def project_back(place, dq, dkv_parts, qkv, n_heads, after=()):
    rows, width = dq.shape
    model, n_parts = qkv.shape[1], len(dkv_parts)
    share = rows // n_heads

    def body(place_ref, dq_ref, *refs):
        part_refs, refs = refs[:n_parts], refs[n_parts:]
        w, dkv_ref = refs[:2]
        chunk_refs, total_ref = refs[2:-1], refs[-1]
        dkv = part_refs[0][...].astype(F32)
        for ref in part_refs[1:]:
            dkv += ref[...].astype(F32)
        dkv = dkv.astype(BF16)
        dkv_ref[...] = dkv
        w_ref = w.ready()
        total_ref[...] = (
            dot_nt(dq_ref[...], w_ref[0])
            + dot_nt(dkv[:, :width], w_ref[1])
            + dot_nt(dkv[:, width:], w_ref[2])
        )
        for r in range(n_heads):
            first = pl.multiple_of((place_ref[1] ^ r) * share, share)
            chunk_refs[r][...] = total_ref[pl.ds(first, share), :].astype(BF16)

    outs = kernel_call(
        body,
        [like(rows, 2 * width)] + [like(share, model)] * n_heads,
        [place, dq, *dkv_parts, qkv],
        [pltpu.VMEM((rows, model), F32)],
        flops=6 * rows * model * width,
        after=after,
    )
    return outs[0], outs[1:]


def tree_sum(values):
    while len(values) > 1:
        values = [values[i] + values[i + 1] for i in range(0, len(values), 2)]
    return values[0]


def share_sum(place, parts, x):
    share, model = parts[0].shape

    def body(place_ref, *refs):
        part_refs, (x_ref, total_ref, dgain_ref) = refs[: len(parts)], refs[len(parts) :]
        total = tree_sum([ref[...].astype(F32) for ref in part_refs])
        total_ref[...] = total.astype(BF16)
        first = pl.multiple_of(place_ref[1] * share, share)
        values = x_ref[pl.ds(first, share), :].astype(F32)
        scale = lax.rsqrt(jnp.mean(values * values, axis=-1, keepdims=True) + EPSILON)
        dgain_ref[...] = jnp.sum(total * (values * scale), axis=0, keepdims=True)

    return kernel_call(
        body, [like(share, model), like(1, model, dtype=F32)], [place, *parts, x]
    )


def input_back(place, dnormed_parts, x, gain, dmiddle, tokens=None, n_ctx=0, per=0, after=()):
    rows, model = x.shape
    n_heads, share = len(dnormed_parts), dnormed_parts[0].shape[0]
    given = [x, gain, dmiddle] + ([] if tokens is None else [tokens])

    def body(place_ref, *refs):
        part_refs, refs = refs[:n_heads], refs[n_heads:]
        x_ref, gain_ref, dmiddle_ref = refs[:3]
        dx_ref, chunk_refs, dnormed_ref = refs[len(given)], refs[len(given) + 1 : -1], refs[-1]
        for r in range(n_heads):
            first = pl.multiple_of((place_ref[1] ^ r) * share, share)
            dnormed_ref[pl.ds(first, share), :] = part_refs[r][...].astype(F32)
        part, _ = norm_back(x_ref[...].astype(F32), gain_ref[...], dnormed_ref[...])
        dx = (dmiddle_ref[...] + part).astype(dx_ref.dtype)
        dx_ref[...] = dx
        if tokens is not None:
            dispatch_into(dx, place_ref, refs[3], chunk_refs)

    outs = kernel_call(
        body,
        [like(rows, model, dtype=F32 if tokens is None else BF16)] + [like(per, model)] * n_ctx,
        [place, *dnormed_parts, *given],
        [pltpu.VMEM((rows, model), F32)],
        after=after,
    )
    return outs[0], outs[1:]


def bucket_of(distance):
    exact_span = BUCKETS // 2
    result = jnp.minimum(distance, exact_span)
    for rank in range(1, BUCKETS - exact_span):
        edge = int(
            math.ceil(exact_span * (REACH / exact_span) ** (rank / (BUCKETS - exact_span)))
        )
        result = result + (distance >= edge).astype(jnp.int32)
    return result


def tile_buckets(half):
    row = lax.broadcasted_iota(jnp.int32, (half, half), 0)
    col = lax.broadcasted_iota(jnp.int32, (half, half), 1)
    same = jnp.where(row >= col, bucket_of(jnp.maximum(row - col, 0)), -1)
    return [same, bucket_of(half + row - col), bucket_of(2 * half + row - col)]


def bias_tables(place, own, other, half, after):
    heads = own.shape[1]

    def body(place_ref, bias_refs, *refs):
        buckets = tile_buckets(half)
        for layer, out_ref in enumerate(refs[-2:]):
            for head in range(heads):
                out_ref[head, 0] = jnp.full((half, half), NEGATIVE, F32)
                values = [jnp.full((half, half), NEGATIVE, F32) for _ in buckets[:2]]
                for bucket in range(BUCKETS):
                    value = bias_refs[place_ref[2] ^ layer, bucket, head]
                    values = [
                        jnp.where(b == bucket, value, v) for b, v in zip(buckets, values)
                    ]
                out_ref[head, 1] = values[0]
                out_ref[head, 2] = values[1]
                far = bias_refs[place_ref[2] ^ layer, BUCKETS - 1, head]
                out_ref[head, 3] = jnp.full((half, half), far, F32)

    shape = like(heads, 4, half, half, dtype=F32)
    return pl.pallas_call(
        body,
        out_shape=[shape] * 2,
        in_specs=[pl.BlockSpec(memory_space=pltpu.SMEM)] * 2
        + [pl.BlockSpec(memory_space=pl.ANY)] * len(after),
        out_specs=[pl.BlockSpec(memory_space=pltpu.VMEM)] * 2,
        compiler_params=pltpu.CompilerParams(vmem_limit_bytes=2 * SPARE_BYTES),
    )(place, jnp.stack([own, other]), *after)


def small_weights(place, gains, routers, after):
    model, n_experts = routers[0].shape

    def body(place_ref, *refs):
        ins, outs = refs[:6], refs[-6:]
        for kind in range(2):
            own, other = (ref[...].astype(F32) for ref in ins[2 * kind : 2 * kind + 2])
            outs[2 * kind][...] = either(place_ref, own, other)
            outs[2 * kind + 1][...] = either(place_ref, other, own)
        own, other = (ref[...].astype(F32) for ref in ins[4:6])
        for out_ref, value in zip(
            outs[4:], (either(place_ref, own, other), either(place_ref, other, own))
        ):
            out_ref[...] = jnp.zeros(out_ref.shape, BF16)
            out_ref[:, :n_experts] = value.astype(BF16)

    args = [place, *gains[0], *gains[1], *routers]
    outs = kernel_call(
        body,
        [like(1, model, dtype=F32)] * 4 + [like(model, LANES)] * 2,
        args,
        after=after,
    )
    return outs[0:2], outs[2:4], outs[4:6]


def layer_row(place_ref, pair_ref, layer, k):
    rows = pair_ref.shape[3]
    row = pair_ref[place_ref[2] ^ layer, place_ref[2], k : k + 1, :]
    eye = lax.broadcasted_iota(jnp.int32, (rows, rows), 0) == lax.broadcasted_iota(
        jnp.int32, (rows, rows), 1
    )
    return jnp.sum(jnp.where(eye, row, 0).astype(F32), axis=1, keepdims=True).astype(jnp.int32)


def earlier(rows):
    row = lax.broadcasted_iota(jnp.int32, (rows, rows), 0)
    col = lax.broadcasted_iota(jnp.int32, (rows, rows), 1)
    return jnp.where(row > col, 1.0, 0.0).astype(BF16)


def quarter_of(rank, per, n_heads):
    return sum([(rank >= h * per).astype(jnp.int32) for h in range(1, n_heads)])


def token_slots(place, pair, n_experts, per, n_heads, after):
    rows = pair.shape[3]

    def body(place_ref, pair_ref, *refs):
        outs = refs[-3:]
        for layer in range(2):
            choices = [layer_row(place_ref, pair_ref, layer, k) for k in range(2)]
            lane = lax.broadcasted_iota(jnp.int32, (rows, LANES), 1)
            hots = [jnp.where(lane == choice, 1.0, 0.0) for choice in choices]
            ranks = dot(earlier(rows), (hots[0] + hots[1]).astype(BF16))
            for k in range(2):
                rank = jnp.sum(ranks * hots[k], axis=1, keepdims=True).astype(jnp.int32)
                quarter = quarter_of(rank, per, n_heads)
                inner = (choices[k] ^ place_ref[0]) * per + rank - quarter * per
                outs[layer][:, k : k + 1] = quarter * (n_experts * per) + inner
                if layer == 1:
                    outs[2][:, k : k + 1] = (quarter ^ place_ref[1]) * (n_experts * per) + inner

    return kernel_call(
        body, [like(rows, 2, dtype=jnp.int32)] * 3, [place, pair], after=after
    )


def other_experts(place, pairs, per, n_heads):
    n_ctx, rows = len(pairs), pairs[0].shape[3]

    def body(place_ref, *refs):
        before = earlier(rows)
        lane = lax.broadcasted_iota(jnp.int32, (rows, per), 1)
        for layer, out_ref in enumerate(refs[n_ctx:]):
            for r, pair_ref in enumerate(refs[:n_ctx]):
                one, two = (layer_row(place_ref, pair_ref, layer, k) for k in range(2))
                here = (one == place_ref[0]) | (two == place_ref[0])
                other = jnp.where(one == place_ref[0], two, one).astype(F32)
                other = jnp.broadcast_to(other, (rows, LANES)).astype(BF16)
                wide = jnp.broadcast_to(jnp.where(here, 1.0, 0.0), (rows, LANES)).astype(BF16)
                rank = dot(before, wide)[:, 0:1].astype(jnp.int32)
                rank = jnp.where(here, rank, -1)
                for h in range(n_heads):
                    picks = jnp.where(lane + h * per == rank, 1.0, 0.0).astype(BF16)
                    found = dot_tn(picks, other)[:, 0:1].astype(jnp.int32)
                    at = (h * n_ctx + r) * per
                    out_ref[at : at + per, :] = found

    return kernel_call(
        body, [like(n_heads * n_ctx * per, 1, dtype=jnp.int32)] * 2, [place, *pairs]
    )


def table_back(dtable, after=()):
    heads, half = dtable.shape[0], dtable.shape[3]

    def body(dtable_ref, *refs):
        out_ref, buckets = refs[-1], tile_buckets(half)
        for bucket in range(BUCKETS):
            hits = [held == bucket for held in buckets]
            for head in range(heads):
                kept = jnp.zeros((half, half), F32)
                for tile, hit in enumerate(hits):
                    kept += jnp.where(hit, dtable_ref[head, 1 + tile], 0.0)
                at = bucket * heads + head
                out_ref[at : at + 1, :] = jnp.sum(kept, axis=0, keepdims=True)

    return kernel_call(
        body, [like(BUCKETS * heads, half, dtype=F32)], [dtable], after=after
    )[0]


def heads_sum(chunks):
    return tree_sum([part.astype(F32) for part in exchange(chunks, "heads")]).astype(BF16)


def back_rows(total, n_ctx):
    per = total.shape[0] // n_ctx
    return exchange([total[r * per : (r + 1) * per] for r in range(n_ctx)], "ctx")


def return_rows(chunks, n_ctx):
    return gather_rows(jnp.concatenate(back_rows(heads_sum(chunks), n_ctx), axis=0), "heads")


def exchange_first(chunks):
    n_ctx = len(chunks)
    parts = [chunks[0]]
    for r in range(1, n_ctx):
        pairs = [(i, i ^ r) for i in range(n_ctx)]
        parts.append(lax.ppermute(chunks[r], ("section", "ctx"), pairs))
    return parts


def send_rows(chunks):
    return gather_rows(jnp.concatenate(exchange(chunks, "ctx"), axis=0), "heads")


def body(
    boundary,
    norm_first,
    qkv_weight,
    position_bias,
    out_weight,
    norm_second,
    router,
    expert_up,
    expert_down,
    routes,
):
    section = lax.axis_index("section")
    ctx_index = lax.axis_index("ctx")
    heads_index = lax.axis_index("heads")
    n_ctx, n_heads = lax.axis_size("ctx"), lax.axis_size("heads")
    first = section == 0
    place = jnp.stack([ctx_index, heads_index, section]).astype(jnp.int32)
    rows, model = boundary.shape[2:]
    half = rows // 2
    n_experts, heads = router.shape[2], position_bias.shape[2]
    per = 5 * rows // (2 * n_experts) // n_heads

    def by_layer(own, other):
        return Pick(own, other), Pick(other, own)

    def with_other(own):
        return own, swap(own, "section")

    given = swap(lax.dynamic_index_in_dim(boundary[0], 1 - section, 0, False), "section")
    gain_pairs = with_other(norm_first), with_other(norm_second)
    qkv = by_layer(*with_other(qkv_weight[0]))
    x0, cotangent, normed0, q0, kv0 = begin(place, boundary[0], given, *gain_pairs[0], qkv[0])
    kv_all0 = gather_rows(kv0, "ctx")

    gains_first, gains_second, routers = small_weights(
        place, gain_pairs, with_other(router[0]), [kv0]
    )
    biases = bias_tables(place, *with_other(position_bias[0]), half, [kv0])
    pair = jnp.stack(with_other(routes[0].transpose(0, 2, 1)))
    *tokens, tokens_near = token_slots(place, pair, n_experts, per, n_heads, [kv0])
    others = other_experts(place, exchange([pair] * n_ctx, "ctx"), per, n_heads)
    up = by_layer(*with_other(expert_up[0, 0]))
    down = by_layer(*with_other(expert_down[0, 0]))
    width = out_weight.shape[1]
    out_gathered = gather_rows(jnp.concatenate(with_other(out_weight[0]), axis=0), "heads")
    out_full = [Rows(out_gathered, layer, width) for layer in range(2)]
    out_own = [Rows(out_gathered, layer, width, own=True) for layer in range(2)]

    def before_experts(layer, x, q, kv_all):
        mix, lse = attend(place, q, [kv_all], biases[layer], n_ctx)
        mixes = exchange([mix] * n_heads, "heads")
        middle, chunks = finish_attention(
            place, mixes, out_full[layer], x, gains_second[layer], tokens[layer], n_ctx, per
        )
        return mix, lse, middle, send_rows(chunks)

    def expert_weights(layer):
        return up[layer], down[layer], routers[layer], others[layer]

    mix0, lse0, middle0, arrived0 = before_experts(0, x0, q0, kv_all0)
    chunks, kept0 = experts(place, arrived0, *expert_weights(0), n_heads)
    dout_chunks = dispatch_whole(place, cotangent, tokens[1], n_ctx, per, n_heads, [middle0])
    returned = return_rows(chunks, n_ctx)
    x1, normed1, q1, kv1 = combine_project(
        place, middle0, returned, tokens[0], gains_first[1], qkv[1]
    )

    kv_all1 = gather_rows(kv1, "ctx")
    mix1, lse1, middle1, arrived1 = before_experts(1, x1, q1, kv_all1)
    dout_rows1 = jnp.stack(exchange(dout_chunks, "ctx"))
    dout_rows1 = dout_rows1.reshape(n_ctx, n_heads, per, model).transpose(1, 0, 2, 3)
    dout_rows1 = dout_rows1.reshape(-1, model)
    chunks, (dpre1, dslots1, dlogits1, hidden1, margin1) = experts_back(
        place, dout_rows1, None, arrived1, *expert_weights(1), n_heads
    )
    dmiddle1, datt1, dmix1, dgain_second1 = middle_back(
        place, return_rows(chunks, n_ctx), tokens[1], middle1, gains_second[1], cotangent, out_own[1]
    )
    dq1, dtable1, dkv1 = attend_back(place, q1, [kv_all1], biases[1], lse1, dmix1, n_ctx)
    out_total = heads_sum(experts_out(place, hidden1, margin1, down[1], n_heads, [dq1]))
    dkv_sum1, chunks = project_back(
        place, dq1, exchange(dkv1, "ctx"), qkv[1], n_heads, [out_total]
    )
    total1, dgain_first1 = share_sum(place, exchange(chunks, "heads"), x1)
    lanes1 = table_back(dtable1)
    shares1 = dense_shares(place, [(normed1, dq1), (datt1, mix1), (normed1, dkv_sum1)], n_ctx)
    dx1, sent = input_back(
        place,
        exchange([total1] * n_heads, "heads"),
        x1,
        gains_first[1],
        dmiddle1,
        tokens[0],
        n_ctx,
        per,
        [lanes1, shares1],
    )

    out_back = back_rows(out_total, n_ctx)
    dout_rows0 = send_rows(sent)
    chunks, (dpre0, dslots0, dlogits0) = experts_back(
        place, dout_rows0, kept0, arrived0, *expert_weights(0), n_heads, out_back
    )
    lists = [(arrived0, arrived1), (dpre0, dpre1), (kept0[1], hidden1), (dslots0, dslots1)]
    mine, theirs = [Pick(a, b) for a, b in lists], [Pick(b, a) for a, b in lists]
    sends = expert_grads(place, [theirs[:2], theirs[2:]])
    sum1 = sum_shares(exchange([shares1[r] for r in range(n_ctx)], "ctx"))
    dmiddle0, datt0, dmix0, dgain_second0 = middle_back(
        place,
        return_rows(chunks, n_ctx),
        tokens[0],
        middle0,
        gains_second[0],
        dx1,
        out_own[0],
        [*sends, sum1],
    )
    dq0, dtable0, dkv0 = attend_back(place, q0, [kv_all0], biases[0], lse0, dmix0, n_ctx)
    lanes0 = table_back(dtable0)
    layers = [
        (dgain_second0, dlogits0, arrived0, lanes0),
        (dgain_second1, dlogits1, arrived1, lanes1),
    ]
    pack = small_pack(place, layers, n_experts, n_heads)
    quarter = jnp.concatenate(out_back, axis=0)
    out = combine(
        middle1, exchange([quarter] * n_heads, "heads"), tokens_near, [dq0]
    )
    dkv_sum0, chunks = project_back(
        place, dq0, exchange(dkv0, "ctx"), qkv[0], n_heads, [pack, out]
    )
    total0, dgain_first0 = share_sum(place, exchange(chunks, "heads"), x0)
    shares0 = dense_shares(place, [(normed0, dq0), (datt0, mix0), (normed0, dkv_sum0)], n_ctx)
    gots = [swap(g, "section") for g in sends]
    grad_up, grad_down = expert_grads(place, [mine[:2], mine[2:]], gots, after=[total0])
    (dx0,) = input_back(
        place,
        exchange([total0] * n_heads, "heads"),
        x0,
        gains_first[0],
        dmiddle0,
        after=[grad_up],
    )[:1]

    got1 = one_way(sum1, 0)
    parts0 = exchange_first(add_shares(shares0, one_way(shares0, 1)))
    grad_qkv, grad_out = dense_grads(place, parts0, sum1, got1, width)
    pack = jnp.concatenate([dgain_first0, dgain_first1, pack])
    pack = tree_sum(exchange([pack] * n_heads, "heads"))
    pack = tree_sum(exchange([pack] * n_ctx, "ctx"))
    count = 1 + n_experts + n_heads
    packs = [jnp.concatenate([pack[i : i + 1], pack[2 + i * count :][:count]]) for i in range(2)]
    pack = jnp.where(first, packs[0], packs[1]) + swap(
        jnp.where(first, packs[1], packs[0]), "section"
    )
    share = model // n_ctx
    mine = lax.dynamic_slice_in_dim(pack, ctx_index * share, share, 1)
    bias_share = BUCKETS // n_ctx * heads
    at = (2 + n_experts + heads_index, ctx_index * bias_share)
    grad_bias = lax.dynamic_slice(pack, at, (1, bias_share))
    boundary_out = assemble(place, dx0, one_way(out, 0), one_way(dx0, 1), out)
    return (
        boundary_out[None],
        mine[0][None],
        grad_qkv[None],
        grad_bias.reshape(1, BUCKETS // n_ctx, heads),
        grad_out[None],
        mine[1][None],
        mine[2 : 2 + n_experts].T[None],
        grad_up[None, None],
        grad_down[None, None],
    )


def solution(mesh):
    placed = (
        P("section", None, "ctx", None),
        P("section", None),
        P("section", None, None, "heads"),
        P("section", None, "heads"),
        P("section", "heads", None),
        P("section", None),
        P("section", None, None),
        P("section", "ctx", None, "heads"),
        P("section", "ctx", "heads", None),
        P("section", None, "ctx", None),
    )
    return jax.shard_map(
        body,
        mesh=mesh,
        in_specs=placed,
        out_specs=(
            P("section", None, "ctx", None),
            P("section", "ctx"),
            P("section", None, "ctx", "heads"),
            P("section", "ctx", "heads"),
            P("section", "heads", "ctx"),
            P("section", "ctx"),
            P("section", "ctx", None),
            P("section", "ctx", None, "heads"),
            P("section", "ctx", "heads", None),
        ),
        check_vma=False,
    )
```

```python
import math

import jax
import jax.numpy as jnp
from jax import lax
from jax.experimental import pallas as pl
from jax.experimental.pallas import tpu as pltpu
from jax.sharding import PartitionSpec as P

HD = 64
BUCKETS = 32
REACH = 128
EPSILON = 1e-06
NEGATIVE = -1e30
F32 = jnp.float32
BF16 = jnp.bfloat16
LANES = 128
SPARE_BYTES = 6 * 1024 * 1024
WIDE_BYTES = 48 * 1024 * 1024
ROOT_2_PI = math.sqrt(2.0 / math.pi)


class Pick:
    def __init__(self, first, second):
        self.arrays, self.shape = (first, second), first.shape
        self.dtype, self.ndim = first.dtype, first.ndim


class Rows:
    def __init__(self, array, layer, width, own=False):
        n_heads = array.shape[0] // (2 * width)
        self.array, self.layer, self.width, self.own = array, layer, width, own
        self.shape = (width if own else n_heads * width,) + array.shape[1:]
        self.dtype, self.ndim, self.n_heads = array.dtype, array.ndim, n_heads


class Held:
    def __init__(self, buffer, wait):
        self.buffer, self.wait, self.here = buffer, wait, False

    def ready(self):
        if not self.here:
            self.wait()
        self.here = True
        return self.buffer


def padded_bytes(array):
    *lead, rows, lanes = (1, 1) + tuple(array.shape)
    return math.prod(lead) * (-(-rows // 16) * 16) * (-(-lanes // LANES) * LANES) * jnp.dtype(array.dtype).itemsize


def kernel_call(body, outs, args, scratch=(), flops=0, after=(), grant=0, mark=False):
    if mark:
        outs = list(outs) + [like(8, LANES, dtype=F32)]
    picks = [a for a in args if isinstance(a, (Pick, Rows))]
    operands, in_specs = [], []
    for a in args:
        if isinstance(a, (Pick, Rows)):
            arrays = a.arrays if isinstance(a, Pick) else (a.array,)
            operands += arrays
            in_specs += [pl.BlockSpec(memory_space=pltpu.HBM)] * len(arrays)
        else:
            scalar = a.ndim == 1 and a.dtype == jnp.int32
            operands.append(a)
            in_specs.append(pl.BlockSpec(memory_space=pltpu.SMEM if scalar else pltpu.VMEM))
    operands += after
    in_specs += [pl.BlockSpec(memory_space=pl.ANY)] * len(after)
    scratch = list(scratch) + [pltpu.VMEM(p.shape, p.dtype) for p in picks]
    if picks:
        scratch.append(pltpu.SemaphoreType.DMA((len(picks),)))
    n_out, n_own = len(outs), len(scratch) - len(picks) - (1 if picks else 0)

    def hold(a, sources, place_ref, buffer, sem):
        if isinstance(a, Pick):
            for section, src in enumerate(sources):

                @pl.when(place_ref[2] == section)
                def _(src=src):
                    pltpu.make_async_copy(src, buffer, sem).start()

            return Held(buffer, pltpu.make_async_copy(sources[0], buffer, sem).wait)
        copies = []
        for h in range(1 if a.own else a.n_heads):
            block = 2 * (place_ref[1] if a.own else h) + (place_ref[2] ^ a.layer)
            src = sources[0].at[pl.ds(pl.multiple_of(block * a.width, a.width), a.width)]
            dst = buffer.at[pl.ds(h * a.width, a.width)]
            copies.append(pltpu.make_async_copy(src, dst, sem))
            copies[-1].start()

        def wait():
            for copy in copies:
                copy.wait()

        return Held(buffer, wait)

    def wrapped(*refs):
        ins, rest = refs[: len(operands)], refs[len(operands) :]
        buffers = list(rest[n_out + n_own :])
        given, at, number = [], 0, 0
        for a in args:
            if not isinstance(a, (Pick, Rows)):
                given.append(ins[at])
                at += 1
                continue
            count = 2 if isinstance(a, Pick) else 1
            sem = buffers[-1].at[number]
            given.append(hold(a, ins[at : at + count], ins[0], buffers[number], sem))
            at, number = at + count, number + 1
        if mark:
            rest[n_out - 1][...] = jnp.zeros((8, LANES), F32)
            rest = rest[: n_out - 1] + rest[n_out:]
        body(*given, *rest[: n_out + n_own - mark])

    size = sum(math.prod(a.shape) * a.dtype.itemsize for a in list(args) + list(outs))
    held = sum(map(padded_bytes, list(args) + list(outs)))
    held += sum(padded_bytes(s) for s in scratch[: n_own])
    return pl.pallas_call(
        wrapped,
        out_shape=outs,
        in_specs=in_specs,
        out_specs=[pl.BlockSpec(memory_space=pltpu.VMEM)] * n_out,
        scratch_shapes=scratch,
        compiler_params=pltpu.CompilerParams(vmem_limit_bytes=max(grant, held + SPARE_BYTES)),
        cost_estimate=pl.CostEstimate(flops=flops, bytes_accessed=size, transcendentals=0),
    )(*operands)


def like(*shape, dtype=BF16):
    return jax.ShapeDtypeStruct(shape, dtype)


def dot(a, b, contract=((1,), (0,))):
    return lax.dot_general(a, b, (contract, ((), ())), preferred_element_type=F32)


def dot_nt(a, b):
    return dot(a, b, ((1,), (1,)))


def dot_tn(a, b):
    return dot(a, b, ((0,), (0,)))


def swap(array, axis, by=1):
    devices = lax.axis_size(axis)
    return lax.ppermute(array, axis, [(i, i ^ by) for i in range(devices)])


def one_way(array, source):
    return lax.ppermute(array, "section", [(source, 1 - source)])


def exchange(chunks, axis):
    return [chunks[0]] + [swap(chunks[r], axis, r) for r in range(1, len(chunks))]


def gather_rows(array, axis):
    return lax.all_gather(array, axis, axis=0, tiled=True)


def project_rows(x, gain, w, normed_ref, q_ref, kv_ref):
    width = q_ref.shape[1]
    scale = lax.rsqrt(jnp.mean(x * x, axis=-1, keepdims=True) + EPSILON)
    normed = (x * scale * gain).astype(BF16)
    normed_ref[...] = normed
    w_ref = w.ready()
    kv_ref[:, :width] = dot(normed, w_ref[1]).astype(BF16)
    kv_ref[:, width:] = dot(normed, w_ref[2]).astype(BF16)
    q_ref[...] = dot(normed, w_ref[0]).astype(BF16)


def either(place_ref, first, second):
    return jnp.where(place_ref[2] == 0, first, second)


def begin(place, own, given, gain_own, gain_other, qkv):
    _, rows, model = own.shape
    width = qkv.shape[2]

    def body(place_ref, own_ref, given_ref, gain_ref, other_ref, w, x_ref, cotangent_ref, *outs):
        x = either(place_ref, own_ref[0], given_ref[...])
        x_ref[...] = x
        cotangent_ref[...] = either(place_ref, given_ref[...], own_ref[1])
        gain = either(place_ref, gain_ref[...].astype(F32), other_ref[...].astype(F32))
        project_rows(x.astype(F32), gain, w, *outs)

    return kernel_call(
        body,
        [like(rows, model)] * 3 + [like(rows, width), like(rows, 2 * width)],
        [place, own, given, gain_own, gain_other, qkv],
        flops=6 * rows * model * width,
    )


def tile_pick(block, key_tile, mine, ordered, n_ctx):
    owner = key_tile // 2 if ordered else mine ^ (key_tile // 2)
    key_block = owner if key_tile % 2 == 0 else 2 * n_ctx - 1 - owner
    return jnp.clip(block - key_block, -1, 2) + 1


def query_parts(mine, half, n_ctx):
    return [
        (slice(0, half), mine),
        (slice(half, 2 * half), 2 * n_ctx - 1 - mine),
    ]


def load_keys(kv_refs, kv_ref):
    rows = kv_refs[0].shape[0]
    for r, ref in enumerate(kv_refs):
        kv_ref[r * rows : (r + 1) * rows, :] = ref[...]


def attend(place, q, kv_parts, table, n_ctx):
    rows, width = q.shape
    half, heads, keys = rows // 2, width // HD, rows * n_ctx
    ordered, count = len(kv_parts) == 1, len(kv_parts)

    def body(place_ref, q_ref, *refs):
        kv_refs, (table_ref, mix_ref, lse_ref, scores_ref, kv_ref) = refs[:count], refs[count:]
        mine = place_ref[0]
        load_keys(kv_refs, kv_ref)
        for head in range(heads):
            cols = slice(head * HD, (head + 1) * HD)
            key_rows = kv_ref[:, cols]
            value_rows = kv_ref[:, width + head * HD : width + (head + 1) * HD]
            for part, (span, block) in enumerate(query_parts(mine, half, n_ctx)):
                raw = dot_nt(q_ref[span, cols], key_rows)
                for key_tile in range(2 * n_ctx):
                    pick = tile_pick(block, key_tile, mine, ordered, n_ctx)
                    tile = slice(key_tile * half, (key_tile + 1) * half)
                    scores_ref[part, :, tile] = raw[:, tile] * 0.125 + table_ref[head, pick]
                scores = scores_ref[part]
                top = jnp.max(scores, axis=1, keepdims=True)
                mass = jnp.exp(scores - top)
                total = jnp.sum(mass, axis=1, keepdims=True)
                out = dot(mass.astype(BF16), value_rows) / total
                mix_ref[span, cols] = out.astype(BF16)
                lse_ref[span, head : head + 1] = top + jnp.log(total)

    return kernel_call(
        body,
        [like(rows, width), like(rows, heads, dtype=F32)],
        [place, q, *kv_parts, table],
        [pltpu.VMEM((2, half, keys), F32), pltpu.VMEM((keys, 2 * width), BF16)],
        flops=4 * rows * keys * width,
    )


def attend_back(place, q, kv_parts, table, lse, dmix, n_ctx):
    rows, width = q.shape
    half, heads, keys = rows // 2, width // HD, rows * n_ctx
    ordered, count = len(kv_parts) == 1, len(kv_parts)

    def body(place_ref, q_ref, *refs):
        kv_refs, refs = refs[:count], refs[count:]
        table_ref, lse_ref, dmix_ref, dq_ref, dtable_ref = refs[:5]
        chunk_refs, (scores_ref, total_ref, kv_ref) = refs[5 : 5 + n_ctx], refs[5 + n_ctx :]
        mine = place_ref[0]
        load_keys(kv_refs, kv_ref)
        dtable_ref[...] = jnp.zeros(dtable_ref.shape, F32)
        for head in range(heads):
            cols = slice(head * HD, (head + 1) * HD)
            value_cols = slice(width + head * HD, width + (head + 1) * HD)
            key_rows = kv_ref[:, cols]
            value_rows = kv_ref[:, value_cols]
            for part, (span, block) in enumerate(query_parts(mine, half, n_ctx)):
                q = q_ref[span, cols]
                dmix = dmix_ref[span, cols]
                raw = dot_nt(q, key_rows)
                for key_tile in range(2 * n_ctx):
                    pick = tile_pick(block, key_tile, mine, ordered, n_ctx)
                    tile = slice(key_tile * half, (key_tile + 1) * half)
                    scores_ref[part, :, tile] = raw[:, tile] * 0.125 + table_ref[head, pick]
                probs = jnp.exp(scores_ref[part] - lse_ref[span, head : head + 1])
                dprobs = dot_nt(dmix, value_rows)
                delta = jnp.sum(probs * dprobs, axis=1, keepdims=True)
                dscores = (probs * (dprobs - delta)).astype(BF16)
                dq_ref[span, cols] = (dot(dscores, key_rows) * 0.125).astype(BF16)
                dkeys = dot_tn(dscores, q) * 0.125
                dvalues = dot_tn(probs.astype(BF16), dmix)
                if part == 0:
                    total_ref[:, cols] = dkeys
                    total_ref[:, value_cols] = dvalues
                else:
                    total_ref[:, cols] += dkeys
                    total_ref[:, value_cols] += dvalues
                for key_tile in range(2 * n_ctx):
                    pick = tile_pick(block, key_tile, mine, ordered, n_ctx)
                    tile = dscores[:, key_tile * half : (key_tile + 1) * half]
                    dtable_ref[head, pick] += tile.astype(F32)
        for r in range(n_ctx):
            first = pl.multiple_of((mine ^ r if ordered else r) * rows, rows)
            chunk_refs[r][...] = total_ref[pl.ds(first, rows), :].astype(BF16)

    outs = kernel_call(
        body,
        [like(rows, width), like(*table.shape, dtype=F32)] + [like(rows, 2 * width)] * n_ctx,
        [place, q, *kv_parts, table, lse, dmix],
        [
            pltpu.VMEM((2, half, keys), F32),
            pltpu.VMEM((keys, 2 * width), F32),
            pltpu.VMEM((keys, 2 * width), BF16),
        ],
        flops=10 * rows * keys * width,
    )
    return outs[0], outs[1], outs[2:]


def token_picks(tokens_ref, count, first=0):
    ids = first + lax.broadcasted_iota(jnp.int32, (tokens_ref.shape[0], count), 1)
    hit = (ids == tokens_ref[:, 0:1]) | (ids == tokens_ref[:, 1:2])
    return jnp.where(hit, 1.0, 0.0).astype(BF16)


def dispatch_into(rows, place_ref, tokens_ref, chunk_refs):
    per = chunk_refs[0].shape[0]
    first = place_ref[1] * (per * len(chunk_refs))
    for r, chunk_ref in enumerate(chunk_refs):
        picks = token_picks(tokens_ref, per, first + r * per)
        chunk_ref[...] = dot_tn(picks, rows).astype(BF16)


def dispatch_whole(place, rows, tokens, n_ctx, per, n_heads, after):
    count, model = rows.shape

    def body(place_ref, rows_ref, tokens_ref, *chunk_refs):
        lane = lax.broadcasted_iota(jnp.int32, (count, n_heads * per), 1)
        ids = lane
        for h in range(1, n_heads):
            ids += jnp.where(lane >= h * per, (n_ctx - 1) * per, 0)
        for r, chunk_ref in enumerate(chunk_refs):
            here = ids + r * per
            hit = (here == tokens_ref[:, 0:1]) | (here == tokens_ref[:, 1:2])
            picks = jnp.where(hit, 1.0, 0.0).astype(BF16)
            chunk_ref[...] = dot_tn(picks, rows_ref[...]).astype(BF16)

    return kernel_call(
        body, [like(n_heads * per, model)] * n_ctx, [place, rows, tokens], after=after
    )


def finish_attention(place, mixes, out_w, x, gain, tokens, n_ctx, per):
    rows, model = x.shape
    n_heads, width = len(mixes), mixes[0].shape[1]

    def body(place_ref, *refs):
        mix_refs, refs = refs[:n_heads], refs[n_heads:]
        w_ref, x_ref, gain_ref, tokens_ref, middle_ref = refs[:5]
        chunk_refs, mixed_ref = refs[5:-1], refs[-1]
        for r in range(n_heads):
            mixed_ref[place_ref[1] ^ r] = mix_refs[r][...]
        middle = x_ref[...].astype(F32)
        w_ref = w_ref.ready()
        attended = dot(mixed_ref[0], w_ref[:width, :])
        for h in range(1, n_heads):
            attended += dot(mixed_ref[h], w_ref[h * width : (h + 1) * width, :])
        middle = middle + attended
        middle_ref[...] = middle
        scale = lax.rsqrt(jnp.mean(middle * middle, axis=-1, keepdims=True) + EPSILON)
        expert_in = (middle * scale * gain_ref[...]).astype(BF16)
        dispatch_into(expert_in, place_ref, tokens_ref, chunk_refs)

    outs = kernel_call(
        body,
        [like(rows, model, dtype=F32)] + [like(per, model)] * n_ctx,
        [place, *mixes, out_w, x, gain, tokens],
        [pltpu.VMEM((n_heads, rows, width), BF16)],
        flops=2 * rows * model * model + 2 * rows * model * per * n_ctx,
    )
    return outs[0], outs[1:]


def gelu_parts(v):
    inner = jnp.tanh(ROOT_2_PI * (v + 0.044715 * v * v * v))
    return inner, 0.5 * v * (1.0 + inner)


def route_signs(place_ref, other):
    lane = lax.broadcasted_iota(jnp.int32, (other.shape[0], LANES), 1)
    return jnp.where(lane == place_ref[0], 1.0, 0.0) - jnp.where(lane == other, 1.0, 0.0)


def expert_hidden(place_ref, rows, up_ref, router_ref, other):
    logits = dot(rows, router_ref[...])
    margin = jnp.sum(logits * route_signs(place_ref, other), axis=1, keepdims=True)
    pre_act = dot(rows, up_ref[...])
    return margin, pre_act, gelu_parts(pre_act)[1].astype(BF16)


def sigmoid(v):
    return 1.0 / (1.0 + jnp.exp(-v))


def experts(place, arrived, up, down, router, other, n_heads):
    slots, model = arrived.shape
    per, hidden_width = slots // n_heads, up.shape[1]

    def body(place_ref, in_ref, up, down, router_ref, other_ref, *refs):
        chunk_refs, (pre_ref, hidden_ref, margin_ref) = refs[:n_heads], refs[n_heads:]
        up_ref = up.ready()
        for r in range(n_heads):
            span = pl.ds(pl.multiple_of((place_ref[1] ^ r) * per, per), per)
            margin, pre_act, hidden = expert_hidden(
                place_ref, in_ref[span, :], up_ref, router_ref, other_ref[span, :]
            )
            margin_ref[span, :] = margin
            pre_ref[span, :] = pre_act
            hidden_ref[span, :] = hidden
            out = sigmoid(margin) * dot(hidden, down.ready()[...])
            chunk_refs[r][...] = out.astype(BF16)

    outs = kernel_call(
        body,
        [like(per, model)] * n_heads
        + [
            like(slots, hidden_width, dtype=F32),
            like(slots, hidden_width),
            like(slots, 1, dtype=F32),
        ],
        [place, arrived, up, down, router, other],
        flops=4 * slots * model * hidden_width,
    )
    return outs[:n_heads], outs[n_heads:]


def experts_out(place, hidden, margin, down, n_heads, after):
    slots, model = hidden.shape[0], down.shape[1]
    per = slots // n_heads

    def body(place_ref, hidden_ref, margin_ref, down, *chunk_refs):
        down_ref = down.ready()
        for r in range(n_heads):
            span = pl.ds(pl.multiple_of((place_ref[1] ^ r) * per, per), per)
            out = sigmoid(margin_ref[span, :]) * dot(hidden_ref[span, :], down_ref[...])
            chunk_refs[r][...] = out.astype(BF16)

    return kernel_call(
        body,
        [like(per, model)] * n_heads,
        [place, hidden, margin, down],
        flops=2 * slots * model * hidden.shape[1],
        after=after,
    )


def experts_back(place, dout_rows, kept, arrived, up, down, router, other, n_heads, after=()):
    slots, model = dout_rows.shape
    per, hidden_width = slots // n_heads, up.shape[1]
    taken = [arrived] if kept is None else list(kept)

    def body(place_ref, dout_ref, *refs):
        kept_refs, refs = refs[: len(taken)], refs[len(taken) :]
        up, down, router_ref, other_ref = refs[:4]
        chunk_refs, refs = refs[4 : 4 + n_heads], refs[4 + n_heads :]
        dpre_ref, dslots_ref, dlogits_ref = refs[:3]
        up_ref, down_ref = up.ready(), down.ready()
        for r in range(n_heads):
            span = pl.ds(pl.multiple_of((place_ref[1] ^ r) * per, per), per)
            if kept is None:
                margin, v, hidden = expert_hidden(
                    place_ref, kept_refs[0][span, :], up_ref, router_ref, other_ref[span, :]
                )
                refs[3][span, :] = hidden
                refs[4][span, :] = margin
            else:
                v, hidden, margin = (ref[span, :] for ref in kept_refs)
            dout = dout_ref[span, :]
            dhidden = dot_nt(dout, down_ref[...])
            gate = sigmoid(margin)
            dgate = jnp.sum(dhidden * hidden.astype(F32), axis=1, keepdims=True)
            inner, _ = gelu_parts(v)
            slope = 0.5 * (1.0 + inner) + 0.5 * v * (1.0 - inner * inner) * ROOT_2_PI * (
                1.0 + 3.0 * 0.044715 * v * v
            )
            dpre = (gate * dhidden * slope).astype(BF16)
            dpre_ref[span, :] = dpre
            dslots_ref[span, :] = (gate * dout.astype(F32)).astype(BF16)
            signs = route_signs(place_ref, other_ref[span, :])
            dlogits = (gate * sigmoid(-margin) * dgate * signs).astype(BF16)
            dlogits_ref[span, :] = dlogits
            chunk_refs[r][...] = (
                dot_nt(dpre, up_ref[...]) + dot_nt(dlogits, router_ref[...])
            ).astype(BF16)

    extra = [like(slots, hidden_width), like(slots, 1, dtype=F32)] if kept is None else []
    outs = kernel_call(
        body,
        [like(per, model)] * n_heads
        + [like(slots, hidden_width), like(slots, model), like(slots, LANES)]
        + extra,
        [place, dout_rows, *taken, up, down, router, other],
        flops=4 * slots * model * hidden_width,
        after=after,
    )
    return outs[:n_heads], outs[n_heads:]


def expert_grads(place, pairs, got=None, after=()):
    shapes = [(p[0].shape[1], p[1].shape[1]) for p in pairs]
    outs = [like(len(pairs), *shapes[0])] if got is None else [like(*x, dtype=F32) for x in shapes]
    picks = [a for pair in pairs for a in pair]

    def body(place_ref, *refs):
        held, refs = refs[: len(picks)], refs[len(picks) :]
        for i in range(len(pairs)):
            grad = dot_tn(held[2 * i].ready()[...], held[2 * i + 1].ready()[...])
            if got is None:
                refs[0][i] = grad.astype(BF16)
            else:
                refs[1 + i][...] = grad + refs[0][i].astype(F32)

    flops = sum(2 * p[0].shape[0] * p[0].shape[1] * p[1].shape[1] for p in pairs)
    args = [place, *picks] + ([] if got is None else [got])
    return kernel_call(body, outs, args, flops=flops, after=after, grant=WIDE_BYTES, mark=True)


def dense_grad(place, pairs, after=()):
    model = pairs[0][0].shape[1]
    widths = [b.shape[1] for _, b in pairs]
    width = sum(widths)

    def body(place_ref, *refs):
        at = 0
        for i, size in enumerate(widths):
            grad = dot_tn(refs[2 * i][...], refs[2 * i + 1][...])
            refs[-1][:, at : at + size] = grad.astype(BF16)
            at += size

    rows = pairs[0][0].shape[0]
    return kernel_call(
        body,
        [like(model, width)],
        [place, *(a for pair in pairs for a in pair)],
        flops=2 * rows * model * width,
        after=after,
        mark=True,
    )


def small_columns(rows_ref):
    rows = rows_ref[...]
    wide = jnp.concatenate([rows, jnp.zeros((LANES - rows.shape[0], rows.shape[1]), F32)])
    return wide.T


def joint_send(place, grad, smalls):
    model, width = grad.shape

    def body(place_ref, grad, one_ref, two_ref, out_ref):
        small = either(place_ref, small_columns(two_ref), small_columns(one_ref))
        out_ref[:, width:] = small.astype(BF16)
        out_ref[:, :width] = grad.ready()[...]

    return kernel_call(body, [like(model, width + LANES)], [place, grad, *smalls])[0]


def joint_sum(place, grad, smalls, got):
    model, width = grad.shape

    def body(place_ref, grad, one_ref, two_ref, got_ref, out_ref):
        small = either(place_ref, small_columns(one_ref), small_columns(two_ref))
        out_ref[:, width:] = (small + got_ref[:, width:].astype(F32)).astype(BF16)
        total = grad.ready()[...].astype(F32) + got_ref[:, :width].astype(F32)
        out_ref[:, :width] = total.astype(BF16)

    return kernel_call(body, [like(model, width + LANES)], [place, grad, *smalls, got])[0]


def joint_split(total, width, n_experts):
    share = total.shape[0]

    def body(total_ref, qkv_ref, out_ref, first_ref, second_ref, router_ref, bias_ref):
        for i, at in enumerate((0, 2, 3)):
            qkv_ref[i] = total_ref[:, at * width : (at + 1) * width].astype(F32)
        out_ref[...] = total_ref[:, width : 2 * width].astype(F32).T
        small = total_ref[:, 4 * width :].astype(F32)
        router_ref[...] = small[:, 2 : 2 + n_experts]
        rows = small.T
        first_ref[...] = rows[0:1]
        second_ref[...] = rows[1:2]
        bias_ref[...] = rows[2 + n_experts : 3 + n_experts]

    shapes = [(3, share, width), (width, share)] + [(1, share)] * 2 + [(share, n_experts), (1, share)]
    return kernel_call(body, [like(*shape, dtype=F32) for shape in shapes], [total])


def join_quarter(pieces, after):
    def body(*refs):
        rows = [ref[...].astype(F32) for ref in refs[:-1]]
        refs[-1][...] = jnp.concatenate(rows).astype(BF16)

    per, model = pieces[0].shape
    return kernel_call(body, [like(per * len(pieces), model)], pieces, after=after)[0]


def router_grads(place, pairs, n_experts):
    model = pairs[0][1].shape[1]

    def body(place_ref, *refs):
        for layer in range(2):
            grad = dot_tn(refs[2 * layer][...], refs[2 * layer + 1][...])
            refs[-1][layer * n_experts : (layer + 1) * n_experts, :] = grad[:n_experts]

    args = [place, *(a for pair in pairs for a in pair)]
    return kernel_call(body, [like(2 * n_experts, model, dtype=F32)], args)[0]


def small_rows(place, layer, dgain_first, dgain_second, router_parts, lanes, n_experts, n_ctx):
    model, count = dgain_first.shape[1], lanes.shape[0]
    share, bias_share = model // n_ctx, count // n_ctx
    rows = -(-(3 + n_experts) // 8) * 8

    def body(place_ref, first_ref, second_ref, lanes_ref, *refs):
        out_ref = refs[-1]
        router = tree_sum([ref[...] for ref in refs[:-1]])
        out_ref[...] = jnp.zeros(out_ref.shape, F32)
        out_ref[0:1, :] = first_ref[...]
        out_ref[1:2, :] = second_ref[...]
        out_ref[2 : 2 + n_experts, :] = router[layer * n_experts : (layer + 1) * n_experts]
        sums = jnp.sum(lanes_ref[...], axis=1, keepdims=True)
        value = lax.broadcasted_iota(jnp.int32, (count, model), 0)
        lane = lax.broadcasted_iota(jnp.int32, (count, model), 1)
        target = value
        for c in range(1, n_ctx):
            target += jnp.where(value >= c * bias_share, share - bias_share, 0)
        row = jnp.sum(jnp.where(lane == target, sums, 0.0), axis=0, keepdims=True)
        out_ref[2 + n_experts : 3 + n_experts, :] = row

    return kernel_call(
        body,
        [like(rows, model, dtype=F32)],
        [place, dgain_first, dgain_second, lanes, *router_parts],
    )[0]


def assemble(place, dx, got_out, got_dx, out):
    def body(place_ref, one, two, both_ref):
        both_ref[0] = one.ready()[...]
        both_ref[1] = two.ready()[...]

    picks = [Pick(dx, got_out), Pick(got_dx, out)]
    return kernel_call(body, [like(2, *dx.shape, dtype=F32)], [place, *picks])[0]


def combine(middle, returned, tokens, after):
    rows, model = middle.shape
    share = returned[0].shape[0]

    def body(middle_ref, tokens_ref, *refs):
        total = 0.0
        for r, ref in enumerate(refs[: len(returned)]):
            total += dot(token_picks(tokens_ref, share, r * share), ref[...])
        refs[-1][...] = middle_ref[...] + total

    return kernel_call(
        body,
        [like(rows, model, dtype=F32)],
        [middle, tokens, *returned],
        flops=2 * rows * model * share * len(returned),
        after=after,
        mark=True,
    )


def combine_project(place, middle, returned, tokens, gain, qkv):
    rows, model = middle.shape
    width = qkv.shape[2]

    def body(place_ref, middle_ref, returned_ref, tokens_ref, gain_ref, w, passed_ref, *outs):
        picks = token_picks(tokens_ref, returned_ref.shape[0])
        passed = (middle_ref[...] + dot(picks, returned_ref[...])).astype(BF16)
        passed_ref[...] = passed
        project_rows(passed.astype(F32), gain_ref[...], w, *outs)

    return kernel_call(
        body,
        [like(rows, model), like(rows, model), like(rows, width), like(rows, 2 * width)],
        [place, middle, returned, tokens, gain, qkv],
        flops=2 * rows * model * returned.shape[0] + 6 * rows * model * width,
    )


def norm_back(values, gain, upstream):
    scale = lax.rsqrt(jnp.mean(values * values, axis=-1, keepdims=True) + EPSILON)
    unit = values * scale
    scaled = upstream * gain
    dvalues = scale * (scaled - unit * jnp.mean(unit * scaled, axis=-1, keepdims=True))
    return dvalues, jnp.sum(upstream * unit, axis=0, keepdims=True)


def middle_back(place, returned, tokens, middle, gain, dout, out_w, after=()):
    rows, model = middle.shape
    width = out_w.shape[0]

    def body(place_ref, returned_ref, tokens_ref, middle_ref, gain_ref, dout_ref, w, *refs):
        dmiddle_ref, datt_ref, dmix_ref, dgain_ref = refs
        picks = token_picks(tokens_ref, returned_ref.shape[0])
        dexpert_in = dot(picks, returned_ref[...])
        part, dgain = norm_back(middle_ref[...], gain_ref[...], dexpert_in)
        dgain_ref[...] = dgain
        dmiddle = dout_ref[...].astype(F32) + part
        dmiddle_ref[...] = dmiddle
        datt = dmiddle.astype(BF16)
        datt_ref[...] = datt
        dmix_ref[...] = dot_nt(datt, w.ready()[...]).astype(BF16)

    return kernel_call(
        body,
        [
            like(rows, model, dtype=F32),
            like(rows, model),
            like(rows, width),
            like(1, model, dtype=F32),
        ],
        [place, returned, tokens, middle, gain, dout, out_w],
        flops=2 * rows * model * (returned.shape[0] + width),
        after=after,
    )


def project_back(place, dq, dkv_parts, qkv, n_heads, after=()):
    rows, width = dq.shape
    model, n_parts = qkv.shape[1], len(dkv_parts)
    share = rows // n_heads

    def body(place_ref, dq_ref, *refs):
        part_refs, refs = refs[:n_parts], refs[n_parts:]
        w, dkv_ref = refs[:2]
        chunk_refs, total_ref = refs[2:-1], refs[-1]
        dkv = part_refs[0][...].astype(F32)
        for ref in part_refs[1:]:
            dkv += ref[...].astype(F32)
        dkv = dkv.astype(BF16)
        dkv_ref[...] = dkv
        w_ref = w.ready()
        total_ref[...] = (
            dot_nt(dq_ref[...], w_ref[0])
            + dot_nt(dkv[:, :width], w_ref[1])
            + dot_nt(dkv[:, width:], w_ref[2])
        )
        for r in range(n_heads):
            first = pl.multiple_of((place_ref[1] ^ r) * share, share)
            chunk_refs[r][...] = total_ref[pl.ds(first, share), :].astype(BF16)

    outs = kernel_call(
        body,
        [like(rows, 2 * width)] + [like(share, model)] * n_heads,
        [place, dq, *dkv_parts, qkv],
        [pltpu.VMEM((rows, model), F32)],
        flops=6 * rows * model * width,
        after=after,
    )
    return outs[0], outs[1:]


def tree_sum(values):
    while len(values) > 1:
        values = [values[i] + values[i + 1] for i in range(0, len(values), 2)]
    return values[0]


def share_sum(parts):
    def body(*refs):
        refs[-1][...] = tree_sum([ref[...].astype(F32) for ref in refs[:-1]]).astype(BF16)

    return kernel_call(body, [like(*parts[0].shape)], parts)[0]


def input_back(place, dnormed_parts, x, gain, dmiddle, tokens=None, n_ctx=0, per=0, after=()):
    rows, model = x.shape
    n_heads, share = len(dnormed_parts), dnormed_parts[0].shape[0]
    given = [x, gain, dmiddle] + ([] if tokens is None else [tokens])

    def body(place_ref, *refs):
        part_refs, refs = refs[:n_heads], refs[n_heads:]
        x_ref, gain_ref, dmiddle_ref = refs[:3]
        (dx_ref, dgain_ref), chunk_refs = refs[len(given) :][:2], refs[len(given) + 2 : -1]
        dnormed_ref = refs[-1]
        for r in range(n_heads):
            first = pl.multiple_of((place_ref[1] ^ r) * share, share)
            dnormed_ref[pl.ds(first, share), :] = part_refs[r][...].astype(F32)
        part, dgain = norm_back(x_ref[...].astype(F32), gain_ref[...], dnormed_ref[...])
        dgain_ref[...] = dgain
        dx = (dmiddle_ref[...] + part).astype(dx_ref.dtype)
        dx_ref[...] = dx
        if tokens is not None:
            dispatch_into(dx, place_ref, refs[3], chunk_refs)

    outs = kernel_call(
        body,
        [like(rows, model, dtype=F32 if tokens is None else BF16), like(1, model, dtype=F32)]
        + [like(per, model)] * n_ctx,
        [place, *dnormed_parts, *given],
        [pltpu.VMEM((rows, model), F32)],
        after=after,
    )
    return outs[0], outs[1], outs[2:]


def bucket_of(distance):
    exact_span = BUCKETS // 2
    result = jnp.minimum(distance, exact_span)
    for rank in range(1, BUCKETS - exact_span):
        edge = int(
            math.ceil(exact_span * (REACH / exact_span) ** (rank / (BUCKETS - exact_span)))
        )
        result = result + (distance >= edge).astype(jnp.int32)
    return result


def tile_buckets(half):
    row = lax.broadcasted_iota(jnp.int32, (half, half), 0)
    col = lax.broadcasted_iota(jnp.int32, (half, half), 1)
    same = jnp.where(row >= col, bucket_of(jnp.maximum(row - col, 0)), -1)
    return [same, bucket_of(half + row - col), bucket_of(2 * half + row - col)]


def bias_tables(place, own, other, half, after):
    heads = own.shape[1]

    def body(place_ref, bias_refs, *refs):
        buckets = tile_buckets(half)
        for layer, out_ref in enumerate(refs[-2:]):
            for head in range(heads):
                out_ref[head, 0] = jnp.full((half, half), NEGATIVE, F32)
                values = [jnp.full((half, half), NEGATIVE, F32) for _ in buckets[:2]]
                for bucket in range(BUCKETS):
                    value = bias_refs[place_ref[2] ^ layer, bucket, head]
                    values = [
                        jnp.where(b == bucket, value, v) for b, v in zip(buckets, values)
                    ]
                out_ref[head, 1] = values[0]
                out_ref[head, 2] = values[1]
                far = bias_refs[place_ref[2] ^ layer, BUCKETS - 1, head]
                out_ref[head, 3] = jnp.full((half, half), far, F32)

    shape = like(heads, 4, half, half, dtype=F32)
    return pl.pallas_call(
        body,
        out_shape=[shape] * 2,
        in_specs=[pl.BlockSpec(memory_space=pltpu.SMEM)] * 2
        + [pl.BlockSpec(memory_space=pl.ANY)] * len(after),
        out_specs=[pl.BlockSpec(memory_space=pltpu.VMEM)] * 2,
        compiler_params=pltpu.CompilerParams(vmem_limit_bytes=2 * SPARE_BYTES),
    )(place, jnp.stack([own, other]), *after)


def small_weights(place, gains, routers, after):
    model, n_experts = routers[0].shape

    def body(place_ref, *refs):
        ins, outs = refs[:6], refs[-6:]
        for kind in range(2):
            own, other = (ref[...].astype(F32) for ref in ins[2 * kind : 2 * kind + 2])
            outs[2 * kind][...] = either(place_ref, own, other)
            outs[2 * kind + 1][...] = either(place_ref, other, own)
        own, other = (ref[...].astype(F32) for ref in ins[4:6])
        for out_ref, value in zip(
            outs[4:], (either(place_ref, own, other), either(place_ref, other, own))
        ):
            out_ref[...] = jnp.zeros(out_ref.shape, BF16)
            out_ref[:, :n_experts] = value.astype(BF16)

    args = [place, *gains[0], *gains[1], *routers]
    outs = kernel_call(
        body,
        [like(1, model, dtype=F32)] * 4 + [like(model, LANES)] * 2,
        args,
        after=after,
    )
    return outs[0:2], outs[2:4], outs[4:6]


def layer_row(place_ref, pair_ref, layer, k):
    rows = pair_ref.shape[3]
    row = pair_ref[place_ref[2] ^ layer, place_ref[2], k : k + 1, :]
    eye = lax.broadcasted_iota(jnp.int32, (rows, rows), 0) == lax.broadcasted_iota(
        jnp.int32, (rows, rows), 1
    )
    return jnp.sum(jnp.where(eye, row, 0).astype(F32), axis=1, keepdims=True).astype(jnp.int32)


def earlier(rows):
    row = lax.broadcasted_iota(jnp.int32, (rows, rows), 0)
    col = lax.broadcasted_iota(jnp.int32, (rows, rows), 1)
    return jnp.where(row > col, 1.0, 0.0).astype(BF16)


def quarter_of(rank, per, n_heads):
    return sum([(rank >= h * per).astype(jnp.int32) for h in range(1, n_heads)])


def token_slots(place, pair, n_experts, per, n_heads, after):
    rows = pair.shape[3]

    def body(place_ref, pair_ref, *refs):
        outs = refs[-3:]
        for layer in range(2):
            choices = [layer_row(place_ref, pair_ref, layer, k) for k in range(2)]
            lane = lax.broadcasted_iota(jnp.int32, (rows, LANES), 1)
            hots = [jnp.where(lane == choice, 1.0, 0.0) for choice in choices]
            ranks = dot(earlier(rows), (hots[0] + hots[1]).astype(BF16))
            for k in range(2):
                rank = jnp.sum(ranks * hots[k], axis=1, keepdims=True).astype(jnp.int32)
                quarter = quarter_of(rank, per, n_heads)
                inner = (choices[k] ^ place_ref[0]) * per + rank - quarter * per
                outs[layer][:, k : k + 1] = quarter * (n_experts * per) + inner
                if layer == 1:
                    outs[2][:, k : k + 1] = (quarter ^ place_ref[1]) * (n_experts * per) + inner

    return kernel_call(
        body, [like(rows, 2, dtype=jnp.int32)] * 3, [place, pair], after=after
    )


def other_experts(place, pairs, per, n_heads):
    n_ctx, rows = len(pairs), pairs[0].shape[3]

    def body(place_ref, *refs):
        before = earlier(rows)
        lane = lax.broadcasted_iota(jnp.int32, (rows, per), 1)
        for layer, out_ref in enumerate(refs[n_ctx:]):
            for r, pair_ref in enumerate(refs[:n_ctx]):
                one, two = (layer_row(place_ref, pair_ref, layer, k) for k in range(2))
                here = (one == place_ref[0]) | (two == place_ref[0])
                other = jnp.where(one == place_ref[0], two, one).astype(F32)
                other = jnp.broadcast_to(other, (rows, LANES)).astype(BF16)
                wide = jnp.broadcast_to(jnp.where(here, 1.0, 0.0), (rows, LANES)).astype(BF16)
                rank = dot(before, wide)[:, 0:1].astype(jnp.int32)
                rank = jnp.where(here, rank, -1)
                for h in range(n_heads):
                    picks = jnp.where(lane + h * per == rank, 1.0, 0.0).astype(BF16)
                    found = dot_tn(picks, other)[:, 0:1].astype(jnp.int32)
                    at = (h * n_ctx + r) * per
                    out_ref[at : at + per, :] = found

    return kernel_call(
        body, [like(n_heads * n_ctx * per, 1, dtype=jnp.int32)] * 2, [place, *pairs]
    )


def table_back(dtable, after=()):
    heads, half = dtable.shape[0], dtable.shape[3]

    def body(dtable_ref, *refs):
        out_ref, buckets = refs[-1], tile_buckets(half)
        for bucket in range(BUCKETS):
            hits = [held == bucket for held in buckets]
            for head in range(heads):
                kept = jnp.zeros((half, half), F32)
                for tile, hit in enumerate(hits):
                    kept += jnp.where(hit, dtable_ref[head, 1 + tile], 0.0)
                at = bucket * heads + head
                out_ref[at : at + 1, :] = jnp.sum(kept, axis=0, keepdims=True)

    return kernel_call(
        body, [like(BUCKETS * heads, half, dtype=F32)], [dtable], after=after
    )[0]


def heads_sum(chunks, n_ctx, after=()):
    parts = exchange(chunks, "heads")
    rows, model = parts[0].shape
    per = rows // n_ctx

    def body(*refs):
        total = tree_sum([ref[...].astype(F32) for ref in refs[: len(parts)]])
        for r, out_ref in enumerate(refs[len(parts) :]):
            out_ref[...] = total[r * per : (r + 1) * per].astype(BF16)

    return kernel_call(body, [like(per, model)] * n_ctx, parts, after=after)


def return_rows(chunks, n_ctx, after=()):
    back = exchange(heads_sum(chunks, n_ctx, after), "ctx")
    return gather_rows(jnp.concatenate(back, axis=0), "heads")


def send_rows(chunks):
    return gather_rows(jnp.concatenate(exchange(chunks, "ctx"), axis=0), "heads")


def body(
    boundary,
    norm_first,
    qkv_weight,
    position_bias,
    out_weight,
    norm_second,
    router,
    expert_up,
    expert_down,
    routes,
):
    section = lax.axis_index("section")
    ctx_index = lax.axis_index("ctx")
    heads_index = lax.axis_index("heads")
    n_ctx, n_heads = lax.axis_size("ctx"), lax.axis_size("heads")
    first = section == 0
    place = jnp.stack([ctx_index, heads_index, section]).astype(jnp.int32)
    rows, model = boundary.shape[2:]
    half = rows // 2
    n_experts, heads = router.shape[2], position_bias.shape[2]
    per = 5 * rows // (2 * n_experts) // n_heads

    def by_layer(own, other):
        return Pick(own, other), Pick(other, own)

    def with_other(own):
        return own, swap(own, "section")

    given = swap(lax.dynamic_index_in_dim(boundary[0], 1 - section, 0, False), "section")
    gain_pairs = with_other(norm_first), with_other(norm_second)
    qkv = by_layer(*with_other(qkv_weight[0]))
    x0, cotangent, normed0, q0, kv0 = begin(place, boundary[0], given, *gain_pairs[0], qkv[0])
    kv_all0 = gather_rows(kv0, "ctx")

    gains_first, gains_second, routers = small_weights(
        place, gain_pairs, with_other(router[0]), [kv0]
    )
    biases = bias_tables(place, *with_other(position_bias[0]), half, [kv0])
    pair = jnp.stack(with_other(routes[0].transpose(0, 2, 1)))
    *tokens, tokens_near = token_slots(place, pair, n_experts, per, n_heads, [kv0])
    others = other_experts(place, exchange([pair] * n_ctx, "ctx"), per, n_heads)
    up = by_layer(*with_other(expert_up[0, 0]))
    down = by_layer(*with_other(expert_down[0, 0]))
    width = out_weight.shape[1]
    out_gathered = gather_rows(jnp.concatenate(with_other(out_weight[0]), axis=0), "heads")
    out_full = [Rows(out_gathered, layer, width) for layer in range(2)]
    out_own = [Rows(out_gathered, layer, width, own=True) for layer in range(2)]

    def before_experts(layer, x, q, kv_all):
        mix, lse = attend(place, q, [kv_all], biases[layer], n_ctx)
        mixes = exchange([mix] * n_heads, "heads")
        middle, chunks = finish_attention(
            place, mixes, out_full[layer], x, gains_second[layer], tokens[layer], n_ctx, per
        )
        return mix, lse, middle, send_rows(chunks)

    def expert_weights(layer):
        return up[layer], down[layer], routers[layer], others[layer]

    mix0, lse0, middle0, arrived0 = before_experts(0, x0, q0, kv_all0)
    chunks, kept0 = experts(place, arrived0, *expert_weights(0), n_heads)
    dout_chunks = dispatch_whole(place, cotangent, tokens[1], n_ctx, per, n_heads, [middle0])
    returned = return_rows(chunks, n_ctx)
    x1, normed1, q1, kv1 = combine_project(
        place, middle0, returned, tokens[0], gains_first[1], qkv[1]
    )

    kv_all1 = gather_rows(kv1, "ctx")
    mix1, lse1, middle1, arrived1 = before_experts(1, x1, q1, kv_all1)
    dout_rows1 = jnp.stack(exchange(dout_chunks, "ctx"))
    dout_rows1 = dout_rows1.reshape(n_ctx, n_heads, per, model).transpose(1, 0, 2, 3)
    dout_rows1 = dout_rows1.reshape(-1, model)
    chunks, (dpre1, dslots1, dlogits1, hidden1, margin1) = experts_back(
        place, dout_rows1, None, arrived1, *expert_weights(1), n_heads
    )
    dmiddle1, datt1, dmix1, dgain_second1 = middle_back(
        place, return_rows(chunks, n_ctx), tokens[1], middle1, gains_second[1], cotangent, out_own[1]
    )
    dq1, dtable1, dkv1 = attend_back(place, q1, [kv_all1], biases[1], lse1, dmix1, n_ctx)
    out_total = heads_sum(
        experts_out(place, hidden1, margin1, down[1], n_heads, [dq1]), n_ctx
    )
    dkv_sum1, chunks = project_back(
        place, dq1, exchange(dkv1, "ctx"), qkv[1], n_heads, [out_total[0]]
    )
    total1 = share_sum(exchange(chunks, "heads"))
    lanes1 = table_back(dtable1)
    out_back = exchange(out_total, "ctx")
    dense1, made = dense_grad(place, [(normed1, dq1), (datt1, mix1), (normed1, dkv_sum1)])
    dx1, dgain_first1, sent = input_back(
        place,
        exchange([total1] * n_heads, "heads"),
        x1,
        gains_first[1],
        dmiddle1,
        tokens[0],
        n_ctx,
        per,
        [lanes1, made, *out_back[1:]],
    )

    dout_rows0 = send_rows(sent)
    chunks, (dpre0, dslots0, dlogits0) = experts_back(
        place, dout_rows0, kept0, arrived0, *expert_weights(0), n_heads
    )
    lists = [(arrived0, arrived1), (dpre0, dpre1), (kept0[1], hidden1), (dslots0, dslots1)]
    mine, theirs = [Pick(a, b) for a, b in lists], [Pick(b, a) for a, b in lists]
    sends, sends_made = expert_grads(place, [theirs[:2], theirs[2:]])
    returned = return_rows(chunks, n_ctx, [sends_made])
    router_part = router_grads(place, [(dlogits0, arrived0), (dlogits1, arrived1)], n_experts)
    dmiddle0, datt0, dmix0, dgain_second0 = middle_back(
        place,
        returned,
        tokens[0],
        middle0,
        gains_second[0],
        dx1,
        out_own[0],
        [router_part],
    )
    dq0, dtable0, dkv0 = attend_back(place, q0, [kv_all0], biases[0], lse0, dmix0, n_ctx)
    lanes0 = table_back(dtable0)
    router_parts = exchange([router_part] * n_heads, "heads")
    small1 = small_rows(
        place, 1, dgain_first1, dgain_second1, router_parts, lanes1, n_experts, n_ctx
    )
    quarter = join_quarter(out_back, [dq0])
    out, out_made = combine(middle1, exchange([quarter] * n_heads, "heads"), tokens_near, [])
    dkv_sum0, chunks = project_back(
        place, dq0, exchange(dkv0, "ctx"), qkv[0], n_heads, [small1, out_made]
    )
    parts = exchange(chunks, "heads")
    total0 = share_sum(parts)
    dense0, made = dense_grad(
        place, [(normed0, dq0), (datt0, mix0), (normed0, dkv_sum0)], parts[1:2]
    )
    dx0, dgain_first0, _ = input_back(
        place,
        exchange([total0] * n_heads, "heads"),
        x0,
        gains_first[0],
        dmiddle0,
        after=[made, lanes0],
    )

    got_dx = one_way(dx0, 1)
    small0 = small_rows(
        place, 0, dgain_first0, dgain_second0, router_parts, lanes0, n_experts, n_ctx
    )
    smalls = [small0, small1]
    got = swap(joint_send(place, Pick(dense1, dense0), smalls), "section")
    joint = joint_sum(place, Pick(dense0, dense1), smalls, got)
    joint = lax.psum_scatter(joint, "ctx", scatter_dimension=0, tiled=True)
    grad_up, grad_down, _ = expert_grads(
        place, [mine[:2], mine[2:]], swap(sends, "section"), after=[dgain_first0]
    )
    grad_qkv, grad_out, grad_first, grad_second, grad_router, grad_bias = joint_split(
        joint, width, n_experts
    )
    bias_share = BUCKETS // n_ctx
    grad_bias = grad_bias[:, : bias_share * heads].reshape(1, bias_share, heads)
    boundary_out = assemble(place, dx0, one_way(out, 0), got_dx, out)
    return (
        boundary_out[None],
        grad_first,
        grad_qkv[None],
        grad_bias,
        grad_out[None],
        grad_second,
        grad_router[None],
        grad_up[None, None],
        grad_down[None, None],
    )


def solution(mesh):
    placed = (
        P("section", None, "ctx", None),
        P("section", None),
        P("section", None, None, "heads"),
        P("section", None, "heads"),
        P("section", "heads", None),
        P("section", None),
        P("section", None, None),
        P("section", "ctx", None, "heads"),
        P("section", "ctx", "heads", None),
        P("section", None, "ctx", None),
    )
    return jax.shard_map(
        body,
        mesh=mesh,
        in_specs=placed,
        out_specs=(
            P("section", None, "ctx", None),
            P("section", "ctx"),
            P("section", None, "ctx", "heads"),
            P("section", "ctx", "heads"),
            P("section", "heads", "ctx"),
            P("section", "ctx"),
            P("section", "ctx", None),
            P("section", "ctx", None, "heads"),
            P("section", "ctx", "heads", None),
        ),
        check_vma=False,
    )
```

```python
import math

import jax
import jax.numpy as jnp
from jax import lax
from jax.experimental import pallas as pl
from jax.experimental.pallas import tpu as pltpu
from jax.sharding import PartitionSpec as P

HD = 64
BUCKETS = 32
REACH = 128
EPSILON = 1e-06
NEGATIVE = -1e30
F32 = jnp.float32
BF16 = jnp.bfloat16
LANES = 128
SPARE_BYTES = 6 * 1024 * 1024
WIDE_BYTES = 48 * 1024 * 1024
ROOT_2_PI = math.sqrt(2.0 / math.pi)


class Pick:
    def __init__(self, first, second):
        self.arrays, self.shape = (first, second), first.shape
        self.dtype, self.ndim = first.dtype, first.ndim


class Rows:
    def __init__(self, array, layer, width, own=False):
        n_heads = array.shape[0] // (2 * width)
        self.array, self.layer, self.width, self.own = array, layer, width, own
        self.shape = (width if own else n_heads * width,) + array.shape[1:]
        self.dtype, self.ndim, self.n_heads = array.dtype, array.ndim, n_heads


class Held:
    def __init__(self, buffer, wait):
        self.buffer, self.wait, self.here = buffer, wait, False

    def ready(self):
        if not self.here:
            self.wait()
        self.here = True
        return self.buffer


def padded_bytes(array):
    *lead, rows, lanes = (1, 1) + tuple(array.shape)
    return math.prod(lead) * (-(-rows // 16) * 16) * (-(-lanes // LANES) * LANES) * jnp.dtype(array.dtype).itemsize


def kernel_call(body, outs, args, scratch=(), flops=0, after=(), grant=0, mark=False):
    if mark:
        outs = list(outs) + [like(8, LANES, dtype=F32)]
    picks = [a for a in args if isinstance(a, (Pick, Rows))]
    operands, in_specs = [], []
    for a in args:
        if isinstance(a, (Pick, Rows)):
            arrays = a.arrays if isinstance(a, Pick) else (a.array,)
            operands += arrays
            in_specs += [pl.BlockSpec(memory_space=pltpu.HBM)] * len(arrays)
        else:
            scalar = a.ndim == 1 and a.dtype == jnp.int32
            operands.append(a)
            in_specs.append(pl.BlockSpec(memory_space=pltpu.SMEM if scalar else pltpu.VMEM))
    operands += after
    in_specs += [pl.BlockSpec(memory_space=pl.ANY)] * len(after)
    scratch = list(scratch) + [pltpu.VMEM(p.shape, p.dtype) for p in picks]
    if picks:
        scratch.append(pltpu.SemaphoreType.DMA((len(picks),)))
    n_out, n_own = len(outs), len(scratch) - len(picks) - (1 if picks else 0)

    def hold(a, sources, place_ref, buffer, sem):
        if isinstance(a, Pick):
            for section, src in enumerate(sources):

                @pl.when(place_ref[2] == section)
                def _(src=src):
                    pltpu.make_async_copy(src, buffer, sem).start()

            return Held(buffer, pltpu.make_async_copy(sources[0], buffer, sem).wait)
        copies = []
        for h in range(1 if a.own else a.n_heads):
            block = 2 * (place_ref[1] if a.own else h) + (place_ref[2] ^ a.layer)
            src = sources[0].at[pl.ds(pl.multiple_of(block * a.width, a.width), a.width)]
            dst = buffer.at[pl.ds(h * a.width, a.width)]
            copies.append(pltpu.make_async_copy(src, dst, sem))
            copies[-1].start()

        def wait():
            for copy in copies:
                copy.wait()

        return Held(buffer, wait)

    def wrapped(*refs):
        ins, rest = refs[: len(operands)], refs[len(operands) :]
        buffers = list(rest[n_out + n_own :])
        given, at, number = [], 0, 0
        for a in args:
            if not isinstance(a, (Pick, Rows)):
                given.append(ins[at])
                at += 1
                continue
            count = 2 if isinstance(a, Pick) else 1
            sem = buffers[-1].at[number]
            given.append(hold(a, ins[at : at + count], ins[0], buffers[number], sem))
            at, number = at + count, number + 1
        if mark:
            rest[n_out - 1][...] = jnp.zeros((8, LANES), F32)
            rest = rest[: n_out - 1] + rest[n_out:]
        body(*given, *rest[: n_out + n_own - mark])

    size = sum(math.prod(a.shape) * a.dtype.itemsize for a in list(args) + list(outs))
    held = sum(map(padded_bytes, list(args) + list(outs)))
    held += sum(padded_bytes(s) for s in scratch[:n_own])
    return pl.pallas_call(
        wrapped,
        out_shape=outs,
        in_specs=in_specs,
        out_specs=[pl.BlockSpec(memory_space=pltpu.VMEM)] * n_out,
        scratch_shapes=scratch,
        compiler_params=pltpu.CompilerParams(vmem_limit_bytes=max(grant, held + SPARE_BYTES)),
        cost_estimate=pl.CostEstimate(flops=flops, bytes_accessed=size, transcendentals=0),
    )(*operands)


def like(*shape, dtype=BF16):
    return jax.ShapeDtypeStruct(shape, dtype)


def dot(a, b, contract=((1,), (0,))):
    return lax.dot_general(a, b, (contract, ((), ())), preferred_element_type=F32)


def dot_nt(a, b):
    return dot(a, b, ((1,), (1,)))


def dot_tn(a, b):
    return dot(a, b, ((0,), (0,)))


def swap(array, axis, by=1):
    devices = lax.axis_size(axis)
    return lax.ppermute(array, axis, [(i, i ^ by) for i in range(devices)])


def one_way(array, source):
    return lax.ppermute(array, "section", [(source, 1 - source)])


def exchange(chunks, axis):
    return [chunks[0]] + [swap(chunks[r], axis, r) for r in range(1, len(chunks))]


def gather_rows(array, axis):
    return lax.all_gather(array, axis, axis=0, tiled=True)


def project_rows(x, gain, w, normed_ref, q_ref, kv_ref):
    width = q_ref.shape[1]
    scale = lax.rsqrt(jnp.mean(x * x, axis=-1, keepdims=True) + EPSILON)
    normed = (x * scale * gain).astype(BF16)
    normed_ref[...] = normed
    w_ref = w.ready()
    kv_ref[:, :width] = dot(normed, w_ref[1]).astype(BF16)
    kv_ref[:, width:] = dot(normed, w_ref[2]).astype(BF16)
    q_ref[...] = dot(normed, w_ref[0]).astype(BF16)


def either(place_ref, first, second):
    return jnp.where(place_ref[2] == 0, first, second)


def begin(place, own, given, gain_own, gain_other, qkv):
    _, rows, model = own.shape
    width = qkv.shape[2]

    def body(place_ref, own_ref, given_ref, gain_ref, other_ref, w, x_ref, cotangent_ref, *outs):
        x = either(place_ref, own_ref[0], given_ref[...])
        x_ref[...] = x
        cotangent_ref[...] = either(place_ref, given_ref[...], own_ref[1])
        gain = either(place_ref, gain_ref[...].astype(F32), other_ref[...].astype(F32))
        project_rows(x.astype(F32), gain, w, *outs)

    return kernel_call(
        body,
        [like(rows, model)] * 3 + [like(rows, width), like(rows, 2 * width)],
        [place, own, given, gain_own, gain_other, qkv],
        flops=6 * rows * model * width,
    )


def tile_pick(block, key_tile, mine, ordered, n_ctx):
    owner = key_tile // 2 if ordered else mine ^ (key_tile // 2)
    key_block = owner if key_tile % 2 == 0 else 2 * n_ctx - 1 - owner
    return jnp.clip(block - key_block, -1, 2) + 1


def query_parts(mine, half, n_ctx):
    return [
        (slice(0, half), mine),
        (slice(half, 2 * half), 2 * n_ctx - 1 - mine),
    ]


def load_keys(kv_refs, kv_ref):
    rows = kv_refs[0].shape[0]
    for r, ref in enumerate(kv_refs):
        kv_ref[r * rows : (r + 1) * rows, :] = ref[...]


def attend(place, q, kv_parts, table, n_ctx):
    rows, width = q.shape
    half, heads, keys = rows // 2, width // HD, rows * n_ctx
    ordered, count = len(kv_parts) == 1, len(kv_parts)

    def body(place_ref, q_ref, *refs):
        kv_refs, (table_ref, mix_ref, lse_ref, scores_ref, kv_ref) = refs[:count], refs[count:]
        mine = place_ref[0]
        load_keys(kv_refs, kv_ref)
        for head in range(heads):
            cols = slice(head * HD, (head + 1) * HD)
            key_rows = kv_ref[:, cols]
            value_rows = kv_ref[:, width + head * HD : width + (head + 1) * HD]
            for part, (span, block) in enumerate(query_parts(mine, half, n_ctx)):
                raw = dot_nt(q_ref[span, cols], key_rows)
                for key_tile in range(2 * n_ctx):
                    pick = tile_pick(block, key_tile, mine, ordered, n_ctx)
                    tile = slice(key_tile * half, (key_tile + 1) * half)
                    scores_ref[part, :, tile] = raw[:, tile] * 0.125 + table_ref[head, pick]
                scores = scores_ref[part]
                top = jnp.max(scores, axis=1, keepdims=True)
                mass = jnp.exp(scores - top)
                total = jnp.sum(mass, axis=1, keepdims=True)
                out = dot(mass.astype(BF16), value_rows) / total
                mix_ref[span, cols] = out.astype(BF16)
                lse_ref[span, head : head + 1] = top + jnp.log(total)

    return kernel_call(
        body,
        [like(rows, width), like(rows, heads, dtype=F32)],
        [place, q, *kv_parts, table],
        [pltpu.VMEM((2, half, keys), F32), pltpu.VMEM((keys, 2 * width), BF16)],
        flops=4 * rows * keys * width,
    )


def attend_back(place, q, kv_parts, table, lse, dmix, n_ctx):
    rows, width = q.shape
    half, heads, keys = rows // 2, width // HD, rows * n_ctx
    ordered, count = len(kv_parts) == 1, len(kv_parts)

    def body(place_ref, q_ref, *refs):
        kv_refs, refs = refs[:count], refs[count:]
        table_ref, lse_ref, dmix_ref, dq_ref, dtable_ref = refs[:5]
        chunk_refs, (scores_ref, total_ref, kv_ref) = refs[5 : 5 + n_ctx], refs[5 + n_ctx :]
        mine = place_ref[0]
        load_keys(kv_refs, kv_ref)
        dtable_ref[...] = jnp.zeros(dtable_ref.shape, F32)
        for head in range(heads):
            cols = slice(head * HD, (head + 1) * HD)
            value_cols = slice(width + head * HD, width + (head + 1) * HD)
            key_rows = kv_ref[:, cols]
            value_rows = kv_ref[:, value_cols]
            for part, (span, block) in enumerate(query_parts(mine, half, n_ctx)):
                q = q_ref[span, cols]
                dmix = dmix_ref[span, cols]
                raw = dot_nt(q, key_rows)
                for key_tile in range(2 * n_ctx):
                    pick = tile_pick(block, key_tile, mine, ordered, n_ctx)
                    tile = slice(key_tile * half, (key_tile + 1) * half)
                    scores_ref[part, :, tile] = raw[:, tile] * 0.125 + table_ref[head, pick]
                probs = jnp.exp(scores_ref[part] - lse_ref[span, head : head + 1])
                dprobs = dot_nt(dmix, value_rows)
                delta = jnp.sum(probs * dprobs, axis=1, keepdims=True)
                dscores = (probs * (dprobs - delta)).astype(BF16)
                dq_ref[span, cols] = (dot(dscores, key_rows) * 0.125).astype(BF16)
                dkeys = dot_tn(dscores, q) * 0.125
                dvalues = dot_tn(probs.astype(BF16), dmix)
                if part == 0:
                    total_ref[:, cols] = dkeys
                    total_ref[:, value_cols] = dvalues
                else:
                    total_ref[:, cols] += dkeys
                    total_ref[:, value_cols] += dvalues
                for key_tile in range(2 * n_ctx):
                    pick = tile_pick(block, key_tile, mine, ordered, n_ctx)
                    tile = dscores[:, key_tile * half : (key_tile + 1) * half]
                    dtable_ref[head, pick] += tile.astype(F32)
        for r in range(n_ctx):
            first = pl.multiple_of((mine ^ r if ordered else r) * rows, rows)
            chunk_refs[r][...] = total_ref[pl.ds(first, rows), :].astype(BF16)

    outs = kernel_call(
        body,
        [like(rows, width), like(*table.shape, dtype=F32)] + [like(rows, 2 * width)] * n_ctx,
        [place, q, *kv_parts, table, lse, dmix],
        [
            pltpu.VMEM((2, half, keys), F32),
            pltpu.VMEM((keys, 2 * width), F32),
            pltpu.VMEM((keys, 2 * width), BF16),
        ],
        flops=10 * rows * keys * width,
    )
    return outs[0], outs[1], outs[2:]


def token_picks(tokens_ref, count, first=0):
    ids = first + lax.broadcasted_iota(jnp.int32, (tokens_ref.shape[0], count), 1)
    hit = (ids == tokens_ref[:, 0:1]) | (ids == tokens_ref[:, 1:2])
    return jnp.where(hit, 1.0, 0.0).astype(BF16)


def dispatch_into(rows, place_ref, tokens_ref, chunk_refs):
    per = chunk_refs[0].shape[0]
    first = place_ref[1] * (per * len(chunk_refs))
    for r, chunk_ref in enumerate(chunk_refs):
        picks = token_picks(tokens_ref, per, first + r * per)
        chunk_ref[...] = dot_tn(picks, rows).astype(BF16)


def dispatch_whole(place, rows, tokens, n_ctx, per, n_heads, after):
    count, model = rows.shape

    def body(place_ref, rows_ref, tokens_ref, *chunk_refs):
        lane = lax.broadcasted_iota(jnp.int32, (count, n_heads * per), 1)
        ids = lane
        for h in range(1, n_heads):
            ids += jnp.where(lane >= h * per, (n_ctx - 1) * per, 0)
        for r, chunk_ref in enumerate(chunk_refs):
            here = ids + r * per
            hit = (here == tokens_ref[:, 0:1]) | (here == tokens_ref[:, 1:2])
            picks = jnp.where(hit, 1.0, 0.0).astype(BF16)
            chunk_ref[...] = dot_tn(picks, rows_ref[...]).astype(BF16)

    return kernel_call(
        body, [like(n_heads * per, model)] * n_ctx, [place, rows, tokens], after=after
    )


def finish_attention(place, mixes, out_w, x, gain, tokens, n_ctx, per):
    rows, model = x.shape
    n_heads, width = len(mixes), mixes[0].shape[1]

    def body(place_ref, *refs):
        mix_refs, refs = refs[:n_heads], refs[n_heads:]
        w_ref, x_ref, gain_ref, tokens_ref, middle_ref = refs[:5]
        chunk_refs, mixed_ref = refs[5:-1], refs[-1]
        for r in range(n_heads):
            mixed_ref[place_ref[1] ^ r] = mix_refs[r][...]
        middle = x_ref[...].astype(F32)
        w_ref = w_ref.ready()
        attended = dot(mixed_ref[0], w_ref[:width, :])
        for h in range(1, n_heads):
            attended += dot(mixed_ref[h], w_ref[h * width : (h + 1) * width, :])
        middle = middle + attended
        middle_ref[...] = middle
        scale = lax.rsqrt(jnp.mean(middle * middle, axis=-1, keepdims=True) + EPSILON)
        expert_in = (middle * scale * gain_ref[...]).astype(BF16)
        dispatch_into(expert_in, place_ref, tokens_ref, chunk_refs)

    outs = kernel_call(
        body,
        [like(rows, model, dtype=F32)] + [like(per, model)] * n_ctx,
        [place, *mixes, out_w, x, gain, tokens],
        [pltpu.VMEM((n_heads, rows, width), BF16)],
        flops=2 * rows * model * model + 2 * rows * model * per * n_ctx,
    )
    return outs[0], outs[1:]


def gelu_parts(v):
    inner = jnp.tanh(ROOT_2_PI * (v + 0.044715 * v * v * v))
    return inner, 0.5 * v * (1.0 + inner)


def route_signs(place_ref, other):
    lane = lax.broadcasted_iota(jnp.int32, (other.shape[0], LANES), 1)
    return jnp.where(lane == place_ref[0], 1.0, 0.0) - jnp.where(lane == other, 1.0, 0.0)


def expert_hidden(place_ref, rows, up_ref, router_ref, other):
    logits = dot(rows, router_ref[...])
    margin = jnp.sum(logits * route_signs(place_ref, other), axis=1, keepdims=True)
    pre_act = dot(rows, up_ref[...])
    return margin, pre_act, gelu_parts(pre_act)[1].astype(BF16)


def sigmoid(v):
    return 1.0 / (1.0 + jnp.exp(-v))


def experts(place, arrived, up, down, router, other, n_heads):
    slots, model = arrived.shape
    per, hidden_width = slots // n_heads, up.shape[1]

    def body(place_ref, in_ref, up, down, router_ref, other_ref, *refs):
        chunk_refs, (pre_ref, hidden_ref, margin_ref) = refs[:n_heads], refs[n_heads:]
        up_ref = up.ready()
        for r in range(n_heads):
            span = pl.ds(pl.multiple_of((place_ref[1] ^ r) * per, per), per)
            margin, pre_act, hidden = expert_hidden(
                place_ref, in_ref[span, :], up_ref, router_ref, other_ref[span, :]
            )
            margin_ref[span, :] = margin
            pre_ref[span, :] = pre_act
            hidden_ref[span, :] = hidden
            out = sigmoid(margin) * dot(hidden, down.ready()[...])
            chunk_refs[r][...] = out.astype(BF16)

    outs = kernel_call(
        body,
        [like(per, model)] * n_heads
        + [
            like(slots, hidden_width, dtype=F32),
            like(slots, hidden_width),
            like(slots, 1, dtype=F32),
        ],
        [place, arrived, up, down, router, other],
        flops=4 * slots * model * hidden_width,
    )
    return outs[:n_heads], outs[n_heads:]


def experts_out(place, hidden, margin, down, n_heads, after):
    slots, model = hidden.shape[0], down.shape[1]
    per = slots // n_heads

    def body(place_ref, hidden_ref, margin_ref, down, *chunk_refs):
        down_ref = down.ready()
        for r in range(n_heads):
            span = pl.ds(pl.multiple_of((place_ref[1] ^ r) * per, per), per)
            out = sigmoid(margin_ref[span, :]) * dot(hidden_ref[span, :], down_ref[...])
            chunk_refs[r][...] = out.astype(BF16)

    return kernel_call(
        body,
        [like(per, model)] * n_heads,
        [place, hidden, margin, down],
        flops=2 * slots * model * hidden.shape[1],
        after=after,
    )


def experts_back(place, dout_rows, kept, arrived, up, down, router, other, n_heads, after=()):
    slots, model = dout_rows.shape
    per, hidden_width = slots // n_heads, up.shape[1]
    taken = [arrived] if kept is None else list(kept)

    def body(place_ref, dout_ref, *refs):
        kept_refs, refs = refs[: len(taken)], refs[len(taken) :]
        up, down, router_ref, other_ref = refs[:4]
        chunk_refs, refs = refs[4 : 4 + n_heads], refs[4 + n_heads :]
        dpre_ref, dslots_ref, dlogits_ref = refs[:3]
        up_ref, down_ref = up.ready(), down.ready()
        for r in range(n_heads):
            span = pl.ds(pl.multiple_of((place_ref[1] ^ r) * per, per), per)
            if kept is None:
                margin, v, hidden = expert_hidden(
                    place_ref, kept_refs[0][span, :], up_ref, router_ref, other_ref[span, :]
                )
                refs[3][span, :] = hidden
                refs[4][span, :] = margin
            else:
                v, hidden, margin = (ref[span, :] for ref in kept_refs)
            dout = dout_ref[span, :]
            dhidden = dot_nt(dout, down_ref[...])
            gate = sigmoid(margin)
            dgate = jnp.sum(dhidden * hidden.astype(F32), axis=1, keepdims=True)
            inner, _ = gelu_parts(v)
            slope = 0.5 * (1.0 + inner) + 0.5 * v * (1.0 - inner * inner) * ROOT_2_PI * (
                1.0 + 3.0 * 0.044715 * v * v
            )
            dpre = (gate * dhidden * slope).astype(BF16)
            dpre_ref[span, :] = dpre
            dslots_ref[span, :] = (gate * dout.astype(F32)).astype(BF16)
            signs = route_signs(place_ref, other_ref[span, :])
            dlogits = (gate * sigmoid(-margin) * dgate * signs).astype(BF16)
            dlogits_ref[span, :] = dlogits
            chunk_refs[r][...] = (
                dot_nt(dpre, up_ref[...]) + dot_nt(dlogits, router_ref[...])
            ).astype(BF16)

    extra = [like(slots, hidden_width), like(slots, 1, dtype=F32)] if kept is None else []
    outs = kernel_call(
        body,
        [like(per, model)] * n_heads
        + [like(slots, hidden_width), like(slots, model), like(slots, LANES)]
        + extra,
        [place, dout_rows, *taken, up, down, router, other],
        flops=4 * slots * model * hidden_width,
        after=after,
    )
    return outs[:n_heads], outs[n_heads:]


def expert_grads(place, pairs, got=None, after=()):
    shapes = [(p[0].shape[1], p[1].shape[1]) for p in pairs]
    outs = [like(len(pairs), *shapes[0])] if got is None else [like(*x, dtype=F32) for x in shapes]
    picks = [a for pair in pairs for a in pair]

    def body(place_ref, *refs):
        held, refs = refs[: len(picks)], refs[len(picks) :]
        for i in range(len(pairs)):
            grad = dot_tn(held[2 * i].ready()[...], held[2 * i + 1].ready()[...])
            if got is None:
                refs[0][i] = grad.astype(BF16)
            else:
                refs[1 + i][...] = grad + refs[0][i].astype(F32)

    flops = sum(2 * p[0].shape[0] * p[0].shape[1] * p[1].shape[1] for p in pairs)
    args = [place, *picks] + ([] if got is None else [got])
    return kernel_call(body, outs, args, flops=flops, after=after, grant=WIDE_BYTES, mark=True)


def dense_grad(place, pairs, after=()):
    model = pairs[0][0].shape[1]
    widths = [b.shape[1] for _, b in pairs]
    width = sum(widths)

    def body(place_ref, *refs):
        at = 0
        for i, size in enumerate(widths):
            grad = dot_tn(refs[2 * i][...], refs[2 * i + 1][...])
            refs[-1][:, at : at + size] = grad.astype(BF16)
            at += size

    rows = pairs[0][0].shape[0]
    return kernel_call(
        body,
        [like(model, width)],
        [place, *(a for pair in pairs for a in pair)],
        flops=2 * rows * model * width,
        after=after,
        mark=True,
    )


def small_columns(rows_ref):
    rows = rows_ref[...]
    wide = jnp.concatenate([rows, jnp.zeros((LANES - rows.shape[0], rows.shape[1]), F32)])
    return wide.T


def joint_send(place, grad, smalls):
    model, width = grad.shape

    def body(place_ref, grad, one_ref, two_ref, out_ref):
        small = either(place_ref, small_columns(two_ref), small_columns(one_ref))
        out_ref[:, width:] = small.astype(BF16)
        out_ref[:, :width] = grad.ready()[...]

    return kernel_call(body, [like(model, width + LANES)], [place, grad, *smalls])[0]


def joint_sum(place, grad, smalls, got):
    model, width = grad.shape

    def body(place_ref, grad, one_ref, two_ref, got_ref, out_ref):
        small = either(place_ref, small_columns(one_ref), small_columns(two_ref))
        out_ref[:, width:] = (small + got_ref[:, width:].astype(F32)).astype(BF16)
        total = grad.ready()[...].astype(F32) + got_ref[:, :width].astype(F32)
        out_ref[:, :width] = total.astype(BF16)

    return kernel_call(body, [like(model, width + LANES)], [place, grad, *smalls, got])[0]


def joint_split(total, width, n_experts):
    share = total.shape[0]

    def body(total_ref, qkv_ref, out_ref, first_ref, second_ref, router_ref, bias_ref):
        for i, at in enumerate((0, 2, 3)):
            qkv_ref[i] = total_ref[:, at * width : (at + 1) * width].astype(F32)
        out_ref[...] = total_ref[:, width : 2 * width].astype(F32).T
        small = total_ref[:, 4 * width :].astype(F32)
        router_ref[...] = small[:, 2 : 2 + n_experts]
        rows = small.T
        first_ref[...] = rows[0:1]
        second_ref[...] = rows[1:2]
        bias_ref[...] = rows[2 + n_experts : 3 + n_experts]

    shapes = [(3, share, width), (width, share)] + [(1, share)] * 2 + [(share, n_experts), (1, share)]
    return kernel_call(body, [like(*shape, dtype=F32) for shape in shapes], [total])


def join_quarter(pieces, after):
    def body(*refs):
        rows = [ref[...].astype(F32) for ref in refs[:-1]]
        refs[-1][...] = jnp.concatenate(rows).astype(BF16)

    per, model = pieces[0].shape
    return kernel_call(body, [like(per * len(pieces), model)], pieces, after=after)[0]


def router_grads(place, pairs, n_experts, after):
    model = pairs[0][1].shape[1]

    def body(place_ref, *refs):
        for layer in range(2):
            grad = dot_tn(refs[2 * layer][...], refs[2 * layer + 1][...])
            refs[-1][layer * n_experts : (layer + 1) * n_experts, :] = grad[:n_experts]

    args = [place, *(a for pair in pairs for a in pair)]
    return kernel_call(body, [like(2 * n_experts, model, dtype=F32)], args, after=after)[0]


def small_rows(place, layer, dgain_first, dgain_second, router_parts, lanes, n_experts, n_ctx):
    model, count = dgain_first.shape[1], lanes.shape[0]
    share, bias_share = model // n_ctx, count // n_ctx
    rows = -(-(3 + n_experts) // 8) * 8

    def body(place_ref, first_ref, second_ref, lanes_ref, *refs):
        out_ref = refs[-1]
        router = tree_sum([ref[...] for ref in refs[:-1]])
        out_ref[...] = jnp.zeros(out_ref.shape, F32)
        out_ref[0:1, :] = first_ref[...]
        out_ref[1:2, :] = second_ref[...]
        out_ref[2 : 2 + n_experts, :] = router[layer * n_experts : (layer + 1) * n_experts]
        sums = jnp.sum(lanes_ref[...], axis=1, keepdims=True)
        value = lax.broadcasted_iota(jnp.int32, (count, model), 0)
        lane = lax.broadcasted_iota(jnp.int32, (count, model), 1)
        target = value
        for c in range(1, n_ctx):
            target += jnp.where(value >= c * bias_share, share - bias_share, 0)
        row = jnp.sum(jnp.where(lane == target, sums, 0.0), axis=0, keepdims=True)
        out_ref[2 + n_experts : 3 + n_experts, :] = row

    return kernel_call(
        body,
        [like(rows, model, dtype=F32)],
        [place, dgain_first, dgain_second, lanes, *router_parts],
    )[0]


def assemble(place, dx, got_out, got_dx, out):
    def body(place_ref, one, two, both_ref):
        both_ref[0] = one.ready()[...]
        both_ref[1] = two.ready()[...]

    picks = [Pick(dx, got_out), Pick(got_dx, out)]
    return kernel_call(body, [like(2, *dx.shape, dtype=F32)], [place, *picks])[0]


def combine(middle, returned, tokens, after):
    rows, model = middle.shape
    share = returned[0].shape[0]

    def body(middle_ref, tokens_ref, *refs):
        total = 0.0
        for r, ref in enumerate(refs[: len(returned)]):
            total += dot(token_picks(tokens_ref, share, r * share), ref[...])
        refs[-1][...] = middle_ref[...] + total

    return kernel_call(
        body,
        [like(rows, model, dtype=F32)],
        [middle, tokens, *returned],
        flops=2 * rows * model * share * len(returned),
        after=after,
        mark=True,
    )


def combine_project(place, middle, returned, tokens, gain, qkv):
    rows, model = middle.shape
    width = qkv.shape[2]

    def body(place_ref, middle_ref, returned_ref, tokens_ref, gain_ref, w, passed_ref, *outs):
        picks = token_picks(tokens_ref, returned_ref.shape[0])
        passed = (middle_ref[...] + dot(picks, returned_ref[...])).astype(BF16)
        passed_ref[...] = passed
        project_rows(passed.astype(F32), gain_ref[...], w, *outs)

    return kernel_call(
        body,
        [like(rows, model), like(rows, model), like(rows, width), like(rows, 2 * width)],
        [place, middle, returned, tokens, gain, qkv],
        flops=2 * rows * model * returned.shape[0] + 6 * rows * model * width,
    )


def norm_back(values, gain, upstream):
    scale = lax.rsqrt(jnp.mean(values * values, axis=-1, keepdims=True) + EPSILON)
    unit = values * scale
    scaled = upstream * gain
    dvalues = scale * (scaled - unit * jnp.mean(unit * scaled, axis=-1, keepdims=True))
    return dvalues, jnp.sum(upstream * unit, axis=0, keepdims=True)


def middle_back(place, returned, tokens, middle, gain, dout, out_w, after=()):
    rows, model = middle.shape
    width = out_w.shape[0]

    def body(place_ref, returned_ref, tokens_ref, middle_ref, gain_ref, dout_ref, w, *refs):
        dmiddle_ref, datt_ref, dmix_ref, dgain_ref = refs
        picks = token_picks(tokens_ref, returned_ref.shape[0])
        dexpert_in = dot(picks, returned_ref[...])
        part, dgain = norm_back(middle_ref[...], gain_ref[...], dexpert_in)
        dgain_ref[...] = dgain
        dmiddle = dout_ref[...].astype(F32) + part
        dmiddle_ref[...] = dmiddle
        datt = dmiddle.astype(BF16)
        datt_ref[...] = datt
        dmix_ref[...] = dot_nt(datt, w.ready()[...]).astype(BF16)

    return kernel_call(
        body,
        [
            like(rows, model, dtype=F32),
            like(rows, model),
            like(rows, width),
            like(1, model, dtype=F32),
        ],
        [place, returned, tokens, middle, gain, dout, out_w],
        flops=2 * rows * model * (returned.shape[0] + width),
        after=after,
    )


def project_back(place, dq, dkv_parts, qkv, n_heads, after=()):
    rows, width = dq.shape
    model, n_parts = qkv.shape[1], len(dkv_parts)
    share = rows // n_heads

    def body(place_ref, dq_ref, *refs):
        part_refs, refs = refs[:n_parts], refs[n_parts:]
        w, dkv_ref = refs[:2]
        chunk_refs, total_ref = refs[2:-1], refs[-1]
        dkv = part_refs[0][...].astype(F32)
        for ref in part_refs[1:]:
            dkv += ref[...].astype(F32)
        dkv = dkv.astype(BF16)
        dkv_ref[...] = dkv
        w_ref = w.ready()
        total_ref[...] = (
            dot_nt(dq_ref[...], w_ref[0])
            + dot_nt(dkv[:, :width], w_ref[1])
            + dot_nt(dkv[:, width:], w_ref[2])
        )
        for r in range(n_heads):
            first = pl.multiple_of((place_ref[1] ^ r) * share, share)
            chunk_refs[r][...] = total_ref[pl.ds(first, share), :].astype(BF16)

    outs = kernel_call(
        body,
        [like(rows, 2 * width)] + [like(share, model)] * n_heads,
        [place, dq, *dkv_parts, qkv],
        [pltpu.VMEM((rows, model), F32)],
        flops=6 * rows * model * width,
        after=after,
    )
    return outs[0], outs[1:]


def tree_sum(values):
    while len(values) > 1:
        values = [values[i] + values[i + 1] for i in range(0, len(values), 2)]
    return values[0]


def share_sum(parts):
    def body(*refs):
        refs[-1][...] = tree_sum([ref[...].astype(F32) for ref in refs[:-1]]).astype(BF16)

    return kernel_call(body, [like(*parts[0].shape)], parts)[0]


def input_back(place, dnormed_parts, x, gain, dmiddle, tokens=None, n_ctx=0, per=0, after=()):
    rows, model = x.shape
    n_heads, share = len(dnormed_parts), dnormed_parts[0].shape[0]
    given = [x, gain, dmiddle] + ([] if tokens is None else [tokens])

    def body(place_ref, *refs):
        part_refs, refs = refs[:n_heads], refs[n_heads:]
        x_ref, gain_ref, dmiddle_ref = refs[:3]
        (dx_ref, dgain_ref), chunk_refs = refs[len(given) :][:2], refs[len(given) + 2 : -1]
        dnormed_ref = refs[-1]
        for r in range(n_heads):
            first = pl.multiple_of((place_ref[1] ^ r) * share, share)
            dnormed_ref[pl.ds(first, share), :] = part_refs[r][...].astype(F32)
        part, dgain = norm_back(x_ref[...].astype(F32), gain_ref[...], dnormed_ref[...])
        dgain_ref[...] = dgain
        dx = (dmiddle_ref[...] + part).astype(dx_ref.dtype)
        dx_ref[...] = dx
        if tokens is not None:
            dispatch_into(dx, place_ref, refs[3], chunk_refs)

    outs = kernel_call(
        body,
        [like(rows, model, dtype=F32 if tokens is None else BF16), like(1, model, dtype=F32)]
        + [like(per, model)] * n_ctx,
        [place, *dnormed_parts, *given],
        [pltpu.VMEM((rows, model), F32)],
        after=after,
    )
    return outs[0], outs[1], outs[2:]


def bucket_of(distance):
    exact_span = BUCKETS // 2
    result = jnp.minimum(distance, exact_span)
    for rank in range(1, BUCKETS - exact_span):
        edge = int(
            math.ceil(exact_span * (REACH / exact_span) ** (rank / (BUCKETS - exact_span)))
        )
        result = result + (distance >= edge).astype(jnp.int32)
    return result


def tile_buckets(half):
    row = lax.broadcasted_iota(jnp.int32, (half, half), 0)
    col = lax.broadcasted_iota(jnp.int32, (half, half), 1)
    same = jnp.where(row >= col, bucket_of(jnp.maximum(row - col, 0)), -1)
    return [same, bucket_of(half + row - col), bucket_of(2 * half + row - col)]


def bias_table(place, own, other, layer, half, after):
    heads, strip = own.shape[1], 8

    def body(place_ref, own_ref, other_ref, *refs):
        out_ref = refs[-1]

        def bias(bucket, head):
            return jnp.where(place_ref[2] == layer, own_ref[bucket, head], other_ref[bucket, head])

        values = [[bias(bucket, head) for head in range(heads)] for bucket in range(BUCKETS)]
        same, near, _ = tile_buckets(half)
        for head in range(heads):
            out_ref[head, 0] = jnp.full((half, half), NEGATIVE, F32)
            out_ref[head, 3] = jnp.full((half, half), values[-1][head], F32)
        for at in range(0, half, strip):
            for kind, held in ((1, same), (2, near)):
                held = held[at : at + strip]
                rows = [jnp.full((strip, half), NEGATIVE, F32) for _ in range(heads)]
                for bucket in range(BUCKETS):
                    hit = held == bucket
                    rows = [
                        jnp.where(hit, values[bucket][head], rows[head]) for head in range(heads)
                    ]
                for head in range(heads):
                    out_ref[head, kind, at : at + strip] = rows[head]

    return pl.pallas_call(
        body,
        out_shape=like(heads, 4, half, half, dtype=F32),
        in_specs=[pl.BlockSpec(memory_space=pltpu.SMEM)] * 3
        + [pl.BlockSpec(memory_space=pl.ANY)] * len(after),
        out_specs=pl.BlockSpec(memory_space=pltpu.VMEM),
        compiler_params=pltpu.CompilerParams(vmem_limit_bytes=2 * SPARE_BYTES),
    )(place, own, other, *after)


def small_weights(place, gains, routers, after):
    model, n_experts = routers[0].shape

    def body(place_ref, *refs):
        ins, outs = refs[:6], refs[-6:]
        for kind in range(2):
            own, other = (ref[...].astype(F32) for ref in ins[2 * kind : 2 * kind + 2])
            outs[2 * kind][...] = either(place_ref, own, other)
            outs[2 * kind + 1][...] = either(place_ref, other, own)
        own, other = (ref[...].astype(F32) for ref in ins[4:6])
        for out_ref, value in zip(
            outs[4:], (either(place_ref, own, other), either(place_ref, other, own))
        ):
            out_ref[...] = jnp.zeros(out_ref.shape, BF16)
            out_ref[:, :n_experts] = value.astype(BF16)

    args = [place, *gains[0], *gains[1], *routers]
    outs = kernel_call(
        body,
        [like(1, model, dtype=F32)] * 4 + [like(model, LANES)] * 2,
        args,
        after=after,
    )
    return outs[0:2], outs[2:4], outs[4:6]


def layer_row(place_ref, own, other, layer, k):
    rows = own.shape[1]
    row = jnp.where(place_ref[2] == layer, own[k : k + 1], other[k : k + 1])
    eye = lax.broadcasted_iota(jnp.int32, (rows, rows), 0) == lax.broadcasted_iota(
        jnp.int32, (rows, rows), 1
    )
    return jnp.sum(jnp.where(eye, row, 0).astype(F32), axis=1, keepdims=True).astype(jnp.int32)


def earlier(rows):
    row = lax.broadcasted_iota(jnp.int32, (rows, rows), 0)
    col = lax.broadcasted_iota(jnp.int32, (rows, rows), 1)
    return jnp.where(row > col, 1.0, 0.0).astype(BF16)


def quarter_of(rank, per, n_heads):
    return sum([(rank >= h * per).astype(jnp.int32) for h in range(1, n_heads)])


def token_slots(place, own, other, n_experts, per, n_heads, after):
    rows = own.shape[2]

    def body(place_ref, own_ref, other_ref, *refs):
        *outs, pair_ref = refs[-4:]
        pair_ref[0] = own_ref[...]
        pair_ref[1] = other_ref[...]
        own, other = own_ref[place_ref[2]], other_ref[place_ref[2]]
        for layer in range(2):
            choices = [layer_row(place_ref, own, other, layer, k) for k in range(2)]
            lane = lax.broadcasted_iota(jnp.int32, (rows, LANES), 1)
            hots = [jnp.where(lane == choice, 1.0, 0.0) for choice in choices]
            ranks = dot(earlier(rows), (hots[0] + hots[1]).astype(BF16))
            for k in range(2):
                rank = jnp.sum(ranks * hots[k], axis=1, keepdims=True).astype(jnp.int32)
                quarter = quarter_of(rank, per, n_heads)
                inner = (choices[k] ^ place_ref[0]) * per + rank - quarter * per
                outs[layer][:, k : k + 1] = quarter * (n_experts * per) + inner
                if layer == 1:
                    outs[2][:, k : k + 1] = (quarter ^ place_ref[1]) * (n_experts * per) + inner

    return kernel_call(
        body,
        [like(rows, 2, dtype=jnp.int32)] * 3 + [like(2, *own.shape, dtype=jnp.int32)],
        [place, own, other],
        after=after,
    )


def other_experts(place, pairs, per, n_heads):
    n_ctx, rows = len(pairs), pairs[0].shape[3]

    def body(place_ref, *refs):
        lane = lax.broadcasted_iota(jnp.int32, (rows, LANES), 1)
        slot = lax.broadcasted_iota(jnp.int32, (rows, n_heads * per), 1)
        found, heres = [], jnp.zeros((rows, LANES), F32)
        for layer in range(2):
            for r in range(n_ctx):
                pair = [refs[r][i, place_ref[2]] for i in range(2)]
                one, two = (layer_row(place_ref, *pair, layer, k) for k in range(2))
                here = (one == place_ref[0]) | (two == place_ref[0])
                other = jnp.where(one == place_ref[0], two, one).astype(F32)
                heres += jnp.where(here & (lane == layer * n_ctx + r), 1.0, 0.0)
                found.append((here, other))
        ranks = dot(earlier(rows), heres.astype(BF16)).astype(jnp.int32)
        for number, (here, other) in enumerate(found):
            layer, r = number // n_ctx, number % n_ctx
            picks = jnp.where(here & (slot == ranks[:, number : number + 1]), 1.0, 0.0)
            other = jnp.broadcast_to(other, (rows, LANES)).astype(BF16)
            column = dot_tn(picks.astype(BF16), other)[:, 0:1].astype(jnp.int32)
            for h in range(n_heads):
                at = (h * n_ctx + r) * per
                refs[n_ctx + layer][at : at + per, :] = column[h * per : (h + 1) * per]

    return kernel_call(
        body, [like(n_heads * n_ctx * per, 1, dtype=jnp.int32)] * 2, [place, *pairs]
    )


def table_back(dtable, after=()):
    heads, half = dtable.shape[0], dtable.shape[3]

    def body(dtable_ref, *refs):
        out_ref, buckets = refs[-1], tile_buckets(half)
        for bucket in range(BUCKETS):
            hits = [held == bucket for held in buckets]
            for head in range(heads):
                kept = jnp.zeros((half, half), F32)
                for tile, hit in enumerate(hits):
                    kept += jnp.where(hit, dtable_ref[head, 1 + tile], 0.0)
                at = bucket * heads + head
                out_ref[at : at + 1, :] = jnp.sum(kept, axis=0, keepdims=True)

    return kernel_call(
        body, [like(BUCKETS * heads, half, dtype=F32)], [dtable], after=after
    )[0]


def heads_sum(chunks, n_ctx, after=()):
    parts = exchange(chunks, "heads")
    rows, model = parts[0].shape
    per = rows // n_ctx

    def body(*refs):
        total = tree_sum([ref[...].astype(F32) for ref in refs[: len(parts)]])
        for r, out_ref in enumerate(refs[len(parts) :]):
            out_ref[...] = total[r * per : (r + 1) * per].astype(BF16)

    return kernel_call(body, [like(per, model)] * n_ctx, parts, after=after)


def return_rows(chunks, n_ctx):
    back = exchange(heads_sum(chunks, n_ctx), "ctx")
    return gather_rows(jnp.concatenate(back, axis=0), "heads")


def send_rows(chunks):
    return gather_rows(jnp.concatenate(exchange(chunks, "ctx"), axis=0), "heads")


def body(
    boundary,
    norm_first,
    qkv_weight,
    position_bias,
    out_weight,
    norm_second,
    router,
    expert_up,
    expert_down,
    routes,
):
    section = lax.axis_index("section")
    ctx_index = lax.axis_index("ctx")
    heads_index = lax.axis_index("heads")
    n_ctx, n_heads = lax.axis_size("ctx"), lax.axis_size("heads")
    first = section == 0
    place = jnp.stack([ctx_index, heads_index, section]).astype(jnp.int32)
    rows, model = boundary.shape[2:]
    half = rows // 2
    n_experts, heads = router.shape[2], position_bias.shape[2]
    per = 5 * rows // (2 * n_experts) // n_heads

    def by_layer(own, other):
        return Pick(own, other), Pick(other, own)

    def with_other(own):
        return own, swap(own, "section")

    qkv = by_layer(*with_other(qkv_weight[0]))
    given = swap(lax.dynamic_index_in_dim(boundary[0], 1 - section, 0, False), "section")
    gain_pairs = with_other(norm_first), with_other(norm_second)
    x0, cotangent, normed0, q0, kv0 = begin(
        place, boundary[0], given, *gain_pairs[0], qkv[0]
    )
    kv_all0 = gather_rows(kv0, "ctx")

    bias_pair = with_other(position_bias[0])
    bias0 = bias_table(place, *bias_pair, 0, half, [kv0])
    up = by_layer(*with_other(expert_up[0, 0]))
    down = by_layer(*with_other(expert_down[0, 0]))
    width = out_weight.shape[1]
    out_gathered = gather_rows(jnp.concatenate(with_other(out_weight[0]), axis=0), "heads")
    out_full = [Rows(out_gathered, layer, width) for layer in range(2)]
    out_own = [Rows(out_gathered, layer, width, own=True) for layer in range(2)]
    mix0, lse0 = attend(place, q0, [kv_all0], bias0, n_ctx)
    gains_first, gains_second, routers = small_weights(
        place, gain_pairs, with_other(router[0]), [lse0]
    )
    *tokens, tokens_near, pair = token_slots(
        place, *with_other(routes[0].transpose(0, 2, 1)), n_experts, per, n_heads, [lse0]
    )
    pairs = exchange([pair] * n_ctx, "ctx")
    others = other_experts(place, pairs, per, n_heads)

    def before_experts(layer, x, mix):
        mixes = exchange([mix] * n_heads, "heads")
        middle, chunks = finish_attention(
            place, mixes, out_full[layer], x, gains_second[layer], tokens[layer], n_ctx, per
        )
        return middle, send_rows(chunks)

    def expert_weights(layer):
        return up[layer], down[layer], routers[layer], others[layer]

    middle0, arrived0 = before_experts(0, x0, mix0)
    chunks, kept0 = experts(place, arrived0, *expert_weights(0), n_heads)
    dout_chunks = dispatch_whole(place, cotangent, tokens[1], n_ctx, per, n_heads, [middle0])
    returned = return_rows(chunks, n_ctx)
    x1, normed1, q1, kv1 = combine_project(
        place, middle0, returned, tokens[0], gains_first[1], qkv[1]
    )

    kv_all1 = gather_rows(kv1, "ctx")
    bias1 = bias_table(place, *bias_pair, 1, half, [middle0])
    mix1, lse1 = attend(place, q1, [kv_all1], bias1, n_ctx)
    middle1, arrived1 = before_experts(1, x1, mix1)
    dout_rows1 = jnp.stack(exchange(dout_chunks, "ctx"))
    dout_rows1 = dout_rows1.reshape(n_ctx, n_heads, per, model).transpose(1, 0, 2, 3)
    dout_rows1 = dout_rows1.reshape(-1, model)
    chunks, (dpre1, dslots1, dlogits1, hidden1, margin1) = experts_back(
        place, dout_rows1, None, arrived1, *expert_weights(1), n_heads
    )
    dmiddle1, datt1, dmix1, dgain_second1 = middle_back(
        place, return_rows(chunks, n_ctx), tokens[1], middle1, gains_second[1], cotangent, out_own[1]
    )
    dq1, dtable1, dkv1 = attend_back(place, q1, [kv_all1], bias1, lse1, dmix1, n_ctx)
    dkv_parts1 = exchange(dkv1, "ctx")
    out_total = heads_sum(
        experts_out(place, hidden1, margin1, down[1], n_heads, dkv_parts1[1:2]), n_ctx
    )
    dkv_sum1, chunks = project_back(place, dq1, dkv_parts1, qkv[1], n_heads)
    total1 = share_sum(exchange(chunks, "heads"))
    lanes1 = table_back(dtable1)
    dense1, made = dense_grad(place, [(normed1, dq1), (datt1, mix1), (normed1, dkv_sum1)])
    dx1, dgain_first1, sent = input_back(
        place,
        exchange([total1] * n_heads, "heads"),
        x1,
        gains_first[1],
        dmiddle1,
        tokens[0],
        n_ctx,
        per,
        [lanes1, made],
    )

    dout_rows0 = send_rows(sent)
    chunks, (dpre0, dslots0, dlogits0) = experts_back(
        place, dout_rows0, kept0, arrived0, *expert_weights(0), n_heads, out_total[:1]
    )
    lists = [(arrived0, arrived1), (dpre0, dpre1), (kept0[1], hidden1), (dslots0, dslots1)]
    mine, theirs = [Pick(a, b) for a, b in lists], [Pick(b, a) for a, b in lists]
    sends, sends_made = expert_grads(place, [theirs[:2], theirs[2:]])
    back = heads_sum(chunks, n_ctx, [sends_made])
    returned = gather_rows(jnp.concatenate(exchange(back, "ctx"), axis=0), "heads")
    router_part = router_grads(
        place, [(dlogits0, arrived0), (dlogits1, arrived1)], n_experts, back[:1]
    )
    router_parts = exchange([router_part] * n_heads, "heads")
    small1 = small_rows(
        place, 1, dgain_first1, dgain_second1, router_parts, lanes1, n_experts, n_ctx
    )
    dmiddle0, datt0, dmix0, dgain_second0 = middle_back(
        place,
        returned,
        tokens[0],
        middle0,
        gains_second[0],
        dx1,
        out_own[0],
        [small1],
    )
    dq0, dtable0, dkv0 = attend_back(place, q0, [kv_all0], bias0, lse0, dmix0, n_ctx)
    lanes0 = table_back(dtable0)
    dkv_sum0, chunks = project_back(place, dq0, exchange(dkv0, "ctx"), qkv[0], n_heads)
    parts = exchange(chunks, "heads")
    total0 = share_sum(parts)
    dense0, made = dense_grad(
        place, [(normed0, dq0), (datt0, mix0), (normed0, dkv_sum0)], parts[1:2]
    )
    near = exchange([total0] * n_heads, "heads")
    dx0, dgain_first0, _ = input_back(
        place,
        near,
        x0,
        gains_first[0],
        dmiddle0,
        after=[made, lanes0],
    )

    got_dx = one_way(dx0, 1)
    small0 = small_rows(
        place, 0, dgain_first0, dgain_second0, router_parts, lanes0, n_experts, n_ctx
    )
    smalls = [small0, small1]
    got = swap(joint_send(place, Pick(dense1, dense0), smalls), "section")
    joint = joint_sum(place, Pick(dense0, dense1), smalls, got)
    joint = lax.psum_scatter(joint, "ctx", scatter_dimension=0, tiled=True)
    out_back = exchange(out_total, "ctx")
    quarter = join_quarter(out_back, ())
    grad_up, grad_down, made = expert_grads(
        place, [mine[:2], mine[2:]], swap(sends, "section"), after=[dgain_first0]
    )
    out, _ = combine(middle1, exchange([quarter] * n_heads, "heads"), tokens_near, [made])
    grad_qkv, grad_out, grad_first, grad_second, grad_router, grad_bias = joint_split(
        joint, width, n_experts
    )
    bias_share = BUCKETS // n_ctx
    grad_bias = grad_bias[:, : bias_share * heads].reshape(1, bias_share, heads)
    boundary_out = assemble(place, dx0, one_way(out, 0), got_dx, out)
    return (
        boundary_out[None],
        grad_first,
        grad_qkv[None],
        grad_bias,
        grad_out[None],
        grad_second,
        grad_router[None],
        grad_up[None, None],
        grad_down[None, None],
    )


def solution(mesh):
    placed = (
        P("section", None, "ctx", None),
        P("section", None),
        P("section", None, None, "heads"),
        P("section", None, "heads"),
        P("section", "heads", None),
        P("section", None),
        P("section", None, None),
        P("section", "ctx", None, "heads"),
        P("section", "ctx", "heads", None),
        P("section", None, "ctx", None),
    )
    return jax.shard_map(
        body,
        mesh=mesh,
        in_specs=placed,
        out_specs=(
            P("section", None, "ctx", None),
            P("section", "ctx"),
            P("section", None, "ctx", "heads"),
            P("section", "ctx", "heads"),
            P("section", "heads", "ctx"),
            P("section", "ctx"),
            P("section", "ctx", None),
            P("section", "ctx", None, "heads"),
            P("section", "ctx", "heads", None),
        ),
        check_vma=False,
    )
```

```python
import math

import jax
import jax.numpy as jnp
from jax import lax
from jax.experimental import pallas as pl
from jax.experimental.pallas import tpu as pltpu
from jax.sharding import PartitionSpec as P

HD = 64
BUCKETS = 32
REACH = 128
EPSILON = 1e-06
NEGATIVE = -1e30
F32 = jnp.float32
BF16 = jnp.bfloat16
LANES = 128
SPARE_BYTES = 6 * 1024 * 1024
WIDE_BYTES = 48 * 1024 * 1024
ROOT_2_PI = math.sqrt(2.0 / math.pi)


class Pick:
    def __init__(self, first, second):
        self.arrays, self.shape = (first, second), first.shape
        self.dtype, self.ndim = first.dtype, first.ndim


class Rows:
    def __init__(self, array, layer, width, own=False):
        n_heads = array.shape[0] // (2 * width)
        self.array, self.layer, self.width, self.own = array, layer, width, own
        self.shape = (width if own else n_heads * width,) + array.shape[1:]
        self.dtype, self.ndim, self.n_heads = array.dtype, array.ndim, n_heads


class Held:
    def __init__(self, buffer, wait):
        self.buffer, self.wait, self.here = buffer, wait, False

    def ready(self):
        if not self.here:
            self.wait()
        self.here = True
        return self.buffer


def padded_bytes(array):
    *lead, rows, lanes = (1, 1) + tuple(array.shape)
    return math.prod(lead) * (-(-rows // 16) * 16) * (-(-lanes // LANES) * LANES) * jnp.dtype(array.dtype).itemsize


def kernel_call(body, outs, args, scratch=(), flops=0, after=(), grant=0, mark=False):
    if mark:
        outs = list(outs) + [like(8, LANES, dtype=F32)]
    picks = [a for a in args if isinstance(a, (Pick, Rows))]
    operands, in_specs = [], []
    for a in args:
        if isinstance(a, (Pick, Rows)):
            arrays = a.arrays if isinstance(a, Pick) else (a.array,)
            operands += arrays
            in_specs += [pl.BlockSpec(memory_space=pltpu.HBM)] * len(arrays)
        else:
            scalar = a.ndim == 1 and a.dtype == jnp.int32
            operands.append(a)
            in_specs.append(pl.BlockSpec(memory_space=pltpu.SMEM if scalar else pltpu.VMEM))
    operands += after
    in_specs += [pl.BlockSpec(memory_space=pl.ANY)] * len(after)
    scratch = list(scratch) + [pltpu.VMEM(p.shape, p.dtype) for p in picks]
    if picks:
        scratch.append(pltpu.SemaphoreType.DMA((len(picks),)))
    n_out, n_own = len(outs), len(scratch) - len(picks) - (1 if picks else 0)

    def hold(a, sources, place_ref, buffer, sem):
        if isinstance(a, Pick):
            for section, src in enumerate(sources):

                @pl.when(place_ref[2] == section)
                def _(src=src):
                    pltpu.make_async_copy(src, buffer, sem).start()

            return Held(buffer, pltpu.make_async_copy(sources[0], buffer, sem).wait)
        copies = []
        for h in range(1 if a.own else a.n_heads):
            block = 2 * (place_ref[1] if a.own else h) + (place_ref[2] ^ a.layer)
            src = sources[0].at[pl.ds(pl.multiple_of(block * a.width, a.width), a.width)]
            dst = buffer.at[pl.ds(h * a.width, a.width)]
            copies.append(pltpu.make_async_copy(src, dst, sem))
            copies[-1].start()

        def wait():
            for copy in copies:
                copy.wait()

        return Held(buffer, wait)

    def wrapped(*refs):
        ins, rest = refs[: len(operands)], refs[len(operands) :]
        buffers = list(rest[n_out + n_own :])
        given, at, number = [], 0, 0
        for a in args:
            if not isinstance(a, (Pick, Rows)):
                given.append(ins[at])
                at += 1
                continue
            count = 2 if isinstance(a, Pick) else 1
            sem = buffers[-1].at[number]
            given.append(hold(a, ins[at : at + count], ins[0], buffers[number], sem))
            at, number = at + count, number + 1
        if mark:
            rest[n_out - 1][...] = jnp.zeros((8, LANES), F32)
            rest = rest[: n_out - 1] + rest[n_out:]
        body(*given, *rest[: n_out + n_own - mark])

    size = sum(math.prod(a.shape) * a.dtype.itemsize for a in list(args) + list(outs))
    held = sum(map(padded_bytes, list(args) + list(outs)))
    held += sum(padded_bytes(s) for s in scratch[:n_own])
    return pl.pallas_call(
        wrapped,
        out_shape=outs,
        in_specs=in_specs,
        out_specs=[pl.BlockSpec(memory_space=pltpu.VMEM)] * n_out,
        scratch_shapes=scratch,
        compiler_params=pltpu.CompilerParams(vmem_limit_bytes=max(grant, held + SPARE_BYTES)),
        cost_estimate=pl.CostEstimate(flops=flops, bytes_accessed=size, transcendentals=0),
    )(*operands)


def like(*shape, dtype=BF16):
    return jax.ShapeDtypeStruct(shape, dtype)


def dot(a, b, contract=((1,), (0,))):
    return lax.dot_general(a, b, (contract, ((), ())), preferred_element_type=F32)


def dot_nt(a, b):
    return dot(a, b, ((1,), (1,)))


def dot_tn(a, b):
    return dot(a, b, ((0,), (0,)))


def swap(array, axis, by=1):
    devices = lax.axis_size(axis)
    return lax.ppermute(array, axis, [(i, i ^ by) for i in range(devices)])


def one_way(array, source):
    return lax.ppermute(array, "section", [(source, 1 - source)])


def exchange(chunks, axis):
    return [chunks[0]] + [swap(chunks[r], axis, r) for r in range(1, len(chunks))]


def gather_rows(array, axis):
    return lax.all_gather(array, axis, axis=0, tiled=True)


def project_rows(x, gain, w, normed_ref, q_ref, kv_ref):
    width = q_ref.shape[1]
    scale = lax.rsqrt(jnp.mean(x * x, axis=-1, keepdims=True) + EPSILON)
    normed = (x * scale * gain).astype(BF16)
    normed_ref[...] = normed
    w_ref = w.ready()
    kv_ref[:, :width] = dot(normed, w_ref[1]).astype(BF16)
    kv_ref[:, width:] = dot(normed, w_ref[2]).astype(BF16)
    q_ref[...] = dot(normed, w_ref[0]).astype(BF16)


def either(place_ref, first, second):
    return jnp.where(place_ref[2] == 0, first, second)


def begin(place, own, given, gain_own, gain_other, qkv):
    _, rows, model = own.shape
    width = qkv.shape[2]

    def body(place_ref, own_ref, given_ref, gain_ref, other_ref, w, x_ref, cotangent_ref, *outs):
        x = either(place_ref, own_ref[0], given_ref[...])
        x_ref[...] = x
        cotangent_ref[...] = either(place_ref, given_ref[...], own_ref[1])
        gain = either(place_ref, gain_ref[...].astype(F32), other_ref[...].astype(F32))
        project_rows(x.astype(F32), gain, w, *outs)

    return kernel_call(
        body,
        [like(rows, model)] * 3 + [like(rows, width), like(rows, 2 * width)],
        [place, own, given, gain_own, gain_other, qkv],
        flops=6 * rows * model * width,
    )


def tile_pick(block, key_tile, mine, ordered, n_ctx):
    owner = key_tile // 2 if ordered else mine ^ (key_tile // 2)
    key_block = owner if key_tile % 2 == 0 else 2 * n_ctx - 1 - owner
    return jnp.clip(block - key_block, -1, 2) + 1


def query_parts(mine, half, n_ctx):
    return [
        (slice(0, half), mine),
        (slice(half, 2 * half), 2 * n_ctx - 1 - mine),
    ]


def attend(place, q, kv_parts, table, n_ctx):
    rows, width = q.shape
    half, heads, keys = rows // 2, width // HD, rows * n_ctx
    ordered, count = len(kv_parts) == 1, len(kv_parts)

    def body(place_ref, q_ref, *refs):
        kv_refs, (table_ref, mix_ref, lse_ref, scores_ref) = refs[:count], refs[count:]
        mine = place_ref[0]
        kv_ref = kv_refs[0]
        for head in range(heads):
            cols = slice(head * HD, (head + 1) * HD)
            key_rows = kv_ref[:, cols]
            value_rows = kv_ref[:, width + head * HD : width + (head + 1) * HD]
            for part, (span, block) in enumerate(query_parts(mine, half, n_ctx)):
                raw = dot_nt(q_ref[span, cols], key_rows)
                for key_tile in range(2 * n_ctx):
                    pick = tile_pick(block, key_tile, mine, ordered, n_ctx)
                    tile = slice(key_tile * half, (key_tile + 1) * half)
                    scores_ref[part, :, tile] = raw[:, tile] * 0.125 + table_ref[head, pick]
                scores = scores_ref[part]
                top = jnp.max(scores, axis=1, keepdims=True)
                mass = jnp.exp(scores - top)
                total = jnp.sum(mass, axis=1, keepdims=True)
                out = dot(mass.astype(BF16), value_rows) / total
                mix_ref[span, cols] = out.astype(BF16)
                lse_ref[span, head : head + 1] = top + jnp.log(total)

    return kernel_call(
        body,
        [like(rows, width), like(rows, heads, dtype=F32)],
        [place, q, *kv_parts, table],
        [pltpu.VMEM((2, half, keys), F32)],
        flops=4 * rows * keys * width,
    )


def attend_back(place, q, kv_parts, table, lse, dmix, n_ctx):
    rows, width = q.shape
    half, heads, keys = rows // 2, width // HD, rows * n_ctx
    ordered, count = len(kv_parts) == 1, len(kv_parts)

    def body(place_ref, q_ref, *refs):
        kv_refs, refs = refs[:count], refs[count:]
        table_ref, lse_ref, dmix_ref, dq_ref, dtable_ref = refs[:5]
        chunk_refs, (scores_ref, total_ref) = refs[5 : 5 + n_ctx], refs[5 + n_ctx :]
        mine = place_ref[0]
        kv_ref = kv_refs[0]
        dtable_ref[...] = jnp.zeros(dtable_ref.shape, F32)
        for head in range(heads):
            cols = slice(head * HD, (head + 1) * HD)
            value_cols = slice(width + head * HD, width + (head + 1) * HD)
            key_rows = kv_ref[:, cols]
            value_rows = kv_ref[:, value_cols]
            for part, (span, block) in enumerate(query_parts(mine, half, n_ctx)):
                q = q_ref[span, cols]
                dmix = dmix_ref[span, cols]
                raw = dot_nt(q, key_rows)
                for key_tile in range(2 * n_ctx):
                    pick = tile_pick(block, key_tile, mine, ordered, n_ctx)
                    tile = slice(key_tile * half, (key_tile + 1) * half)
                    scores_ref[part, :, tile] = raw[:, tile] * 0.125 + table_ref[head, pick]
                probs = jnp.exp(scores_ref[part] - lse_ref[span, head : head + 1])
                dprobs = dot_nt(dmix, value_rows)
                delta = jnp.sum(probs * dprobs, axis=1, keepdims=True)
                dscores = (probs * (dprobs - delta)).astype(BF16)
                dq_ref[span, cols] = (dot(dscores, key_rows) * 0.125).astype(BF16)
                dkeys = dot_tn(dscores, q) * 0.125
                dvalues = dot_tn(probs.astype(BF16), dmix)
                if part == 0:
                    total_ref[:, cols] = dkeys
                    total_ref[:, value_cols] = dvalues
                else:
                    total_ref[:, cols] += dkeys
                    total_ref[:, value_cols] += dvalues
                for key_tile in range(2 * n_ctx):
                    pick = tile_pick(block, key_tile, mine, ordered, n_ctx)
                    tile = dscores[:, key_tile * half : (key_tile + 1) * half]
                    dtable_ref[head, pick] += tile.astype(F32)
        for r in range(n_ctx):
            first = pl.multiple_of((mine ^ r if ordered else r) * rows, rows)
            chunk_refs[r][...] = total_ref[pl.ds(first, rows), :].astype(BF16)

    outs = kernel_call(
        body,
        [like(rows, width), like(*table.shape, dtype=F32)] + [like(rows, 2 * width)] * n_ctx,
        [place, q, *kv_parts, table, lse, dmix],
        [
            pltpu.VMEM((2, half, keys), F32),
            pltpu.VMEM((keys, 2 * width), F32),
        ],
        flops=10 * rows * keys * width,
    )
    return outs[0], outs[1], outs[2:]


def token_picks(tokens_ref, count, first=0):
    ids = first + lax.broadcasted_iota(jnp.int32, (tokens_ref.shape[0], count), 1)
    hit = (ids == tokens_ref[:, 0:1]) | (ids == tokens_ref[:, 1:2])
    return jnp.where(hit, 1.0, 0.0).astype(BF16)


def dispatch_into(rows, place_ref, tokens_ref, chunk_refs):
    per = chunk_refs[0].shape[0]
    first = place_ref[1] * (per * len(chunk_refs))
    for r, chunk_ref in enumerate(chunk_refs):
        picks = token_picks(tokens_ref, per, first + r * per)
        chunk_ref[...] = dot_tn(picks, rows).astype(BF16)


def dispatch_whole(place, rows, tokens, n_ctx, per, n_heads, after):
    count, model = rows.shape

    def body(place_ref, rows_ref, tokens_ref, *chunk_refs):
        lane = lax.broadcasted_iota(jnp.int32, (count, n_heads * per), 1)
        ids = lane
        for h in range(1, n_heads):
            ids += jnp.where(lane >= h * per, (n_ctx - 1) * per, 0)
        for r, chunk_ref in enumerate(chunk_refs):
            here = ids + r * per
            hit = (here == tokens_ref[:, 0:1]) | (here == tokens_ref[:, 1:2])
            picks = jnp.where(hit, 1.0, 0.0).astype(BF16)
            chunk_ref[...] = dot_tn(picks, rows_ref[...]).astype(BF16)

    return kernel_call(
        body, [like(n_heads * per, model)] * n_ctx, [place, rows, tokens], after=after
    )


def finish_attention(place, mixes, out_w, x, gain, tokens, n_ctx, per):
    rows, model = x.shape
    n_heads, width = len(mixes), mixes[0].shape[1]

    def body(place_ref, *refs):
        mix_refs, refs = refs[:n_heads], refs[n_heads:]
        w_ref, x_ref, gain_ref, tokens_ref, middle_ref = refs[:5]
        chunk_refs, mixed_ref = refs[5:-1], refs[-1]
        for r in range(n_heads):
            mixed_ref[place_ref[1] ^ r] = mix_refs[r][...]
        middle = x_ref[...].astype(F32)
        w_ref = w_ref.ready()
        attended = dot(mixed_ref[0], w_ref[:width, :])
        for h in range(1, n_heads):
            attended += dot(mixed_ref[h], w_ref[h * width : (h + 1) * width, :])
        middle = middle + attended
        middle_ref[...] = middle
        scale = lax.rsqrt(jnp.mean(middle * middle, axis=-1, keepdims=True) + EPSILON)
        expert_in = (middle * scale * gain_ref[...]).astype(BF16)
        dispatch_into(expert_in, place_ref, tokens_ref, chunk_refs)

    outs = kernel_call(
        body,
        [like(rows, model, dtype=F32)] + [like(per, model)] * n_ctx,
        [place, *mixes, out_w, x, gain, tokens],
        [pltpu.VMEM((n_heads, rows, width), BF16)],
        flops=2 * rows * model * model + 2 * rows * model * per * n_ctx,
    )
    return outs[0], outs[1:]


def gelu_parts(v):
    inner = jnp.tanh(ROOT_2_PI * (v + 0.044715 * v * v * v))
    return inner, 0.5 * v * (1.0 + inner)


def route_signs(place_ref, other):
    lane = lax.broadcasted_iota(jnp.int32, (other.shape[0], LANES), 1)
    return jnp.where(lane == place_ref[0], 1.0, 0.0) - jnp.where(lane == other, 1.0, 0.0)


def expert_hidden(place_ref, rows, up_ref, router_ref, other):
    logits = dot(rows, router_ref[...])
    margin = jnp.sum(logits * route_signs(place_ref, other), axis=1, keepdims=True)
    pre_act = dot(rows, up_ref[...])
    return margin, pre_act, gelu_parts(pre_act)[1].astype(BF16)


def sigmoid(v):
    return 1.0 / (1.0 + jnp.exp(-v))


def experts(place, arrived, up, down, router, other, n_heads):
    slots, model = arrived.shape
    per, hidden_width = slots // n_heads, up.shape[1]

    def body(place_ref, in_ref, up, down, router_ref, other_ref, *refs):
        chunk_refs, (pre_ref, hidden_ref, margin_ref) = refs[:n_heads], refs[n_heads:]
        up_ref = up.ready()
        for r in range(n_heads):
            span = pl.ds(pl.multiple_of((place_ref[1] ^ r) * per, per), per)
            margin, pre_act, hidden = expert_hidden(
                place_ref, in_ref[span, :], up_ref, router_ref, other_ref[span, :]
            )
            margin_ref[span, :] = margin
            pre_ref[span, :] = pre_act
            hidden_ref[span, :] = hidden
            out = sigmoid(margin) * dot(hidden, down.ready()[...])
            chunk_refs[r][...] = out.astype(BF16)

    outs = kernel_call(
        body,
        [like(per, model)] * n_heads
        + [
            like(slots, hidden_width, dtype=F32),
            like(slots, hidden_width),
            like(slots, 1, dtype=F32),
        ],
        [place, arrived, up, down, router, other],
        flops=4 * slots * model * hidden_width,
    )
    return outs[:n_heads], outs[n_heads:]


def experts_out(place, hidden, margin, down, n_heads, after):
    slots, model = hidden.shape[0], down.shape[1]
    per = slots // n_heads

    def body(place_ref, hidden_ref, margin_ref, down, *chunk_refs):
        down_ref = down.ready()
        for r in range(n_heads):
            span = pl.ds(pl.multiple_of((place_ref[1] ^ r) * per, per), per)
            out = sigmoid(margin_ref[span, :]) * dot(hidden_ref[span, :], down_ref[...])
            chunk_refs[r][...] = out.astype(BF16)

    return kernel_call(
        body,
        [like(per, model)] * n_heads,
        [place, hidden, margin, down],
        flops=2 * slots * model * hidden.shape[1],
        after=after,
    )


def experts_back(place, dout_rows, kept, arrived, up, down, router, other, n_heads, after=()):
    slots, model = dout_rows.shape
    per, hidden_width = slots // n_heads, up.shape[1]
    taken = [arrived] if kept is None else list(kept)

    def body(place_ref, dout_ref, *refs):
        kept_refs, refs = refs[: len(taken)], refs[len(taken) :]
        up, down, router_ref, other_ref = refs[:4]
        chunk_refs, refs = refs[4 : 4 + n_heads], refs[4 + n_heads :]
        dpre_ref, dslots_ref, dlogits_ref = refs[:3]
        up_ref, down_ref = up.ready(), down.ready()
        for r in range(n_heads):
            span = pl.ds(pl.multiple_of((place_ref[1] ^ r) * per, per), per)
            if kept is None:
                margin, v, hidden = expert_hidden(
                    place_ref, kept_refs[0][span, :], up_ref, router_ref, other_ref[span, :]
                )
                refs[3][span, :] = hidden
                refs[4][span, :] = margin
            else:
                v, hidden, margin = (ref[span, :] for ref in kept_refs)
            dout = dout_ref[span, :]
            dhidden = dot_nt(dout, down_ref[...])
            gate = sigmoid(margin)
            dgate = jnp.sum(dhidden * hidden.astype(F32), axis=1, keepdims=True)
            inner, _ = gelu_parts(v)
            slope = 0.5 * (1.0 + inner) + 0.5 * v * (1.0 - inner * inner) * ROOT_2_PI * (
                1.0 + 3.0 * 0.044715 * v * v
            )
            dpre = (gate * dhidden * slope).astype(BF16)
            dpre_ref[span, :] = dpre
            dslots_ref[span, :] = (gate * dout.astype(F32)).astype(BF16)
            signs = route_signs(place_ref, other_ref[span, :])
            dlogits = (gate * sigmoid(-margin) * dgate * signs).astype(BF16)
            dlogits_ref[span, :] = dlogits
            chunk_refs[r][...] = (
                dot_nt(dpre, up_ref[...]) + dot_nt(dlogits, router_ref[...])
            ).astype(BF16)

    extra = [like(slots, hidden_width), like(slots, 1, dtype=F32)] if kept is None else []
    outs = kernel_call(
        body,
        [like(per, model)] * n_heads
        + [like(slots, hidden_width), like(slots, model), like(slots, LANES)]
        + extra,
        [place, dout_rows, *taken, up, down, router, other],
        flops=4 * slots * model * hidden_width,
        after=after,
    )
    return outs[:n_heads], outs[n_heads:]


def expert_grads(place, pairs, got=None, after=()):
    shapes = [(p[0].shape[1], p[1].shape[1]) for p in pairs]
    outs = [like(len(pairs), *shapes[0])] if got is None else [like(*x, dtype=F32) for x in shapes]
    picks = [a for pair in pairs for a in pair]

    def body(place_ref, *refs):
        held, refs = refs[: len(picks)], refs[len(picks) :]
        for i in range(len(pairs)):
            grad = dot_tn(held[2 * i].ready()[...], held[2 * i + 1].ready()[...])
            if got is None:
                refs[0][i] = grad.astype(BF16)
            else:
                refs[1 + i][...] = grad + refs[0][i].astype(F32)

    flops = sum(2 * p[0].shape[0] * p[0].shape[1] * p[1].shape[1] for p in pairs)
    args = [place, *picks] + ([] if got is None else [got])
    return kernel_call(body, outs, args, flops=flops, after=after, grant=WIDE_BYTES, mark=True)


def dense_grad(place, pairs, after=()):
    model = pairs[0][0].shape[1]
    widths = [b.shape[1] for _, b in pairs]
    width = sum(widths)

    def body(place_ref, *refs):
        at = 0
        for i, size in enumerate(widths):
            grad = dot_tn(refs[2 * i][...], refs[2 * i + 1][...])
            refs[-1][:, at : at + size] = grad.astype(BF16)
            at += size

    rows = pairs[0][0].shape[0]
    return kernel_call(
        body,
        [like(model, width)],
        [place, *(a for pair in pairs for a in pair)],
        flops=2 * rows * model * width,
        after=after,
        mark=True,
    )


def small_columns(rows_ref):
    rows = rows_ref[...]
    wide = jnp.concatenate([rows, jnp.zeros((LANES - rows.shape[0], rows.shape[1]), F32)])
    return wide.T


def joint_send(place, grad, smalls):
    model, width = grad.shape

    def body(place_ref, grad, one_ref, two_ref, out_ref):
        small = either(place_ref, small_columns(two_ref), small_columns(one_ref))
        out_ref[:, width:] = small.astype(BF16)
        out_ref[:, :width] = grad.ready()[...]

    return kernel_call(body, [like(model, width + LANES)], [place, grad, *smalls])[0]


def joint_sum(place, grad, smalls, got):
    model, width = grad.shape

    def body(place_ref, grad, one_ref, two_ref, got_ref, out_ref):
        small = either(place_ref, small_columns(one_ref), small_columns(two_ref))
        out_ref[:, width:] = (small + got_ref[:, width:].astype(F32)).astype(BF16)
        total = grad.ready()[...].astype(F32) + got_ref[:, :width].astype(F32)
        out_ref[:, :width] = total.astype(BF16)

    return kernel_call(body, [like(model, width + LANES)], [place, grad, *smalls, got])[0]


def joint_split(total, width, n_experts, bias_shape):
    share = total.shape[0]

    def body(total_ref, qkv_ref, out_ref, first_ref, second_ref, router_ref, bias_ref):
        for i, at in enumerate((0, 2, 3)):
            qkv_ref[i] = total_ref[:, at * width : (at + 1) * width].astype(F32)
        out_ref[...] = total_ref[:, width : 2 * width].astype(F32).T
        small = total_ref[:, 4 * width :].astype(F32)
        rows = small.T
        first_ref[...] = rows[0:1]
        second_ref[...] = rows[1:2]
        router_ref[...] = rows[2 : 2 + n_experts]
        column = small[:, 2 + n_experts : 3 + n_experts]
        held = lax.broadcasted_iota(jnp.int32, (share, bias_shape[1]), 0)
        bucket = lax.broadcasted_iota(jnp.int32, (share, bias_shape[1]), 1)
        for head in range(bias_shape[0]):
            hit = held == bucket * bias_shape[0] + head
            picked = jnp.sum(jnp.where(hit, column, 0.0), axis=0, keepdims=True)
            bias_ref[head : head + 1, :] = picked

    shapes = [(3, share, width), (width, share)] + [(1, share)] * 2
    shapes += [(n_experts, share), bias_shape]
    return kernel_call(body, [like(*shape, dtype=F32) for shape in shapes], [total])


def joined(pair, after):
    rows, model = pair[0].shape

    def body(one_ref, two_ref, out_ref):
        out_ref[:rows, :] = one_ref[...]
        out_ref[rows:, :] = two_ref[...]

    return kernel_call(body, [like(2 * rows, model)], list(pair), after=after)[0]


def join_quarter(pieces, after):
    def body(*refs):
        rows = [ref[...].astype(F32) for ref in refs[:-1]]
        refs[-1][...] = jnp.concatenate(rows).astype(BF16)

    per, model = pieces[0].shape
    return kernel_call(body, [like(per * len(pieces), model)], pieces, after=after)[0]


def router_grads(place, pairs, n_experts, after):
    model = pairs[0][1].shape[1]

    def body(place_ref, *refs):
        for layer in range(2):
            grad = dot_tn(refs[2 * layer][...], refs[2 * layer + 1][...])
            refs[-1][layer * n_experts : (layer + 1) * n_experts, :] = grad[:n_experts]

    args = [place, *(a for pair in pairs for a in pair)]
    return kernel_call(body, [like(2 * n_experts, model, dtype=F32)], args, after=after)[0]


def small_rows(place, layer, dgain_first, dgain_second, router_parts, lanes, n_experts, n_ctx):
    model, count = dgain_first.shape[1], lanes.shape[0]
    share, bias_share = model // n_ctx, count // n_ctx
    rows = -(-(3 + n_experts) // 8) * 8

    def body(place_ref, first_ref, second_ref, lanes_ref, *refs):
        out_ref = refs[-1]
        router = tree_sum([ref[...] for ref in refs[:-1]])
        out_ref[...] = jnp.zeros(out_ref.shape, F32)
        out_ref[0:1, :] = first_ref[...]
        out_ref[1:2, :] = second_ref[...]
        out_ref[2 : 2 + n_experts, :] = router[layer * n_experts : (layer + 1) * n_experts]
        sums = jnp.sum(lanes_ref[...], axis=1, keepdims=True)
        value = lax.broadcasted_iota(jnp.int32, (count, model), 0)
        lane = lax.broadcasted_iota(jnp.int32, (count, model), 1)
        target = value
        for c in range(1, n_ctx):
            target += jnp.where(value >= c * bias_share, share - bias_share, 0)
        row = jnp.sum(jnp.where(lane == target, sums, 0.0), axis=0, keepdims=True)
        out_ref[2 + n_experts : 3 + n_experts, :] = row

    return kernel_call(
        body,
        [like(rows, model, dtype=F32)],
        [place, dgain_first, dgain_second, lanes, *router_parts],
    )[0]


def assemble(place, dx, got_out, got_dx, out):
    def body(place_ref, one, two, both_ref):
        both_ref[0] = one.ready()[...]
        both_ref[1] = two.ready()[...]

    picks = [Pick(dx, got_out), Pick(got_dx, out)]
    return kernel_call(body, [like(2, *dx.shape, dtype=F32)], [place, *picks])[0]


def combine(middle, returned, tokens, after):
    rows, model = middle.shape
    share = returned[0].shape[0]

    def body(middle_ref, tokens_ref, *refs):
        total = 0.0
        for r, ref in enumerate(refs[: len(returned)]):
            total += dot(token_picks(tokens_ref, share, r * share), ref[...])
        refs[-1][...] = middle_ref[...] + total

    return kernel_call(
        body,
        [like(rows, model, dtype=F32)],
        [middle, tokens, *returned],
        flops=2 * rows * model * share * len(returned),
        after=after,
        mark=True,
    )


def combine_project(place, middle, returned, tokens, gain, qkv):
    rows, model = middle.shape
    width = qkv.shape[2]

    def body(place_ref, middle_ref, returned_ref, tokens_ref, gain_ref, w, passed_ref, *outs):
        picks = token_picks(tokens_ref, returned_ref.shape[0])
        passed = (middle_ref[...] + dot(picks, returned_ref[...])).astype(BF16)
        passed_ref[...] = passed
        project_rows(passed.astype(F32), gain_ref[...], w, *outs)

    return kernel_call(
        body,
        [like(rows, model), like(rows, model), like(rows, width), like(rows, 2 * width)],
        [place, middle, returned, tokens, gain, qkv],
        flops=2 * rows * model * returned.shape[0] + 6 * rows * model * width,
    )


def norm_back(values, gain, upstream):
    scale = lax.rsqrt(jnp.mean(values * values, axis=-1, keepdims=True) + EPSILON)
    unit = values * scale
    scaled = upstream * gain
    dvalues = scale * (scaled - unit * jnp.mean(unit * scaled, axis=-1, keepdims=True))
    return dvalues, jnp.sum(upstream * unit, axis=0, keepdims=True)


def middle_back(place, returned, tokens, middle, gain, dout, out_w, after=()):
    rows, model = middle.shape
    width = out_w.shape[0]

    def body(place_ref, returned_ref, tokens_ref, middle_ref, gain_ref, dout_ref, w, *refs):
        dmiddle_ref, datt_ref, dmix_ref, dgain_ref = refs
        picks = token_picks(tokens_ref, returned_ref.shape[0])
        dexpert_in = dot(picks, returned_ref[...])
        part, dgain = norm_back(middle_ref[...], gain_ref[...], dexpert_in)
        dgain_ref[...] = dgain
        dmiddle = dout_ref[...].astype(F32) + part
        dmiddle_ref[...] = dmiddle
        datt = dmiddle.astype(BF16)
        datt_ref[...] = datt
        dmix_ref[...] = dot_nt(datt, w.ready()[...]).astype(BF16)

    return kernel_call(
        body,
        [
            like(rows, model, dtype=F32),
            like(rows, model),
            like(rows, width),
            like(1, model, dtype=F32),
        ],
        [place, returned, tokens, middle, gain, dout, out_w],
        flops=2 * rows * model * (returned.shape[0] + width),
        after=after,
    )


def project_back(place, dq, dkv_parts, qkv, n_heads, after=()):
    rows, width = dq.shape
    model, n_parts = qkv.shape[1], len(dkv_parts)
    share = rows // n_heads

    def body(place_ref, dq_ref, *refs):
        part_refs, refs = refs[:n_parts], refs[n_parts:]
        w, dkv_ref = refs[:2]
        chunk_refs, total_ref = refs[2:-1], refs[-1]
        dkv = part_refs[0][...].astype(F32)
        for ref in part_refs[1:]:
            dkv += ref[...].astype(F32)
        dkv = dkv.astype(BF16)
        dkv_ref[...] = dkv
        w_ref = w.ready()
        total_ref[...] = (
            dot_nt(dq_ref[...], w_ref[0])
            + dot_nt(dkv[:, :width], w_ref[1])
            + dot_nt(dkv[:, width:], w_ref[2])
        )
        for r in range(n_heads):
            first = pl.multiple_of((place_ref[1] ^ r) * share, share)
            chunk_refs[r][...] = total_ref[pl.ds(first, share), :].astype(BF16)

    outs = kernel_call(
        body,
        [like(rows, 2 * width)] + [like(share, model)] * n_heads,
        [place, dq, *dkv_parts, qkv],
        [pltpu.VMEM((rows, model), F32)],
        flops=6 * rows * model * width,
        after=after,
    )
    return outs[0], outs[1:]


def tree_sum(values):
    while len(values) > 1:
        values = [values[i] + values[i + 1] for i in range(0, len(values), 2)]
    return values[0]


def share_sum(parts):
    def body(*refs):
        refs[-1][...] = tree_sum([ref[...].astype(F32) for ref in refs[:-1]]).astype(BF16)

    return kernel_call(body, [like(*parts[0].shape)], parts)[0]


def input_back(place, dnormed_parts, x, gain, dmiddle, tokens=None, n_ctx=0, per=0, after=()):
    rows, model = x.shape
    n_heads, share = len(dnormed_parts), dnormed_parts[0].shape[0]
    given = [x, gain, dmiddle] + ([] if tokens is None else [tokens])

    def body(place_ref, *refs):
        part_refs, refs = refs[:n_heads], refs[n_heads:]
        x_ref, gain_ref, dmiddle_ref = refs[:3]
        (dx_ref, dgain_ref), chunk_refs = refs[len(given) :][:2], refs[len(given) + 2 : -1]
        dnormed_ref = refs[-1]
        for r in range(n_heads):
            first = pl.multiple_of((place_ref[1] ^ r) * share, share)
            dnormed_ref[pl.ds(first, share), :] = part_refs[r][...].astype(F32)
        part, dgain = norm_back(x_ref[...].astype(F32), gain_ref[...], dnormed_ref[...])
        dgain_ref[...] = dgain
        dx = (dmiddle_ref[...] + part).astype(dx_ref.dtype)
        dx_ref[...] = dx
        if tokens is not None:
            dispatch_into(dx, place_ref, refs[3], chunk_refs)

    outs = kernel_call(
        body,
        [like(rows, model, dtype=F32 if tokens is None else BF16), like(1, model, dtype=F32)]
        + [like(per, model)] * n_ctx,
        [place, *dnormed_parts, *given],
        [pltpu.VMEM((rows, model), F32)],
        after=after,
    )
    return outs[0], outs[1], outs[2:]


def bucket_of(distance):
    exact_span = BUCKETS // 2
    result = jnp.minimum(distance, exact_span)
    for rank in range(1, BUCKETS - exact_span):
        edge = int(
            math.ceil(exact_span * (REACH / exact_span) ** (rank / (BUCKETS - exact_span)))
        )
        result = result + (distance >= edge).astype(jnp.int32)
    return result


def tile_buckets(half):
    row = lax.broadcasted_iota(jnp.int32, (half, half), 0)
    col = lax.broadcasted_iota(jnp.int32, (half, half), 1)
    same = jnp.where(row >= col, bucket_of(jnp.maximum(row - col, 0)), -1)
    return [same, bucket_of(half + row - col), bucket_of(2 * half + row - col)]


def bias_table(place, own, other, layer, half, after):
    heads, strip = own.shape[1], 8

    def body(place_ref, own_ref, other_ref, *refs):
        out_ref = refs[-1]

        def bias(bucket, head):
            return jnp.where(place_ref[2] == layer, own_ref[bucket, head], other_ref[bucket, head])

        values = [[bias(bucket, head) for head in range(heads)] for bucket in range(BUCKETS)]
        same, near, _ = tile_buckets(half)
        for head in range(heads):
            out_ref[head, 0] = jnp.full((half, half), NEGATIVE, F32)
            out_ref[head, 3] = jnp.full((half, half), values[-1][head], F32)
        for at in range(0, half, strip):
            for kind, held in ((1, same), (2, near)):
                held = held[at : at + strip]
                rows = [jnp.full((strip, half), NEGATIVE, F32) for _ in range(heads)]
                for bucket in range(BUCKETS):
                    hit = held == bucket
                    rows = [
                        jnp.where(hit, values[bucket][head], rows[head]) for head in range(heads)
                    ]
                for head in range(heads):
                    out_ref[head, kind, at : at + strip] = rows[head]

    return pl.pallas_call(
        body,
        out_shape=like(heads, 4, half, half, dtype=F32),
        in_specs=[pl.BlockSpec(memory_space=pltpu.SMEM)] * 3
        + [pl.BlockSpec(memory_space=pl.ANY)] * len(after),
        out_specs=pl.BlockSpec(memory_space=pltpu.VMEM),
        compiler_params=pltpu.CompilerParams(vmem_limit_bytes=2 * SPARE_BYTES),
    )(place, own, other, *after)


def small_weights(place, gains, routers, after):
    model, n_experts = routers[0].shape

    def body(place_ref, *refs):
        ins, outs = refs[:6], refs[-6:]
        for kind in range(2):
            own, other = (ref[...].astype(F32) for ref in ins[2 * kind : 2 * kind + 2])
            outs[2 * kind][...] = either(place_ref, own, other)
            outs[2 * kind + 1][...] = either(place_ref, other, own)
        own, other = (ref[...].astype(F32) for ref in ins[4:6])
        for out_ref, value in zip(
            outs[4:], (either(place_ref, own, other), either(place_ref, other, own))
        ):
            out_ref[...] = jnp.zeros(out_ref.shape, BF16)
            out_ref[:, :n_experts] = value.astype(BF16)

    args = [place, *gains[0], *gains[1], *routers]
    outs = kernel_call(
        body,
        [like(1, model, dtype=F32)] * 4 + [like(model, LANES)] * 2,
        args,
        after=after,
    )
    return outs[0:2], outs[2:4], outs[4:6]


def layer_row(place_ref, own, other, layer, k):
    rows = own.shape[1]
    row = jnp.where(place_ref[2] == layer, own[k : k + 1], other[k : k + 1])
    eye = lax.broadcasted_iota(jnp.int32, (rows, rows), 0) == lax.broadcasted_iota(
        jnp.int32, (rows, rows), 1
    )
    return jnp.sum(jnp.where(eye, row, 0).astype(F32), axis=1, keepdims=True).astype(jnp.int32)


def earlier(rows):
    row = lax.broadcasted_iota(jnp.int32, (rows, rows), 0)
    col = lax.broadcasted_iota(jnp.int32, (rows, rows), 1)
    return jnp.where(row > col, 1.0, 0.0).astype(BF16)


def quarter_of(rank, per, n_heads):
    return sum([(rank >= h * per).astype(jnp.int32) for h in range(1, n_heads)])


def token_slots(place, own, other, n_experts, per, n_heads, after):
    rows = own.shape[2]

    def body(place_ref, own_ref, other_ref, *refs):
        *outs, pair_ref = refs[-4:]
        pair_ref[0] = own_ref[...]
        pair_ref[1] = other_ref[...]
        own, other = own_ref[place_ref[2]], other_ref[place_ref[2]]
        for layer in range(2):
            choices = [layer_row(place_ref, own, other, layer, k) for k in range(2)]
            lane = lax.broadcasted_iota(jnp.int32, (rows, LANES), 1)
            hots = [jnp.where(lane == choice, 1.0, 0.0) for choice in choices]
            ranks = dot(earlier(rows), (hots[0] + hots[1]).astype(BF16))
            for k in range(2):
                rank = jnp.sum(ranks * hots[k], axis=1, keepdims=True).astype(jnp.int32)
                quarter = quarter_of(rank, per, n_heads)
                inner = (choices[k] ^ place_ref[0]) * per + rank - quarter * per
                outs[layer][:, k : k + 1] = quarter * (n_experts * per) + inner
                if layer == 1:
                    outs[2][:, k : k + 1] = (quarter ^ place_ref[1]) * (n_experts * per) + inner

    return kernel_call(
        body,
        [like(rows, 2, dtype=jnp.int32)] * 3 + [like(2, *own.shape, dtype=jnp.int32)],
        [place, own, other],
        after=after,
    )


def other_experts(place, pairs, per, n_heads):
    n_ctx, rows = len(pairs), pairs[0].shape[3]

    def body(place_ref, *refs):
        lane = lax.broadcasted_iota(jnp.int32, (rows, LANES), 1)
        slot = lax.broadcasted_iota(jnp.int32, (rows, n_heads * per), 1)
        found, heres = [], jnp.zeros((rows, LANES), F32)
        for layer in range(2):
            for r in range(n_ctx):
                pair = [refs[r][i, place_ref[2]] for i in range(2)]
                one, two = (layer_row(place_ref, *pair, layer, k) for k in range(2))
                here = (one == place_ref[0]) | (two == place_ref[0])
                other = jnp.where(one == place_ref[0], two, one).astype(F32)
                heres += jnp.where(here & (lane == layer * n_ctx + r), 1.0, 0.0)
                found.append((here, other))
        ranks = dot(earlier(rows), heres.astype(BF16)).astype(jnp.int32)
        for number, (here, other) in enumerate(found):
            layer, r = number // n_ctx, number % n_ctx
            picks = jnp.where(here & (slot == ranks[:, number : number + 1]), 1.0, 0.0)
            other = jnp.broadcast_to(other, (rows, LANES)).astype(BF16)
            column = dot_tn(picks.astype(BF16), other)[:, 0:1].astype(jnp.int32)
            for h in range(n_heads):
                at = (h * n_ctx + r) * per
                refs[n_ctx + layer][at : at + per, :] = column[h * per : (h + 1) * per]

    return kernel_call(
        body, [like(n_heads * n_ctx * per, 1, dtype=jnp.int32)] * 2, [place, *pairs]
    )


def table_back(dtable, after=()):
    heads, half = dtable.shape[0], dtable.shape[3]

    def body(dtable_ref, *refs):
        out_ref, buckets = refs[-1], tile_buckets(half)
        for bucket in range(BUCKETS):
            hits = [held == bucket for held in buckets]
            for head in range(heads):
                kept = jnp.zeros((half, half), F32)
                for tile, hit in enumerate(hits):
                    kept += jnp.where(hit, dtable_ref[head, 1 + tile], 0.0)
                at = bucket * heads + head
                out_ref[at : at + 1, :] = jnp.sum(kept, axis=0, keepdims=True)

    return kernel_call(
        body, [like(BUCKETS * heads, half, dtype=F32)], [dtable], after=after
    )[0]


def heads_sum(chunks, n_ctx, after=()):
    parts = exchange(chunks, "heads")
    rows, model = parts[0].shape
    per = rows // n_ctx

    def body(*refs):
        total = tree_sum([ref[...].astype(F32) for ref in refs[: len(parts)]])
        for r, out_ref in enumerate(refs[len(parts) :]):
            out_ref[...] = total[r * per : (r + 1) * per].astype(BF16)

    return kernel_call(body, [like(per, model)] * n_ctx, parts, after=after)


def return_rows(chunks, n_ctx):
    back = exchange(heads_sum(chunks, n_ctx), "ctx")
    return gather_rows(jnp.concatenate(back, axis=0), "heads")


def send_rows(chunks):
    return gather_rows(jnp.concatenate(exchange(chunks, "ctx"), axis=0), "heads")


def body(
    boundary,
    norm_first,
    qkv_weight,
    position_bias,
    out_weight,
    norm_second,
    router,
    expert_up,
    expert_down,
    routes,
):
    section = lax.axis_index("section")
    ctx_index = lax.axis_index("ctx")
    heads_index = lax.axis_index("heads")
    n_ctx, n_heads = lax.axis_size("ctx"), lax.axis_size("heads")
    first = section == 0
    place = jnp.stack([ctx_index, heads_index, section]).astype(jnp.int32)
    rows, model = boundary.shape[2:]
    half = rows // 2
    n_experts, heads = router.shape[2], position_bias.shape[2]
    per = 5 * rows // (2 * n_experts) // n_heads

    def by_layer(own, other):
        return Pick(own, other), Pick(other, own)

    def with_other(own):
        return own, swap(own, "section")

    qkv = by_layer(*with_other(qkv_weight[0]))
    given = swap(lax.dynamic_index_in_dim(boundary[0], 1 - section, 0, False), "section")
    gain_pairs = with_other(norm_first), with_other(norm_second)
    x0, cotangent, normed0, q0, kv0 = begin(
        place, boundary[0], given, *gain_pairs[0], qkv[0]
    )
    kv_all0 = gather_rows(kv0, "ctx")

    bias_pair = with_other(position_bias[0])
    bias0 = bias_table(place, *bias_pair, 0, half, [kv0])
    up = by_layer(*with_other(expert_up[0, 0]))
    down = by_layer(*with_other(expert_down[0, 0]))
    width = out_weight.shape[1]
    out_gathered = gather_rows(joined(with_other(out_weight[0]), [kv0]), "heads")
    out_full = [Rows(out_gathered, layer, width) for layer in range(2)]
    out_own = [Rows(out_gathered, layer, width, own=True) for layer in range(2)]
    mix0, lse0 = attend(place, q0, [kv_all0], bias0, n_ctx)
    gains_first, gains_second, routers = small_weights(
        place, gain_pairs, with_other(router[0]), [lse0]
    )
    *tokens, tokens_near, pair = token_slots(
        place, *with_other(routes[0].transpose(0, 2, 1)), n_experts, per, n_heads, [lse0]
    )
    pairs = exchange([pair] * n_ctx, "ctx")
    others = other_experts(place, pairs, per, n_heads)

    def before_experts(layer, x, mix):
        mixes = exchange([mix] * n_heads, "heads")
        middle, chunks = finish_attention(
            place, mixes, out_full[layer], x, gains_second[layer], tokens[layer], n_ctx, per
        )
        return middle, send_rows(chunks)

    def expert_weights(layer):
        return up[layer], down[layer], routers[layer], others[layer]

    middle0, arrived0 = before_experts(0, x0, mix0)
    chunks, kept0 = experts(place, arrived0, *expert_weights(0), n_heads)
    dout_chunks = dispatch_whole(place, cotangent, tokens[1], n_ctx, per, n_heads, [middle0])
    returned = return_rows(chunks, n_ctx)
    x1, normed1, q1, kv1 = combine_project(
        place, middle0, returned, tokens[0], gains_first[1], qkv[1]
    )

    kv_all1 = gather_rows(kv1, "ctx")
    bias1 = bias_table(place, *bias_pair, 1, half, [middle0])
    mix1, lse1 = attend(place, q1, [kv_all1], bias1, n_ctx)
    middle1, arrived1 = before_experts(1, x1, mix1)
    dout_rows1 = jnp.stack(exchange(dout_chunks, "ctx"))
    dout_rows1 = dout_rows1.reshape(n_ctx, n_heads, per, model).transpose(1, 0, 2, 3)
    dout_rows1 = dout_rows1.reshape(-1, model)
    chunks, (dpre1, dslots1, dlogits1, hidden1, margin1) = experts_back(
        place, dout_rows1, None, arrived1, *expert_weights(1), n_heads
    )
    dmiddle1, datt1, dmix1, dgain_second1 = middle_back(
        place, return_rows(chunks, n_ctx), tokens[1], middle1, gains_second[1], cotangent, out_own[1]
    )
    dq1, dtable1, dkv1 = attend_back(place, q1, [kv_all1], bias1, lse1, dmix1, n_ctx)
    dkv_parts1 = exchange(dkv1, "ctx")
    out_total = heads_sum(
        experts_out(place, hidden1, margin1, down[1], n_heads, dkv_parts1[1:2]), n_ctx
    )
    dkv_sum1, chunks = project_back(place, dq1, dkv_parts1, qkv[1], n_heads)
    total1 = share_sum(exchange(chunks, "heads"))
    lanes1 = table_back(dtable1)
    dense1, made = dense_grad(place, [(normed1, dq1), (datt1, mix1), (normed1, dkv_sum1)])
    dx1, dgain_first1, sent = input_back(
        place,
        exchange([total1] * n_heads, "heads"),
        x1,
        gains_first[1],
        dmiddle1,
        tokens[0],
        n_ctx,
        per,
        [lanes1, made],
    )

    dout_rows0 = send_rows(sent)
    chunks, (dpre0, dslots0, dlogits0) = experts_back(
        place, dout_rows0, kept0, arrived0, *expert_weights(0), n_heads, out_total[:1]
    )
    lists = [(arrived0, arrived1), (dpre0, dpre1), (kept0[1], hidden1), (dslots0, dslots1)]
    mine, theirs = [Pick(a, b) for a, b in lists], [Pick(b, a) for a, b in lists]
    out_back = exchange(out_total, "ctx")
    back = heads_sum(chunks, n_ctx, out_back[1:])
    returned = gather_rows(jnp.concatenate(exchange(back, "ctx"), axis=0), "heads")
    router_part = router_grads(
        place, [(dlogits0, arrived0), (dlogits1, arrived1)], n_experts, back[:1]
    )
    router_parts = exchange([router_part] * n_heads, "heads")
    small1 = small_rows(
        place, 1, dgain_first1, dgain_second1, router_parts, lanes1, n_experts, n_ctx
    )
    dmiddle0, datt0, dmix0, dgain_second0 = middle_back(
        place,
        returned,
        tokens[0],
        middle0,
        gains_second[0],
        dx1,
        out_own[0],
        [small1],
    )
    dq0, dtable0, dkv0 = attend_back(place, q0, [kv_all0], bias0, lse0, dmix0, n_ctx)
    lanes0 = table_back(dtable0)
    dkv_parts0 = exchange(dkv0, "ctx")
    sends, made = expert_grads(place, [theirs[:2], theirs[2:]], after=dkv_parts0[1:2])
    dkv_sum0, chunks = project_back(place, dq0, dkv_parts0, qkv[0], n_heads, [made])
    parts = exchange(chunks, "heads")
    total0 = share_sum(parts)
    dense0, made = dense_grad(
        place, [(normed0, dq0), (datt0, mix0), (normed0, dkv_sum0)], parts[1:2]
    )
    near = exchange([total0] * n_heads, "heads")
    dx0, dgain_first0, _ = input_back(
        place,
        near,
        x0,
        gains_first[0],
        dmiddle0,
        after=[made, lanes0],
    )

    got_dx = one_way(dx0, 1)
    small0 = small_rows(
        place, 0, dgain_first0, dgain_second0, router_parts, lanes0, n_experts, n_ctx
    )
    smalls = [small0, small1]
    got = swap(joint_send(place, Pick(dense1, dense0), smalls), "section")
    joint = joint_sum(place, Pick(dense0, dense1), smalls, got)
    joint = lax.psum_scatter(joint, "ctx", scatter_dimension=0, tiled=True)
    quarter = join_quarter(out_back, ())
    grad_up, grad_down, made = expert_grads(
        place, [mine[:2], mine[2:]], swap(sends, "section"), after=[dgain_first0]
    )
    out, _ = combine(middle1, exchange([quarter] * n_heads, "heads"), tokens_near, [made])
    grad_qkv, grad_out, grad_first, grad_second, grad_router, grad_bias = joint_split(
        joint, width, n_experts, (heads, BUCKETS // n_ctx)
    )
    boundary_out = assemble(place, dx0, one_way(out, 0), got_dx, out)
    return (
        boundary_out[None],
        grad_first,
        grad_qkv[None],
        grad_bias.T[None],
        grad_out[None],
        grad_second,
        grad_router.T[None],
        grad_up[None, None],
        grad_down[None, None],
    )


def solution(mesh):
    placed = (
        P("section", None, "ctx", None),
        P("section", None),
        P("section", None, None, "heads"),
        P("section", None, "heads"),
        P("section", "heads", None),
        P("section", None),
        P("section", None, None),
        P("section", "ctx", None, "heads"),
        P("section", "ctx", "heads", None),
        P("section", None, "ctx", None),
    )
    return jax.shard_map(
        body,
        mesh=mesh,
        in_specs=placed,
        out_specs=(
            P("section", None, "ctx", None),
            P("section", "ctx"),
            P("section", None, "ctx", "heads"),
            P("section", "ctx", "heads"),
            P("section", "heads", "ctx"),
            P("section", "ctx"),
            P("section", "ctx", None),
            P("section", "ctx", None, "heads"),
            P("section", "ctx", "heads", None),
        ),
        check_vma=False,
    )
```
